512 devices in a mesh: dp: 32 (over y, z_lo), height: 16 (over x, z_hi, core).
Axes of the slice: x: 4, y: 4, z: 16 (z_hi: 2, z_lo: 8; z = z_hi * 8 + z_lo), core: 2. Of those that a mesh axis runs over, the one named last changes fastest.
Arguments:
- frames: bfloat16 [32, 256, 128, 128], P('dp', 'height'), may hold values from -6 to 6
- cotangent: bfloat16 [32, 256, 128, 128], P('dp', 'height'), may hold values from -6 to 6
- w_in: bfloat16 [3, 3, 128, 128], P(None, None, 'dp'), may hold values from -0.1875 to 0.1875
- w_down: bfloat16 [3, 3, 128, 256], P(None, None, 'dp'), may hold values from -0.1875 to 0.1875
- w_up: bfloat16 [3, 3, 256, 128], P(None, None, 'dp'), may hold values from -0.25 to 0.25
Outputs:
- output: bfloat16 [32, 256, 128, 128], P('dp', 'height')
- input_grad: bfloat16 [32, 256, 128, 128], P('dp', 'height')
- grad_in: float32 [3, 3, 128, 128], P(None, None, 'dp', 'height')
- grad_down: float32 [3, 3, 128, 256], P(None, None, 'dp', 'height')
- grad_up: float32 [3, 3, 256, 128], P(None, None, 'dp', 'height')
The draws below stay inside these ranges and needn't reach their ends.
All inputs are finite; a program needn't handle non-finite values.
Results may differ from the reference program's by a relative error of at most 0.0055.
Values may be sent and summed in bfloat16 or wider, within the bound.
A program may use at most 64 MiB of HBM per device.

```python
import math
import jax
import jax.numpy as jnp
from jax import lax

C = 128
C2 = 256
COLS = 128
FRAMES = 32
ROWS = 256


def with_spikes(values, stream_key, source, target, blocks, factor):
    def block_of(position):
        return (jnp.arange(values.shape[position]) // (values.shape[position] // blocks)).reshape((-1,) + (1,) * (values.ndim - 1 - position))

    near = jax.random.permutation(stream_key, blocks)[block_of(target)]
    far = (block_of(target) + blocks // 2) % blocks
    return jnp.where((block_of(source) == near) | (block_of(source) == far), factor * values, values)


def level_of(key, extent, split, least, largest):
    factor_of = 1.0
    for dim, shards_of in split:
        steps = jax.random.uniform(jax.random.fold_in(jax.random.fold_in(key, 6), dim), (shards_of,), jnp.float32, least / len(split), largest / len(split))
        factor_of = factor_of * jnp.repeat(jnp.exp(steps), extent[dim] // shards_of).reshape((-1,) + (1,) * (len(extent) - 1 - dim))
    return factor_of


def centred(key, dims, spread, bound, cuts=(), kind=jnp.bfloat16):
    array = spread * jax.random.normal(key, dims, jnp.float32)
    if cuts:
        array = array * level_of(key, dims, cuts, -0.22, 0.18)
    return jnp.clip(array, -bound, bound).astype(kind)


def noise_with(key, extent, deviation, most, cuts, heavy, dtype=jnp.bfloat16):
    values = deviation * jax.random.normal(key, extent, jnp.float32)
    if cuts:
        values = values * level_of(key, extent, cuts, -0.22, 0.18)
    return jnp.clip(with_spikes(values, jax.random.fold_in(key, 3), *heavy), -most, most).astype(dtype)


def setup_inputs(seed: int = 0) -> dict:
    arg_keys = jax.random.split(jax.random.key(seed), 6)
    frames = noise_with(arg_keys[0], (FRAMES, ROWS, COLS, C), 1.0, 6.0, ((0, 32), (1, 16)), (0, 3, 32, 2.75))
    cotangent = noise_with(arg_keys[1], (FRAMES, ROWS, COLS, C), 1.0, 6.0, ((0, 32), (1, 16)), (1, 3, 16, 2.0))
    w_in = centred(arg_keys[2], (3, 3, C, C), (9 * C) ** -0.5, 0.1875, ((2, 32),))
    w_down = centred(arg_keys[3], (3, 3, C, C2), (9 * C) ** -0.5, 0.1875, ((2, 32),))
    w_up = centred(arg_keys[4], (3, 3, C2, C), (9 * C2 // 4) ** -0.5, 0.25, ((2, 32),))
    return dict(frames=frames, cotangent=cotangent, w_in=w_in, w_down=w_down, w_up=w_up)


LAYOUT = ('NHWC', 'HWIO', 'NHWC')
FLAT = ((0, 0), (0, 0))

def conv_plain(inputs, kernel, stride, padding, dilate):
    return lax.conv_general_dilated(inputs, kernel, (stride, stride), padding, lhs_dilation=(dilate, dilate), dimension_numbers=LAYOUT, preferred_element_type=jnp.float32)

def flipped(kernel):
    return jnp.transpose(kernel[::-1, ::-1], (0, 1, 3, 2))

def silu_slope(pre_act):
    sigmoid = jax.nn.sigmoid(pre_act)
    return sigmoid * (1.0 + pre_act * (1.0 - sigmoid))

def kernel_grad(source, cotangent_part, stride):
    rows_out, cols_out = (cotangent_part.shape[1], cotangent_part.shape[2])
    flat_cotangent = cotangent_part.reshape(-1, cotangent_part.shape[3])
    tap_list = []
    for row_tap in range(3):
        for col_tap in range(3):
            window = source[:, row_tap:row_tap + stride * (rows_out - 1) + 1:stride, col_tap:col_tap + stride * (cols_out - 1) + 1:stride, :]
            tap_list.append(jnp.dot(window.reshape(-1, source.shape[3]).T, flat_cotangent, preferred_element_type=jnp.float32))
    return jnp.stack(tap_list).reshape(3, 3, source.shape[3], cotangent_part.shape[3])

def frame_step(weights, frame, cotangent):
    w_in, w_down, w_up = weights
    padded_in = jnp.pad(frame, ((0, 0), (1, 1), (1, 1), (0, 0)))
    pre_fine = conv_plain(padded_in, w_in, 1, FLAT, 1)
    hidden = jax.nn.silu(pre_fine).astype(jnp.bfloat16)
    padded_hidden = jnp.pad(hidden, ((0, 0), (1, 0), (1, 0), (0, 0)))
    pre_coarse = conv_plain(padded_hidden, w_down, 2, FLAT, 1)
    coarse = jax.nn.silu(pre_coarse).astype(jnp.bfloat16)
    upsampled = conv_plain(coarse, w_up, 1, ((1, 2), (1, 2)), 2)
    output = (frame.astype(jnp.float32) + upsampled).astype(jnp.bfloat16)
    padded_cotangent = jnp.pad(cotangent, ((0, 0), (1, 0), (1, 0), (0, 0)))
    grad_coarse = conv_plain(padded_cotangent, flipped(w_up), 2, FLAT, 1)
    grad_pre_coarse = (grad_coarse * silu_slope(pre_coarse)).astype(jnp.bfloat16)
    grad_hidden = conv_plain(grad_pre_coarse, flipped(w_down), 1, ((1, 2), (1, 2)), 2)
    grad_pre_fine = (grad_hidden * silu_slope(pre_fine)).astype(jnp.bfloat16)
    padded_grad = jnp.pad(grad_pre_fine, ((0, 0), (1, 1), (1, 1), (0, 0)))
    grad_input = conv_plain(padded_grad, flipped(w_in), 1, FLAT, 1)
    input_grad = (cotangent.astype(jnp.float32) + grad_input).astype(jnp.bfloat16)
    grads = (kernel_grad(padded_in, grad_pre_fine, 1), kernel_grad(padded_hidden, grad_pre_coarse, 2), flipped(kernel_grad(padded_cotangent, coarse, 2)))
    return (output, input_grad, grads)

def reference(frames, cotangent, w_in, w_down, w_up):
    weights = (w_in, w_down, w_up)

    def per_frame(running, frame_pair):
        output, input_grad, grads = frame_step(weights, frame_pair[0][None], frame_pair[1][None])
        summed = tuple((earlier + addend for earlier, addend in zip(running, grads)))
        return (summed, (output[0], input_grad[0]))
    zero_grads = tuple((jnp.zeros(weight.shape, jnp.float32) for weight in weights))
    totals, (outputs, input_grads) = lax.scan(per_frame, zero_grads, (frames, cotangent))
    factor = 1.0 / math.sqrt(frames.shape[0] * frames.shape[1] * frames.shape[2])
    return (outputs, input_grads, totals[0] * factor, totals[1] * factor, totals[2] * factor)
```

```python
import math

import jax
import jax.numpy as jnp
from jax import lax
from jax.experimental import pallas as pl
from jax.experimental.pallas import tpu as pltpu
from jax.sharding import PartitionSpec as P

LAYOUT = ("NHWC", "HWIO", "NHWC")
FLAT = ((0, 0), (0, 0))
SIDE_PAD = ((0, 0), (0, 0), (1, 1), (0, 0))
LEFT_PAD = ((0, 0), (0, 0), (1, 0), (0, 0))
MESH = pl.DeviceIdType.MESH

PACK = 208
DOWN_AT = 48
UP_AT = 128
PIECE = 64
PIECE_STEP = 48
HOPS = (1, -1, 2, -2, 3, -3, 4)


def place():
    d = lax.axis_index("dp")
    h = lax.axis_index("height")
    z = lax.rem(lax.div(h, 2), 2) * 8 + lax.rem(d, 8)
    return lax.div(h, 4), lax.div(d, 8), z, lax.rem(h, 2)


def device(x, y, z, core):
    return (y * 8 + lax.rem(z, 8), x * 4 + lax.div(z, 8) * 2 + core)


def on_ring(position, by, size):
    return lax.rem(position + by + size, size)


def remote(source, target, sends, recvs, slot, where):
    return pltpu.make_async_remote_copy(
        src_ref=source,
        dst_ref=target,
        send_sem=sends.at[slot],
        recv_sem=recvs.at[slot],
        device_id=where,
        device_id_type=MESH,
    )


def meet(partners):
    barrier = pltpu.get_barrier_semaphore()
    for partner in partners:
        pl.semaphore_signal(barrier, inc=1, device_id=partner, device_id_type=MESH)
    pl.semaphore_wait(barrier, len(partners))


def gather_kernel(own, full, z_send, z_recv, y_send, y_recv, c_send, c_recv):
    x, y, z, core = place()
    z_lo = lax.rem(z, 8)
    mine = y * 8 + z_lo
    holder = lax.div(z_lo, 4) == core
    other = device(x, y, z, 1 - core)
    meet(
        [device(x, y, on_ring(z, by, 16), core) for by in (1, -1, 2, -2, 3, -3, 4, -4)]
        + [device(x, on_ring(y, by, 4), z, core) for by in (1, 2, 3)]
        + [other]
    )

    def along_z(slot, by):
        return remote(own, full.at[mine], z_send, z_recv, slot, device(x, y, on_ring(z, by, 16), core))

    @pl.when(holder)
    def _():
        for slot, by in enumerate(HOPS):
            along_z(slot, by).start()
        full[mine] = own[...]

    for slot, by in enumerate(HOPS):
        source = lax.rem(on_ring(z, -by, 16), 8)

        @pl.when(lax.div(source, 4) == core)
        def _():
            along_z(slot, by).wait_recv()

    def block(by, half):
        return full.at[pl.ds(on_ring(y, -by, 4) * 8 + half * 4, 4)]

    def along_y(by):
        return remote(block(0, core), block(0, core), y_send, y_recv, by - 1, device(x, on_ring(y, by, 4), z, core))

    def across(by):
        return remote(block(by, core), block(by, core), c_send, c_recv, by, other)

    for by in (1, 3, 2):
        along_y(by).start()
    across(0).start()
    for by in (1, 3, 2):
        along_y(by).wait_recv()
        across(by).start()
    for by in range(4):
        across(by).wait_recv()

    @pl.when(holder)
    def _():
        for slot, by in enumerate(HOPS):
            along_z(slot, by).wait_send()

    for by in (1, 2, 3):
        along_y(by).wait_send()
    for by in range(4):
        across(by).wait_send()


def gather(packed):
    return pl.pallas_call(
        gather_kernel,
        out_shape=jax.ShapeDtypeStruct((32, PACK, 128), jnp.bfloat16),
        in_specs=[pl.BlockSpec(memory_space=pltpu.VMEM)],
        out_specs=pl.BlockSpec(memory_space=pltpu.VMEM),
        scratch_shapes=[
            pltpu.SemaphoreType.DMA((7,)),
            pltpu.SemaphoreType.DMA((7,)),
            pltpu.SemaphoreType.DMA((3,)),
            pltpu.SemaphoreType.DMA((3,)),
            pltpu.SemaphoreType.DMA((4,)),
            pltpu.SemaphoreType.DMA((4,)),
        ],
        compiler_params=pltpu.CompilerParams(
            collective_id=0, has_side_effects=True, vmem_limit_bytes=32 << 20
        ),
    )(packed)


def reduce_kernel(
    parts,
    total,
    from_core,
    to_y,
    from_y,
    sums,
    to_z,
    from_z,
    column,
    from_x,
    piece,
    from_far,
    done,
    all_pieces,
    c_send,
    c_recv,
    y_send,
    y_recv,
    z_send,
    z_recv,
    x_send,
    x_recv,
    f_send,
    f_recv,
    a_send,
    a_recv,
    b_send,
    b_recv,
):
    x, y, z, core = place()
    z_lo = lax.rem(z, 8)
    holder = lax.div(z_lo, 4) == core
    other = device(x, y, z, 1 - core)
    far = on_ring(z, 8, 16)
    meet(
        [device(x, y, on_ring(z, by, 16), core) for by in (1, -1, 2, -2, 3, -3, 4, -4, 8)]
        + [device(x, on_ring(y, by, 4), z, core) for by in (1, 2, 3)]
        + [device(on_ring(x, by, 4), y, z, core) for by in (1, 2, 3)]
        + [device(on_ring(x, by, 4), y, z, 1 - core) for by in (0, 1, 2, 3)]
    )

    def rows_of(by, half):
        return pl.ds(on_ring(y, by, 4) * 8 + half * 4, 4)

    def across(by):
        return remote(parts.at[rows_of(by, 1 - core)], from_core.at[by], c_send, c_recv, by, other)

    def along_y(by):
        return remote(to_y.at[by - 1], from_y.at[by - 1], y_send, y_recv, by - 1, device(x, on_ring(y, by, 4), z, core))

    for by in (1, 3, 2, 0):
        across(by).start()
    for by in (1, 3, 2):
        across(by).wait_recv()
        to_y[by - 1] = (
            parts[rows_of(by, core)].astype(jnp.float32) + from_core[by].astype(jnp.float32)
        ).astype(jnp.bfloat16)
        along_y(by).start()
    across(0).wait_recv()
    sums[...] = parts[rows_of(0, core)].astype(jnp.float32) + from_core[0].astype(jnp.float32)
    for by in (1, 3, 2):
        along_y(by).wait_recv()
        sums[...] += from_y[by - 1].astype(jnp.float32)
    to_z[...] = sums[...].astype(jnp.bfloat16)

    def along_z(slot, by):
        where = on_ring(z, by, 16)
        return remote(
            to_z.at[lax.rem(where, 4)], from_z.at[slot], z_send, z_recv, slot, device(x, y, where, core)
        )

    for slot, by in enumerate(HOPS):

        @pl.when(lax.div(lax.rem(on_ring(z, by, 16), 8), 4) == core)
        def _():
            along_z(slot, by).start()

    def along_x(by):
        where = on_ring(x, by, 4)
        return remote(
            column.at[pl.ds(where * PIECE_STEP, PIECE)],
            from_x.at[by - 1],
            x_send,
            x_recv,
            by - 1,
            device(where, y, z, core),
        )

    def to_far():
        return remote(piece, from_far, f_send, f_recv, 0, device(x, y, far, core))

    def spread(by):
        return remote(done, all_pieces.at[x], a_send, a_recv, by, device(on_ring(x, by, 4), y, z, core))

    def spread_other(by):
        return remote(done, all_pieces.at[x], b_send, b_recv, by, device(on_ring(x, by, 4), y, z, 1 - core))

    @pl.when(holder)
    def _():
        column[...] = sums[lax.rem(z_lo, 4)]
        for slot, by in enumerate(HOPS):
            along_z(slot, by).wait_recv()
            column[...] += from_z[slot].astype(jnp.float32)
        for by in (1, 3, 2):
            along_x(by).start()
        piece[...] = column[pl.ds(x * PIECE_STEP, PIECE)]
        for by in (1, 3, 2):
            along_x(by).wait_recv()
            piece[...] += from_x[by - 1]
        to_far().start()
        to_far().wait_recv()
        done[...] = piece[...] + from_far[...]
        for by in (2, 1, 3):
            spread(by).start()
        for by in (2, 1, 3, 0):
            spread_other(by).start()
        all_pieces[x] = done[...]
        for by in (1, 2, 3):
            spread(by).wait_recv()
        for by in (1, 2, 3):
            along_x(by).wait_send()
        to_far().wait_send()
        for by in (1, 2, 3):
            spread(by).wait_send()
        for by in range(4):
            spread_other(by).wait_send()

    @pl.when(jnp.logical_not(holder))
    def _():
        for by in range(4):
            spread_other(by).wait_recv()

    for source in range(4):
        total[pl.ds(source * PIECE_STEP, PIECE)] = all_pieces[source]
    for by in range(4):
        across(by).wait_send()
    for by in (1, 2, 3):
        along_y(by).wait_send()
    for slot, by in enumerate(HOPS):

        @pl.when(lax.div(lax.rem(on_ring(z, by, 16), 8), 4) == core)
        def _():
            along_z(slot, by).wait_send()


def reduce_over_all(parts):
    dma = pltpu.SemaphoreType.DMA
    counts = (4, 3, 7, 3, 1, 4, 4)
    return pl.pallas_call(
        reduce_kernel,
        out_shape=jax.ShapeDtypeStruct((PACK, 128), jnp.float32),
        in_specs=[pl.BlockSpec(memory_space=pltpu.VMEM)],
        out_specs=pl.BlockSpec(memory_space=pltpu.VMEM),
        scratch_shapes=[
            pltpu.VMEM((4, 4, PACK, 128), jnp.bfloat16),
            pltpu.VMEM((3, 4, PACK, 128), jnp.bfloat16),
            pltpu.VMEM((3, 4, PACK, 128), jnp.bfloat16),
            pltpu.VMEM((4, PACK, 128), jnp.float32),
            pltpu.VMEM((4, PACK, 128), jnp.bfloat16),
            pltpu.VMEM((7, PACK, 128), jnp.bfloat16),
            pltpu.VMEM((PACK, 128), jnp.float32),
            pltpu.VMEM((3, PIECE, 128), jnp.float32),
            pltpu.VMEM((PIECE, 128), jnp.float32),
            pltpu.VMEM((PIECE, 128), jnp.float32),
            pltpu.VMEM((PIECE, 128), jnp.float32),
            pltpu.VMEM((4, PIECE, 128), jnp.float32),
        ]
        + [dma((count,)) for count in counts for _ in range(2)],
        compiler_params=pltpu.CompilerParams(
            collective_id=1, has_side_effects=True, vmem_limit_bytes=32 << 20
        ),
    )(parts)


def pack(w_in, w_down, w_up):
    def rows(kernel, size):
        return jnp.pad(kernel, ((0, 0), (0, size - kernel.shape[1]), (0, 0)))

    count = w_in.shape[0]
    halves = w_down.reshape(count, 36, 2, 128).transpose(0, 2, 1, 3).reshape(count, 72, 128)
    return jnp.concatenate(
        [
            rows(w_in.reshape(count, 36, 128), DOWN_AT),
            rows(halves, UP_AT - DOWN_AT),
            rows(w_up.reshape(count, 72, 128), PACK - UP_AT),
        ],
        axis=1,
    )


def unpack(packed):
    count = packed.shape[0]
    halves = packed[:, DOWN_AT : DOWN_AT + 72].reshape(count, 2, 36, 128).transpose(0, 2, 1, 3)
    return (
        packed[:, :36].reshape(count, 9, 4, 128),
        halves.reshape(count, 9, 4, 256),
        packed[:, UP_AT : UP_AT + 72].reshape(count, 9, 8, 128),
    )


def padded(cells, sides, width):
    for axis, dim in sides:
        count = lax.axis_size(axis)
        ends = count - 1
        head = lax.slice_in_dim(cells, 0, width, axis=dim)
        tail = lax.slice_in_dim(cells, cells.shape[dim] - width, cells.shape[dim], axis=dim)
        cells = jnp.concatenate(
            [
                lax.ppermute(tail, axis, [(i, (i + 1) % count) for i in range(ends)]),
                cells,
                lax.ppermute(head, axis, [((i + 1) % count, i) for i in range(ends)]),
            ],
            axis=dim,
        )
    return cells


def from_behind(shard, axis, by):
    devices = lax.axis_size(axis)
    pairs = [(i, i + by) for i in range(devices) if 0 <= i + by < devices]
    return lax.ppermute(shard, axis, pairs)


def conv_plain(inputs, kernel, stride, padding, dilate):
    return lax.conv_general_dilated(
        inputs,
        kernel,
        (stride, stride),
        padding,
        lhs_dilation=(dilate, dilate),
        dimension_numbers=LAYOUT,
        preferred_element_type=jnp.float32,
    )


def flipped(kernel):
    return jnp.transpose(kernel[::-1, ::-1], (0, 1, 3, 2))


def silu_slope(pre_act):
    sigmoid = jax.nn.sigmoid(pre_act)
    return sigmoid * (1.0 + pre_act * (1.0 - sigmoid))


def kernel_grad(source, cotangent_part, stride):
    rows_out, cols_out = (cotangent_part.shape[1], cotangent_part.shape[2])
    flat_cotangent = cotangent_part.reshape(-1, cotangent_part.shape[3])
    tap_list = []
    for row_tap in range(3):
        for col_tap in range(3):
            window = source[
                :,
                row_tap : row_tap + stride * (rows_out - 1) + 1 : stride,
                col_tap : col_tap + stride * (cols_out - 1) + 1 : stride,
                :,
            ]
            tap_list.append(
                jnp.dot(
                    window.reshape(-1, source.shape[3]).T,
                    flat_cotangent,
                    preferred_element_type=jnp.float32,
                )
            )
    return jnp.stack(tap_list).reshape(3, 3, source.shape[3], cotangent_part.shape[3])


def by_shard(grad, count):
    rows, columns = grad.shape[2] // count, grad.shape[3]
    return grad.astype(jnp.bfloat16).reshape(9, count, rows, columns).transpose(1, 0, 2, 3)


def on_device(frames, cotangent, w_in, w_down, w_up):
    gathered = unpack(gather(pack(w_in[None], w_down[None], w_up[None])[0]))
    full_in, full_down, full_up = (
        part.transpose(1, 0, 2, 3).reshape(3, 3, -1, part.shape[3]) for part in gathered
    )
    halo_in = padded(frames, (("height", 1),), 1)
    padded_in = jnp.pad(halo_in, SIDE_PAD)
    pre_fine = conv_plain(padded_in, full_in, 1, FLAT, 1)
    hidden = jax.nn.silu(pre_fine).astype(jnp.bfloat16)
    above_row = from_behind(hidden[:, -1:], "height", 1)
    padded_hidden = jnp.pad(jnp.concatenate([above_row, hidden], 1), LEFT_PAD)
    pre_coarse = conv_plain(padded_hidden, full_down, 2, FLAT, 1)
    coarse = jax.nn.silu(pre_coarse).astype(jnp.bfloat16)
    below_row = from_behind(coarse[:, :1], "height", -1)
    upsampled = conv_plain(jnp.concatenate([coarse, below_row], 1), full_up, 1, ((1, 0), (1, 2)), 2)
    output = (frames.astype(jnp.float32) + upsampled).astype(jnp.bfloat16)
    cotangent_above = from_behind(cotangent[:, -1:], "height", 1)
    padded_cotangent = jnp.pad(jnp.concatenate([cotangent_above, cotangent], 1), LEFT_PAD)
    grad_coarse = conv_plain(padded_cotangent, flipped(full_up), 2, FLAT, 1)
    grad_pre_coarse = (grad_coarse * silu_slope(pre_coarse)).astype(jnp.bfloat16)
    grad_below = from_behind(grad_pre_coarse[:, :1], "height", -1)
    grad_hidden = conv_plain(
        jnp.concatenate([grad_pre_coarse, grad_below], 1),
        flipped(full_down),
        1,
        ((1, 0), (1, 2)),
        2,
    )
    grad_pre_fine = (grad_hidden * silu_slope(pre_fine)).astype(jnp.bfloat16)
    halo_grad = padded(grad_pre_fine, (("height", 1),), 1)
    grad_input = conv_plain(jnp.pad(halo_grad, SIDE_PAD), flipped(full_in), 1, FLAT, 1)
    input_grad = (cotangent.astype(jnp.float32) + grad_input).astype(jnp.bfloat16)
    grad_first = kernel_grad(padded_in, grad_pre_fine, 1)
    grad_second = kernel_grad(padded_hidden, grad_pre_coarse, 2)
    grad_third = flipped(kernel_grad(padded_cotangent, coarse, 2))
    count = lax.axis_size("dp")
    summed = reduce_over_all(pack(*(by_shard(grad, count) for grad in (grad_first, grad_second, grad_third))))
    pixel_count = count * frames.shape[0] * frames.shape[1] * lax.axis_size("height") * frames.shape[2]
    factor = 1.0 / math.sqrt(pixel_count)
    index = lax.axis_index("height")
    shares = []
    for part in unpack(summed[None] * factor):
        width = part.shape[3] // lax.axis_size("height")
        share = lax.dynamic_slice_in_dim(part[0], index * width, width, axis=2)
        shares.append(share.reshape(3, 3, part.shape[2], width))
    return (output, input_grad, *shares)


def solution(mesh):
    in_specs = (
        P("dp", "height", None, None),
        P("dp", "height", None, None),
        P(None, None, "dp", None),
        P(None, None, "dp", None),
        P(None, None, "dp", None),
    )
    out_specs = (
        P("dp", "height", None, None),
        P("dp", "height", None, None),
        P(None, None, "dp", "height"),
        P(None, None, "dp", "height"),
        P(None, None, "dp", "height"),
    )
    return jax.shard_map(
        on_device, mesh=mesh, in_specs=in_specs, out_specs=out_specs, check_vma=False
    )
```

```python
import math

import jax
import jax.numpy as jnp
from jax import lax
from jax.experimental import pallas as pl
from jax.experimental.pallas import tpu as pltpu
from jax.sharding import PartitionSpec as P

F32, BF16 = jnp.float32, jnp.bfloat16
MESH = pl.DeviceIdType.MESH

PACK = 208
DOWN_AT = 48
UP_AT = 128
PIECE = 64
PIECE_STEP = 48
HOPS = (1, -1, 2, -2, 3, -3, 4)


def place():
    d = lax.axis_index("dp")
    h = lax.axis_index("height")
    z = lax.rem(lax.div(h, 2), 2) * 8 + lax.rem(d, 8)
    return lax.div(h, 4), lax.div(d, 8), z, lax.rem(h, 2)


def device(x, y, z, core):
    return (y * 8 + lax.rem(z, 8), x * 4 + lax.div(z, 8) * 2 + core)


def on_ring(position, by, size):
    return lax.rem(position + by + size, size)


def remote(source, target, sends, recvs, slot, where):
    return pltpu.make_async_remote_copy(
        src_ref=source,
        dst_ref=target,
        send_sem=sends.at[slot],
        recv_sem=recvs.at[slot],
        device_id=where,
        device_id_type=MESH,
    )


def meet(partners):
    barrier = pltpu.get_barrier_semaphore()
    for partner in partners:
        pl.semaphore_signal(barrier, inc=1, device_id=partner, device_id_type=MESH)
    pl.semaphore_wait(barrier, len(partners))


def gather_kernel(
    own,
    frames,
    cotangent,
    full,
    frames_above,
    frames_below,
    cotangent_above,
    cotangent_below,
    z_send,
    z_recv,
    y_send,
    y_recv,
    c_send,
    c_recv,
    h_send,
    h_recv,
):
    x, y, z, core = place()
    z_lo = lax.rem(z, 8)
    mine = y * 8 + z_lo
    holder = lax.div(z_lo, 4) == core
    other = device(x, y, z, 1 - core)
    row, band = lax.axis_index("dp"), lax.axis_index("height")
    over, under = (row, on_ring(band, -1, 16)), (row, on_ring(band, 1, 16))
    meet(
        [device(x, y, on_ring(z, by, 16), core) for by in (1, -1, 2, -2, 3, -3, 4, -4)]
        + [device(x, on_ring(y, by, 4), z, core) for by in (1, 2, 3)]
        + [other, over, under]
    )

    def halo(slot, source, rows, target, where):
        return remote(source.at[rows], target, h_send, h_recv, slot, where)

    downward = (
        halo(0, frames, pl.ds(12, 4), frames_above, under),
        halo(1, cotangent, pl.ds(13, 3), cotangent_above, under),
    )
    upward = (
        halo(2, frames, pl.ds(0, 3), frames_below, over),
        halo(3, cotangent, pl.ds(0, 2), cotangent_below, over),
    )
    first, last = band == 0, band == 15

    def unless(condition, action):
        @pl.when(jnp.logical_not(condition))
        def _():
            action()

    def along_z(slot, by):
        return remote(own, full.at[mine], z_send, z_recv, slot, device(x, y, on_ring(z, by, 16), core))

    @pl.when(holder)
    def _():
        for slot, by in enumerate(HOPS):
            along_z(slot, by).start()
        full[mine] = own[...]

    unless(last, lambda: [copy.start() for copy in downward])
    unless(first, lambda: [copy.start() for copy in upward])

    @pl.when(first)
    def _():
        frames_above[...] = jnp.zeros_like(frames_above)
        cotangent_above[...] = jnp.zeros_like(cotangent_above)

    @pl.when(last)
    def _():
        frames_below[...] = jnp.zeros_like(frames_below)
        cotangent_below[...] = jnp.zeros_like(cotangent_below)

    for slot, by in enumerate(HOPS):
        source = lax.rem(on_ring(z, -by, 16), 8)

        @pl.when(lax.div(source, 4) == core)
        def _():
            along_z(slot, by).wait_recv()

    def block(by, half):
        return full.at[pl.ds(on_ring(y, -by, 4) * 8 + half * 4, 4)]

    def along_y(by):
        return remote(block(0, core), block(0, core), y_send, y_recv, by - 1, device(x, on_ring(y, by, 4), z, core))

    def across(by):
        return remote(block(by, core), block(by, core), c_send, c_recv, by, other)

    for by in (1, 3, 2):
        along_y(by).start()
    across(0).start()
    for by in (1, 3, 2):
        along_y(by).wait_recv()
        across(by).start()
    for by in range(4):
        across(by).wait_recv()

    @pl.when(holder)
    def _():
        for slot, by in enumerate(HOPS):
            along_z(slot, by).wait_send()

    for by in (1, 2, 3):
        along_y(by).wait_send()
    for by in range(4):
        across(by).wait_send()
    unless(first, lambda: [copy.wait_recv() for copy in downward])
    unless(last, lambda: [copy.wait_recv() for copy in upward])
    unless(last, lambda: [copy.wait_send() for copy in downward])
    unless(first, lambda: [copy.wait_send() for copy in upward])


def gather(packed, frames, cotangent):
    return pl.pallas_call(
        gather_kernel,
        out_shape=(
            jax.ShapeDtypeStruct((32, PACK, 128), BF16),
            jax.ShapeDtypeStruct((4, 128, 128), BF16),
            jax.ShapeDtypeStruct((3, 128, 128), BF16),
            jax.ShapeDtypeStruct((3, 128, 128), BF16),
            jax.ShapeDtypeStruct((2, 128, 128), BF16),
        ),
        in_specs=[pl.BlockSpec(memory_space=pltpu.VMEM)] + [pl.BlockSpec(memory_space=pl.ANY)] * 2,
        out_specs=(pl.BlockSpec(memory_space=pltpu.VMEM),) * 5,
        scratch_shapes=[
            pltpu.SemaphoreType.DMA((7,)),
            pltpu.SemaphoreType.DMA((7,)),
            pltpu.SemaphoreType.DMA((3,)),
            pltpu.SemaphoreType.DMA((3,)),
            pltpu.SemaphoreType.DMA((4,)),
            pltpu.SemaphoreType.DMA((4,)),
            pltpu.SemaphoreType.DMA((4,)),
            pltpu.SemaphoreType.DMA((4,)),
        ],
        compiler_params=pltpu.CompilerParams(
            collective_id=0, has_side_effects=True, vmem_limit_bytes=32 << 20
        ),
    )(packed, frames, cotangent)


def spread_columns(rows, first, wide, stacked, slots):
    count = rows.shape[0]
    wide[pl.ds(first, count), 8:136] = rows[...].astype(F32)
    for row in range(first, first + count):
        target = stacked.at[row] if len(stacked.shape) == 3 else stacked.at[row // 2, row % 2]
        for slot in range(slots):
            target[:, slot * 128 : slot * 128 + 128] = wide[row, pl.ds(7 + slot, 64, stride=2), :].astype(BF16)


def matmul(left, right):
    return lax.dot_general(left, right, (((1,), (0,)), ((), ())), preferred_element_type=F32)


def matmul_t(left, right):
    return lax.dot_general(left, right, (((1,), (1,)), ((), ())), preferred_element_type=F32)


def flat(cells):
    return cells.reshape(cells.shape[0] * cells.shape[1], cells.shape[2])


def shuffle(taps, channels, pitch, transposed):
    shards = 16 // channels
    dims = (shards * pitch, taps * 16) if transposed else (taps * 16, shards * pitch)
    row = lax.broadcasted_iota(jnp.int32, dims, 1 if transposed else 0)
    column = lax.broadcasted_iota(jnp.int32, dims, 0 if transposed else 1)
    bits = channels.bit_length() - 1
    wanted = ((row & 15) >> bits) * pitch + (row >> 4) * channels + (row & (channels - 1))
    return (column == wanted).astype(F32).astype(BF16)


def unpack_weights(full, win, wdn, wup):
    order = shuffle(9, 4, 48, False)
    for group in range(8):
        rows = matmul(order, full[4 * group : 4 * group + 4, 0:DOWN_AT].reshape(192, 128)).astype(BF16)
        win[:, 16 * group : 16 * group + 16] = rows.reshape(9, 16, 128)
    order = shuffle(18, 4, 80, False)
    for group in range(8):
        rows = matmul(order, full[4 * group : 4 * group + 4, DOWN_AT:UP_AT].reshape(320, 128)).astype(BF16)
        wdn[:, 16 * group : 16 * group + 16, 0:128] = rows[0:144].reshape(9, 16, 128)
        wdn[:, 16 * group : 16 * group + 16, 128:256] = rows[144:288].reshape(9, 16, 128)
    order = shuffle(9, 8, 80, False)
    for group in range(16):
        rows = matmul(order, full[2 * group : 2 * group + 2, UP_AT:PACK].reshape(160, 128)).astype(BF16)
        wup[:, 16 * group : 16 * group + 16] = rows.reshape(9, 16, 128)


def pack_sums(parts, sin, sdn, sup):
    order = shuffle(9, 4, 48, True)
    for group in range(8):
        rows = matmul(order, sin[:, 16 * group : 16 * group + 16].reshape(144, 128)).astype(BF16)
        parts[4 * group : 4 * group + 4, 0:DOWN_AT] = rows.reshape(4, 48, 128)
    order = shuffle(18, 4, 80, True)
    for group in range(8):
        halves = [sdn[:, 16 * group : 16 * group + 16, at : at + 128].reshape(144, 128) for at in (0, 128)]
        rows = matmul(order, jnp.concatenate(halves, axis=0)).astype(BF16)
        parts[4 * group : 4 * group + 4, DOWN_AT:UP_AT] = rows.reshape(4, 80, 128)
    order = shuffle(9, 8, 80, True)
    for group in range(16):
        rows = matmul(order, sup[:, 16 * group : 16 * group + 16].reshape(144, 128)).astype(BF16)
        parts[2 * group : 2 * group + 2, UP_AT:PACK] = rows.reshape(2, 80, 128)


def stack_weights(win, wdn, wup, fine, down, up, back_fine, back_down, back_up):
    blank = jnp.zeros((128, 128), BF16)
    for j in range(3):
        for slot in range(4):
            at = slice(slot * 128, slot * 128 + 128)
            fine[j, at, 0:128] = win[3 * j + slot] if slot < 3 else blank
            fine[j, at, 128:256] = win[3 * j + slot - 1] if slot > 0 else blank
            back_fine[j, 0:128, at] = win[3 * (2 - j) + 2 - slot] if slot < 3 else blank
            back_fine[j, 128:256, at] = win[3 * (2 - j) + 3 - slot] if slot > 0 else blank
        for slot in range(3):
            at = slice(slot * 128, slot * 128 + 128)
            down[j, at, :] = wdn[3 * j + slot]
            back_up[j, :, at] = wup[3 * (2 - j) + 2 - slot]
        up[j, 0:256, 0:128] = wup[3 * j + 1]
        up[j, 0:256, 128:256] = wup[3 * j]
        up[j, 256:512, 0:128] = jnp.zeros((256, 128), BF16)
        up[j, 256:512, 128:256] = wup[3 * j + 2]
        back_down[j, 0:128, 0:256] = wdn[3 * j + 1]
        back_down[j, 0:128, 256:512] = jnp.zeros((128, 256), BF16)
        back_down[j, 128:256, 0:256] = wdn[3 * j + 2]
        back_down[j, 128:256, 256:512] = wdn[3 * j]


def sigmoid(value):
    return 1.0 / (1.0 + jnp.exp(-value))


def compute_kernel(
    frames,
    frames_above,
    frames_below,
    cotangent,
    cotangent_above,
    cotangent_below,
    full,
    output,
    input_grad,
    parts,
    wide,
    fx,
    h3,
    c3,
    slopes,
    shifted,
    shifted_wide,
    coarse2,
    grad2,
    gx,
    mixed,
    win,
    wdn,
    wup,
    fine,
    down,
    up,
    back_fine,
    back_down,
    back_up,
):
    band = lax.axis_index("height")
    top, bottom = band == 0, band == lax.axis_size("height") - 1
    unpack_weights(full, win, wdn, wup)
    stack_weights(win, wdn, wup, fine, down, up, back_fine, back_down, back_up)

    wide[:, 0:8] = jnp.zeros((23, 8, 128), F32)
    wide[:, 136:144] = jnp.zeros((23, 8, 128), F32)
    shifted[:, 0:8] = jnp.zeros((9, 8, 128), F32)
    shifted[:, 72:80] = jnp.zeros((9, 8, 128), F32)
    shifted_wide[:, 64:72] = jnp.zeros((10, 8, 256), F32)
    spread_columns(frames_above, 0, wide, fx, 4)
    spread_columns(frames, 4, wide, fx, 4)
    spread_columns(frames_below, 20, wide, fx, 4)

    for first in (0, 7, 14):
        pre = sum(matmul(flat(fx[first + j : first + j + 7]), fine[j]) for j in range(3))
        gate = sigmoid(pre)
        hidden = (pre * gate).reshape(7, 64, 256)
        slope = (gate * (1.0 + pre * (1.0 - gate))).reshape(7, 64, 256)
        shifted[0:7, 8:72] = hidden[:, :, 128:256]
        before = shifted[0:7, 7:71].astype(BF16)
        hidden = hidden.astype(BF16)
        for row in range(7):
            i = first + row
            h3[i // 2, i % 2, :, 0:128] = before[row]
            h3[i // 2, i % 2, :, 128:384] = hidden[row]
            if 2 <= i < 20:
                slopes[i - 2] = slope[row]

    @pl.when(top)
    def _():
        for i in range(3):
            h3[i // 2, i % 2] = jnp.zeros((64, 384), BF16)

    @pl.when(bottom)
    def _():
        for i in (19, 20):
            h3[i // 2, i % 2] = jnp.zeros((64, 384), BF16)

    spread_columns(cotangent_above, 0, wide, c3, 3)
    spread_columns(cotangent, 3, wide, c3, 3)
    spread_columns(cotangent_below, 19, wide, c3, 3)

    views = ((0, 0), (0, 1), (1, 0))
    pre = sum(matmul(flat(h3[a : a + 10, b]), down[j]) for j, (a, b) in enumerate(views))
    gate = sigmoid(pre)
    coarse = (pre * gate).reshape(10, 64, 256)
    shifted_wide[:, 0:64] = coarse
    coarse2[:, :, 0:256] = coarse.astype(BF16)
    coarse2[:, :, 256:512] = shifted_wide[:, 1:65].astype(BF16)
    back = sum(matmul_t(flat(c3[a : a + 10, b]), back_up[j]) for j, (a, b) in enumerate(views))
    grad = (back * (gate * (1.0 + pre * (1.0 - gate)))).reshape(10, 64, 256)
    shifted_wide[:, 0:64] = grad
    grad2[:, :, 0:256] = grad.astype(BF16)
    grad2[:, :, 256:512] = shifted_wide[:, 1:65].astype(BF16)

    @pl.when(top)
    def _():
        grad2[0] = jnp.zeros((64, 512), BF16)

    @pl.when(bottom)
    def _():
        coarse2[9] = jnp.zeros((64, 512), BF16)
        grad2[9] = jnp.zeros((64, 512), BF16)

    def mix(row, cells):
        mixed[row, pl.ds(0, 64, stride=2), :] = cells[:, 0:128]
        mixed[row, pl.ds(1, 64, stride=2), :] = cells[:, 128:256]

    even = matmul(flat(coarse2[1:9]), up[1])
    odd = matmul(flat(coarse2[1:9]), up[0]) + matmul(flat(coarse2[2:10]), up[2])
    for t in range(8):
        mix(2 * t, even[64 * t : 64 * t + 64])
        mix(2 * t + 1, odd[64 * t : 64 * t + 64])
    output[...] = (frames[...].astype(F32) + mixed[...]).astype(BF16)

    grad_even = matmul_t(flat(grad2[1:10]), back_down[1]).reshape(9, 64, 256)
    grad_odd = (
        matmul_t(flat(grad2[0:9]), back_down[2]) + matmul_t(flat(grad2[1:10]), back_down[0])
    ).reshape(9, 64, 256)
    for start, rows in ((0, grad_odd), (1, grad_even)):
        rows = jnp.concatenate([rows[m : m + 1] * slopes[start + 2 * m][None] for m in range(9)], axis=0)
        ready = rows.astype(BF16)
        shifted[:, 8:72] = rows[:, :, 128:256]
        before = shifted[:, 7:71].astype(BF16)
        shifted[:, 8:72] = rows[:, :, 0:128]
        after = shifted[:, 9:73].astype(BF16)
        for m in range(9):
            gx[start + 2 * m, :, 0:128] = before[m]
            gx[start + 2 * m, :, 128:384] = ready[m]
            gx[start + 2 * m, :, 384:512] = after[m]

    @pl.when(top)
    def _():
        gx[0] = jnp.zeros((64, 512), BF16)

    @pl.when(bottom)
    def _():
        gx[17] = jnp.zeros((64, 512), BF16)

    for first in (0, 8):
        back = sum(matmul_t(flat(gx[first + j : first + j + 8]), back_fine[j]) for j in range(3))
        for row in range(8):
            mix(first + row, back[64 * row : 64 * row + 64])
    input_grad[...] = (cotangent[...].astype(F32) + mixed[...]).astype(BF16)

    turned = flat(coarse2[1:9, :, 0:256]).T
    for j, (a, b) in enumerate(views):
        found = matmul(turned, flat(c3[a + 1 : a + 9, b]))
        for slot in range(3):
            wup[3 * (2 - j) + 2 - slot] = found[:, slot * 128 : slot * 128 + 128].astype(BF16)
    turned = flat(grad2[1:9, :, 0:256]).T
    for j, (a, b) in enumerate(views):
        found = matmul(turned, flat(h3[a + 1 : a + 9, b]))
        for slot in range(3):
            wdn[3 * j + slot] = found[:, slot * 128 : slot * 128 + 128].T.astype(BF16)
    turned = flat(gx[1:17, :, 128:384]).T
    for j in range(3):
        found = matmul(turned, flat(fx[3 + j : 19 + j]))
        for l in range(3):
            both = found[0:128, l * 128 : l * 128 + 128] + found[128:256, (l + 1) * 128 : (l + 2) * 128]
            win[3 * j + l] = both.T.astype(BF16)
    pack_sums(parts, win, wdn, wup)


def compute(frames, frames_above, frames_below, cotangent, cotangent_above, cotangent_below, full):
    vmem = pltpu.VMEM
    whole = pl.BlockSpec(memory_space=vmem)
    return pl.pallas_call(
        compute_kernel,
        out_shape=(
            jax.ShapeDtypeStruct((16, 128, 128), BF16),
            jax.ShapeDtypeStruct((16, 128, 128), BF16),
            jax.ShapeDtypeStruct((32, PACK, 128), BF16),
        ),
        in_specs=[whole] * 7,
        out_specs=(whole,) * 3,
        scratch_shapes=[
            vmem((23, 144, 128), F32),
            vmem((23, 64, 512), BF16),
            vmem((11, 2, 64, 384), BF16),
            vmem((11, 2, 64, 384), BF16),
            vmem((18, 64, 256), F32),
            vmem((9, 80, 128), F32),
            vmem((10, 72, 256), F32),
            vmem((10, 64, 512), BF16),
            vmem((10, 64, 512), BF16),
            vmem((18, 64, 512), BF16),
            vmem((16, 128, 128), F32),
            vmem((9, 128, 128), BF16),
            vmem((9, 128, 256), BF16),
            vmem((9, 256, 128), BF16),
            vmem((3, 512, 256), BF16),
            vmem((3, 384, 256), BF16),
            vmem((3, 512, 256), BF16),
            vmem((3, 256, 512), BF16),
            vmem((3, 256, 512), BF16),
            vmem((3, 256, 384), BF16),
        ],
        compiler_params=pltpu.CompilerParams(vmem_limit_bytes=48 << 20),
    )(frames, frames_above, frames_below, cotangent, cotangent_above, cotangent_below, full)


def reduce_kernel(
    parts,
    total,
    from_core,
    to_y,
    from_y,
    sums,
    to_z,
    from_z,
    column,
    from_x,
    piece,
    from_far,
    done,
    all_pieces,
    c_send,
    c_recv,
    y_send,
    y_recv,
    z_send,
    z_recv,
    x_send,
    x_recv,
    f_send,
    f_recv,
    a_send,
    a_recv,
    b_send,
    b_recv,
):
    x, y, z, core = place()
    z_lo = lax.rem(z, 8)
    holder = lax.div(z_lo, 4) == core
    other = device(x, y, z, 1 - core)
    far = on_ring(z, 8, 16)
    meet(
        [device(x, y, on_ring(z, by, 16), core) for by in (1, -1, 2, -2, 3, -3, 4, -4, 8)]
        + [device(x, on_ring(y, by, 4), z, core) for by in (1, 2, 3)]
        + [device(on_ring(x, by, 4), y, z, core) for by in (1, 2, 3)]
        + [device(on_ring(x, by, 4), y, z, 1 - core) for by in (0, 1, 2, 3)]
    )

    def rows_of(by, half):
        return pl.ds(on_ring(y, by, 4) * 8 + half * 4, 4)

    def across(by):
        return remote(parts.at[rows_of(by, 1 - core)], from_core.at[by], c_send, c_recv, by, other)

    def along_y(by):
        return remote(to_y.at[by - 1], from_y.at[by - 1], y_send, y_recv, by - 1, device(x, on_ring(y, by, 4), z, core))

    for by in (1, 3, 2, 0):
        across(by).start()
    for by in (1, 3, 2):
        across(by).wait_recv()
        to_y[by - 1] = (
            parts[rows_of(by, core)].astype(F32) + from_core[by].astype(F32)
        ).astype(BF16)
        along_y(by).start()
    across(0).wait_recv()
    sums[...] = parts[rows_of(0, core)].astype(F32) + from_core[0].astype(F32)
    for by in (1, 3, 2):
        along_y(by).wait_recv()
        sums[...] += from_y[by - 1].astype(F32)
    to_z[...] = sums[...].astype(BF16)

    def along_z(slot, by):
        where = on_ring(z, by, 16)
        return remote(
            to_z.at[lax.rem(where, 4)], from_z.at[slot], z_send, z_recv, slot, device(x, y, where, core)
        )

    for slot, by in enumerate(HOPS):

        @pl.when(lax.div(lax.rem(on_ring(z, by, 16), 8), 4) == core)
        def _():
            along_z(slot, by).start()

    def along_x(by):
        where = on_ring(x, by, 4)
        return remote(
            column.at[pl.ds(where * PIECE_STEP, PIECE)],
            from_x.at[by - 1],
            x_send,
            x_recv,
            by - 1,
            device(where, y, z, core),
        )

    def to_far():
        return remote(piece, from_far, f_send, f_recv, 0, device(x, y, far, core))

    def spread(by):
        return remote(done, all_pieces.at[x], a_send, a_recv, by, device(on_ring(x, by, 4), y, z, core))

    def spread_other(by):
        return remote(done, all_pieces.at[x], b_send, b_recv, by, device(on_ring(x, by, 4), y, z, 1 - core))

    @pl.when(holder)
    def _():
        column[...] = sums[lax.rem(z_lo, 4)]
        for slot, by in enumerate(HOPS):
            along_z(slot, by).wait_recv()
            column[...] += from_z[slot].astype(F32)
        for by in (1, 3, 2):
            along_x(by).start()
        piece[...] = column[pl.ds(x * PIECE_STEP, PIECE)]
        for by in (1, 3, 2):
            along_x(by).wait_recv()
            piece[...] += from_x[by - 1]
        to_far().start()
        to_far().wait_recv()
        done[...] = piece[...] + from_far[...]
        for by in (2, 1, 3):
            spread(by).start()
        for by in (2, 1, 3, 0):
            spread_other(by).start()
        all_pieces[x] = done[...]
        for by in (1, 2, 3):
            spread(by).wait_recv()
        for by in (1, 2, 3):
            along_x(by).wait_send()
        to_far().wait_send()
        for by in (1, 2, 3):
            spread(by).wait_send()
        for by in range(4):
            spread_other(by).wait_send()

    @pl.when(jnp.logical_not(holder))
    def _():
        for by in range(4):
            spread_other(by).wait_recv()

    for source in range(4):
        total[pl.ds(source * PIECE_STEP, PIECE)] = all_pieces[source]
    for by in range(4):
        across(by).wait_send()
    for by in (1, 2, 3):
        along_y(by).wait_send()
    for slot, by in enumerate(HOPS):

        @pl.when(lax.div(lax.rem(on_ring(z, by, 16), 8), 4) == core)
        def _():
            along_z(slot, by).wait_send()


def reduce_over_all(parts):
    dma = pltpu.SemaphoreType.DMA
    counts = (4, 3, 7, 3, 1, 4, 4)
    return pl.pallas_call(
        reduce_kernel,
        out_shape=jax.ShapeDtypeStruct((PACK, 128), F32),
        in_specs=[pl.BlockSpec(memory_space=pltpu.VMEM)],
        out_specs=pl.BlockSpec(memory_space=pltpu.VMEM),
        scratch_shapes=[
            pltpu.VMEM((4, 4, PACK, 128), BF16),
            pltpu.VMEM((3, 4, PACK, 128), BF16),
            pltpu.VMEM((3, 4, PACK, 128), BF16),
            pltpu.VMEM((4, PACK, 128), F32),
            pltpu.VMEM((4, PACK, 128), BF16),
            pltpu.VMEM((7, PACK, 128), BF16),
            pltpu.VMEM((PACK, 128), F32),
            pltpu.VMEM((3, PIECE, 128), F32),
            pltpu.VMEM((PIECE, 128), F32),
            pltpu.VMEM((PIECE, 128), F32),
            pltpu.VMEM((PIECE, 128), F32),
            pltpu.VMEM((4, PIECE, 128), F32),
        ]
        + [dma((count,)) for count in counts for _ in range(2)],
        compiler_params=pltpu.CompilerParams(
            collective_id=1, has_side_effects=True, vmem_limit_bytes=32 << 20
        ),
    )(parts)


def pack(w_in, w_down, w_up):
    def rows(kernel, size):
        return jnp.pad(kernel, ((0, 0), (0, size - kernel.shape[1]), (0, 0)))

    count = w_in.shape[0]
    halves = w_down.reshape(count, 36, 2, 128).transpose(0, 2, 1, 3).reshape(count, 72, 128)
    return jnp.concatenate(
        [
            rows(w_in.reshape(count, 36, 128), DOWN_AT),
            rows(halves, UP_AT - DOWN_AT),
            rows(w_up.reshape(count, 72, 128), PACK - UP_AT),
        ],
        axis=1,
    )


def unpack(packed):
    count = packed.shape[0]
    halves = packed[:, DOWN_AT : DOWN_AT + 72].reshape(count, 2, 36, 128).transpose(0, 2, 1, 3)
    return (
        packed[:, :36].reshape(count, 9, 4, 128),
        halves.reshape(count, 9, 4, 256),
        packed[:, UP_AT : UP_AT + 72].reshape(count, 9, 8, 128),
    )


def on_device(frames, cotangent, w_in, w_down, w_up):
    frames, cotangent = frames[0], cotangent[0]
    full, *halos = gather(pack(w_in[None], w_down[None], w_up[None])[0], frames, cotangent)
    output, input_grad, parts = compute(frames, *halos[:2], cotangent, *halos[2:], full)
    summed = reduce_over_all(parts)
    height = lax.axis_size("height")
    pixel_count = lax.axis_size("dp") * height * frames.shape[0] * frames.shape[1]
    factor = 1.0 / math.sqrt(pixel_count)
    index = lax.axis_index("height")
    shares = []
    for part in unpack(summed[None] * factor):
        width = part.shape[3] // height
        share = lax.dynamic_slice_in_dim(part[0], index * width, width, axis=2)
        shares.append(share.reshape(3, 3, part.shape[2], width))
    return (output[None], input_grad[None], *shares)


def solution(mesh):
    in_specs = (
        P("dp", "height", None, None),
        P("dp", "height", None, None),
        P(None, None, "dp", None),
        P(None, None, "dp", None),
        P(None, None, "dp", None),
    )
    out_specs = (
        P("dp", "height", None, None),
        P("dp", "height", None, None),
        P(None, None, "dp", "height"),
        P(None, None, "dp", "height"),
        P(None, None, "dp", "height"),
    )
    return jax.shard_map(
        on_device, mesh=mesh, in_specs=in_specs, out_specs=out_specs, check_vma=False
    )
```

```python
import math

import jax
import jax.numpy as jnp
from jax import lax
from jax.experimental import pallas as pl
from jax.experimental.pallas import tpu as pltpu
from jax.sharding import PartitionSpec as P

F32, BF16 = jnp.float32, jnp.bfloat16
MESH = pl.DeviceIdType.MESH

PACK = 208
DOWN_AT = 48
UP_AT = 128
PIECE = 64
PIECE_STEP = 48
HOPS = (1, -1, 2, -2, 3, -3, 4)


def place():
    d = lax.axis_index("dp")
    h = lax.axis_index("height")
    z = lax.rem(lax.div(h, 2), 2) * 8 + lax.rem(d, 8)
    return lax.div(h, 4), lax.div(d, 8), z, lax.rem(h, 2)


def device(x, y, z, core):
    return (y * 8 + lax.rem(z, 8), x * 4 + lax.div(z, 8) * 2 + core)


def on_ring(position, by, size):
    return lax.rem(position + by + size, size)


def remote(source, target, sends, recvs, slot, where):
    return pltpu.make_async_remote_copy(
        src_ref=source,
        dst_ref=target,
        send_sem=sends.at[slot],
        recv_sem=recvs.at[slot],
        device_id=where,
        device_id_type=MESH,
    )


def meet(partners):
    barrier = pltpu.get_barrier_semaphore()
    for partner in partners:
        pl.semaphore_signal(barrier, inc=1, device_id=partner, device_id_type=MESH)
    pl.semaphore_wait(barrier, len(partners))


def gather_kernel(
    own,
    frames,
    cotangent,
    full,
    frames_above,
    frames_below,
    cotangent_above,
    cotangent_below,
    z_send,
    z_recv,
    y_send,
    y_recv,
    c_send,
    c_recv,
    h_send,
    h_recv,
):
    x, y, z, core = place()
    z_lo = lax.rem(z, 8)
    mine = y * 8 + z_lo
    holder = lax.div(z_lo, 4) == core
    other = device(x, y, z, 1 - core)
    row, band = lax.axis_index("dp"), lax.axis_index("height")
    over, under = (row, on_ring(band, -1, 16)), (row, on_ring(band, 1, 16))

    def halo(slot, source, rows, target, where):
        return remote(source.at[rows], target, h_send, h_recv, slot, where)

    downward = (
        halo(0, frames, pl.ds(12, 4), frames_above, under),
        halo(1, cotangent, pl.ds(13, 3), cotangent_above, under),
    )
    upward = (
        halo(2, frames, pl.ds(0, 3), frames_below, over),
        halo(3, cotangent, pl.ds(0, 2), cotangent_below, over),
    )
    first, last = band == 0, band == 15

    def unless(condition, action):
        @pl.when(jnp.logical_not(condition))
        def _():
            action()

    def along_z(slot, by):
        return remote(own, full.at[mine], z_send, z_recv, slot, device(x, y, on_ring(z, by, 16), core))

    @pl.when(holder)
    def _():
        for slot, by in enumerate(HOPS):
            along_z(slot, by).start()
        full[mine] = own[...]

    unless(last, lambda: [copy.start() for copy in downward])
    unless(first, lambda: [copy.start() for copy in upward])

    @pl.when(first)
    def _():
        frames_above[...] = jnp.zeros_like(frames_above)
        cotangent_above[...] = jnp.zeros_like(cotangent_above)

    @pl.when(last)
    def _():
        frames_below[...] = jnp.zeros_like(frames_below)
        cotangent_below[...] = jnp.zeros_like(cotangent_below)

    for slot, by in enumerate(HOPS):
        source = lax.rem(on_ring(z, -by, 16), 8)

        @pl.when(lax.div(source, 4) == core)
        def _():
            along_z(slot, by).wait_recv()

    def block(by, half):
        return full.at[pl.ds(on_ring(y, -by, 4) * 8 + half * 4, 4)]

    def along_y(by):
        return remote(block(0, core), block(0, core), y_send, y_recv, by - 1, device(x, on_ring(y, by, 4), z, core))

    def across(by):
        return remote(block(by, core), block(by, core), c_send, c_recv, by, other)

    for by in (1, 3, 2):
        along_y(by).start()
    across(0).start()
    for by in (1, 3, 2):
        along_y(by).wait_recv()
        across(by).start()
    for by in range(4):
        across(by).wait_recv()

    @pl.when(holder)
    def _():
        for slot, by in enumerate(HOPS):
            along_z(slot, by).wait_send()

    for by in (1, 2, 3):
        along_y(by).wait_send()
    for by in range(4):
        across(by).wait_send()
    unless(first, lambda: [copy.wait_recv() for copy in downward])
    unless(last, lambda: [copy.wait_recv() for copy in upward])
    unless(last, lambda: [copy.wait_send() for copy in downward])
    unless(first, lambda: [copy.wait_send() for copy in upward])


def spread_columns(rows, first, wide, stacked, slots):
    count = rows.shape[0]
    wide[pl.ds(first, count), 8:136] = rows[...].astype(F32)
    for row in range(first, first + count):
        target = stacked.at[row] if len(stacked.shape) == 3 else stacked.at[row // 2, row % 2]
        for slot in range(slots):
            target[:, slot * 128 : slot * 128 + 128] = wide[row, pl.ds(7 + slot, 64, stride=2), :].astype(BF16)


def matmul(left, right):
    return lax.dot_general(left, right, (((1,), (0,)), ((), ())), preferred_element_type=F32)


def matmul_t(left, right):
    return lax.dot_general(left, right, (((1,), (1,)), ((), ())), preferred_element_type=F32)


def flat(cells):
    return cells.reshape(cells.shape[0] * cells.shape[1], cells.shape[2])


def shuffle(taps, channels, pitch, transposed):
    shards = 16 // channels
    dims = (shards * pitch, taps * 16) if transposed else (taps * 16, shards * pitch)
    row = lax.broadcasted_iota(jnp.int32, dims, 1 if transposed else 0)
    column = lax.broadcasted_iota(jnp.int32, dims, 0 if transposed else 1)
    bits = channels.bit_length() - 1
    wanted = ((row & 15) >> bits) * pitch + (row >> 4) * channels + (row & (channels - 1))
    return (column == wanted).astype(F32).astype(BF16)


def unpack_weights(full, win, wdn, wup):
    order = shuffle(9, 4, 48, False)
    for group in range(8):
        rows = matmul(order, full[4 * group : 4 * group + 4, 0:DOWN_AT].reshape(192, 128)).astype(BF16)
        win[:, 16 * group : 16 * group + 16] = rows.reshape(9, 16, 128)
    order = shuffle(18, 4, 80, False)
    for group in range(8):
        rows = matmul(order, full[4 * group : 4 * group + 4, DOWN_AT:UP_AT].reshape(320, 128)).astype(BF16)
        wdn[:, 16 * group : 16 * group + 16, 0:128] = rows[0:144].reshape(9, 16, 128)
        wdn[:, 16 * group : 16 * group + 16, 128:256] = rows[144:288].reshape(9, 16, 128)
    order = shuffle(9, 8, 80, False)
    for group in range(16):
        rows = matmul(order, full[2 * group : 2 * group + 2, UP_AT:PACK].reshape(160, 128)).astype(BF16)
        wup[:, 16 * group : 16 * group + 16] = rows.reshape(9, 16, 128)


def pack_sums(parts, sin, sdn, sup):
    order = shuffle(9, 4, 48, True)
    for group in range(8):
        rows = matmul(order, sin[:, 16 * group : 16 * group + 16].reshape(144, 128)).astype(BF16)
        parts[4 * group : 4 * group + 4, 0:DOWN_AT] = rows.reshape(4, 48, 128)
    order = shuffle(18, 4, 80, True)
    for group in range(8):
        halves = [sdn[:, 16 * group : 16 * group + 16, at : at + 128].reshape(144, 128) for at in (0, 128)]
        rows = matmul(order, jnp.concatenate(halves, axis=0)).astype(BF16)
        parts[4 * group : 4 * group + 4, DOWN_AT:UP_AT] = rows.reshape(4, 80, 128)
    order = shuffle(9, 8, 80, True)
    for group in range(16):
        rows = matmul(order, sup[:, 16 * group : 16 * group + 16].reshape(144, 128)).astype(BF16)
        parts[2 * group : 2 * group + 2, UP_AT:PACK] = rows.reshape(2, 80, 128)


def stack_weights(win, wdn, wup, fine, down, up, back_fine, back_down, back_up):
    blank = jnp.zeros((128, 128), BF16)
    for j in range(3):
        for slot in range(4):
            at = slice(slot * 128, slot * 128 + 128)
            fine[j, at, 0:128] = win[3 * j + slot] if slot < 3 else blank
            fine[j, at, 128:256] = win[3 * j + slot - 1] if slot > 0 else blank
            back_fine[j, 0:128, at] = win[3 * (2 - j) + 2 - slot] if slot < 3 else blank
            back_fine[j, 128:256, at] = win[3 * (2 - j) + 3 - slot] if slot > 0 else blank
        for slot in range(3):
            at = slice(slot * 128, slot * 128 + 128)
            down[j, at, :] = wdn[3 * j + slot]
            back_up[j, :, at] = wup[3 * (2 - j) + 2 - slot]
        up[j, 0:256, 0:128] = wup[3 * j + 1]
        up[j, 0:256, 128:256] = wup[3 * j]
        up[j, 256:512, 0:128] = jnp.zeros((256, 128), BF16)
        up[j, 256:512, 128:256] = wup[3 * j + 2]
        back_down[j, 0:128, 0:256] = wdn[3 * j + 1]
        back_down[j, 0:128, 256:512] = jnp.zeros((128, 256), BF16)
        back_down[j, 128:256, 0:256] = wdn[3 * j + 2]
        back_down[j, 128:256, 256:512] = wdn[3 * j]


def sigmoid(value):
    return 1.0 / (1.0 + jnp.exp(-value))


def compute_kernel(
    frames,
    frames_above,
    frames_below,
    cotangent,
    cotangent_above,
    cotangent_below,
    full,
    output,
    input_grad,
    parts,
    wide,
    fx,
    h3,
    c3,
    slopes,
    shifted,
    shifted_wide,
    coarse2,
    grad2,
    gx,
    mixed,
    win,
    wdn,
    wup,
    fine,
    down,
    up,
    back_fine,
    back_down,
    back_up,
):
    band = lax.axis_index("height")
    top, bottom = band == 0, band == lax.axis_size("height") - 1
    unpack_weights(full, win, wdn, wup)
    stack_weights(win, wdn, wup, fine, down, up, back_fine, back_down, back_up)

    wide[:, 0:8] = jnp.zeros((23, 8, 128), F32)
    wide[:, 136:144] = jnp.zeros((23, 8, 128), F32)
    shifted[:, 0:8] = jnp.zeros((9, 8, 128), F32)
    shifted[:, 72:80] = jnp.zeros((9, 8, 128), F32)
    shifted_wide[:, 64:72] = jnp.zeros((10, 8, 256), F32)
    spread_columns(frames_above, 0, wide, fx, 4)
    spread_columns(frames, 4, wide, fx, 4)
    spread_columns(frames_below, 20, wide, fx, 4)

    for first in (0, 7, 14):
        pre = sum(matmul(flat(fx[first + j : first + j + 7]), fine[j]) for j in range(3))
        gate = sigmoid(pre)
        hidden = (pre * gate).reshape(7, 64, 256)
        slope = (gate * (1.0 + pre * (1.0 - gate))).reshape(7, 64, 256)
        shifted[0:7, 8:72] = hidden[:, :, 128:256]
        before = shifted[0:7, 7:71].astype(BF16)
        hidden = hidden.astype(BF16)
        for row in range(7):
            i = first + row
            h3[i // 2, i % 2, :, 0:128] = before[row]
            h3[i // 2, i % 2, :, 128:384] = hidden[row]
            if 2 <= i < 20:
                slopes[i - 2] = slope[row]

    @pl.when(top)
    def _():
        for i in range(3):
            h3[i // 2, i % 2] = jnp.zeros((64, 384), BF16)

    @pl.when(bottom)
    def _():
        for i in (19, 20):
            h3[i // 2, i % 2] = jnp.zeros((64, 384), BF16)

    spread_columns(cotangent_above, 0, wide, c3, 3)
    spread_columns(cotangent, 3, wide, c3, 3)
    spread_columns(cotangent_below, 19, wide, c3, 3)

    views = ((0, 0), (0, 1), (1, 0))
    pre = sum(matmul(flat(h3[a : a + 10, b]), down[j]) for j, (a, b) in enumerate(views))
    gate = sigmoid(pre)
    coarse = (pre * gate).reshape(10, 64, 256)
    shifted_wide[:, 0:64] = coarse
    coarse2[:, :, 0:256] = coarse.astype(BF16)
    coarse2[:, :, 256:512] = shifted_wide[:, 1:65].astype(BF16)
    back = sum(matmul_t(flat(c3[a : a + 10, b]), back_up[j]) for j, (a, b) in enumerate(views))
    grad = (back * (gate * (1.0 + pre * (1.0 - gate)))).reshape(10, 64, 256)
    shifted_wide[:, 0:64] = grad
    grad2[:, :, 0:256] = grad.astype(BF16)
    grad2[:, :, 256:512] = shifted_wide[:, 1:65].astype(BF16)

    @pl.when(top)
    def _():
        grad2[0] = jnp.zeros((64, 512), BF16)

    @pl.when(bottom)
    def _():
        coarse2[9] = jnp.zeros((64, 512), BF16)
        grad2[9] = jnp.zeros((64, 512), BF16)

    def mix(row, cells):
        mixed[row, pl.ds(0, 64, stride=2), :] = cells[:, 0:128]
        mixed[row, pl.ds(1, 64, stride=2), :] = cells[:, 128:256]

    even = matmul(flat(coarse2[1:9]), up[1])
    odd = matmul(flat(coarse2[1:9]), up[0]) + matmul(flat(coarse2[2:10]), up[2])
    for t in range(8):
        mix(2 * t, even[64 * t : 64 * t + 64])
        mix(2 * t + 1, odd[64 * t : 64 * t + 64])
    output[...] = (frames[...].astype(F32) + mixed[...]).astype(BF16)

    grad_even = matmul_t(flat(grad2[1:10]), back_down[1]).reshape(9, 64, 256)
    grad_odd = (
        matmul_t(flat(grad2[0:9]), back_down[2]) + matmul_t(flat(grad2[1:10]), back_down[0])
    ).reshape(9, 64, 256)
    for start, rows in ((0, grad_odd), (1, grad_even)):
        rows = jnp.concatenate([rows[m : m + 1] * slopes[start + 2 * m][None] for m in range(9)], axis=0)
        ready = rows.astype(BF16)
        shifted[:, 8:72] = rows[:, :, 128:256]
        before = shifted[:, 7:71].astype(BF16)
        shifted[:, 8:72] = rows[:, :, 0:128]
        after = shifted[:, 9:73].astype(BF16)
        for m in range(9):
            gx[start + 2 * m, :, 0:128] = before[m]
            gx[start + 2 * m, :, 128:384] = ready[m]
            gx[start + 2 * m, :, 384:512] = after[m]

    @pl.when(top)
    def _():
        gx[0] = jnp.zeros((64, 512), BF16)

    @pl.when(bottom)
    def _():
        gx[17] = jnp.zeros((64, 512), BF16)

    for first in (0, 8):
        back = sum(matmul_t(flat(gx[first + j : first + j + 8]), back_fine[j]) for j in range(3))
        for row in range(8):
            mix(first + row, back[64 * row : 64 * row + 64])
    input_grad[...] = (cotangent[...].astype(F32) + mixed[...]).astype(BF16)

    turned = flat(coarse2[1:9, :, 0:256]).T
    for j, (a, b) in enumerate(views):
        found = matmul(turned, flat(c3[a + 1 : a + 9, b]))
        for slot in range(3):
            wup[3 * (2 - j) + 2 - slot] = found[:, slot * 128 : slot * 128 + 128].astype(BF16)
    turned = flat(grad2[1:9, :, 0:256]).T
    for j, (a, b) in enumerate(views):
        found = matmul(turned, flat(h3[a + 1 : a + 9, b]))
        for slot in range(3):
            wdn[3 * j + slot] = found[:, slot * 128 : slot * 128 + 128].T.astype(BF16)
    turned = flat(gx[1:17, :, 128:384]).T
    for j in range(3):
        found = matmul(turned, flat(fx[3 + j : 19 + j]))
        for l in range(3):
            both = found[0:128, l * 128 : l * 128 + 128] + found[128:256, (l + 1) * 128 : (l + 2) * 128]
            win[3 * j + l] = both.T.astype(BF16)
    pack_sums(parts, win, wdn, wup)


def reduce_kernel(
    parts,
    total,
    from_core,
    to_y,
    from_y,
    sums,
    to_z,
    from_z,
    column,
    from_x,
    piece,
    from_far,
    done,
    all_pieces,
    c_send,
    c_recv,
    y_send,
    y_recv,
    z_send,
    z_recv,
    x_send,
    x_recv,
    f_send,
    f_recv,
    a_send,
    a_recv,
    b_send,
    b_recv,
):
    x, y, z, core = place()
    z_lo = lax.rem(z, 8)
    holder = lax.div(z_lo, 4) == core
    other = device(x, y, z, 1 - core)
    far = on_ring(z, 8, 16)

    def rows_of(by, half):
        return pl.ds(on_ring(y, by, 4) * 8 + half * 4, 4)

    def across(by):
        return remote(parts.at[rows_of(by, 1 - core)], from_core.at[by], c_send, c_recv, by, other)

    def along_y(by):
        return remote(to_y.at[by - 1], from_y.at[by - 1], y_send, y_recv, by - 1, device(x, on_ring(y, by, 4), z, core))

    for by in (1, 3, 2, 0):
        across(by).start()
    for by in (1, 3, 2):
        across(by).wait_recv()
        to_y[by - 1] = (
            parts[rows_of(by, core)].astype(F32) + from_core[by].astype(F32)
        ).astype(BF16)
        along_y(by).start()
    across(0).wait_recv()
    sums[...] = parts[rows_of(0, core)].astype(F32) + from_core[0].astype(F32)
    for by in (1, 3, 2):
        along_y(by).wait_recv()
        sums[...] += from_y[by - 1].astype(F32)
    to_z[...] = sums[...].astype(BF16)

    def along_z(slot, by):
        where = on_ring(z, by, 16)
        return remote(
            to_z.at[lax.rem(where, 4)], from_z.at[slot], z_send, z_recv, slot, device(x, y, where, core)
        )

    for slot, by in enumerate(HOPS):

        @pl.when(lax.div(lax.rem(on_ring(z, by, 16), 8), 4) == core)
        def _():
            along_z(slot, by).start()

    def along_x(by):
        where = on_ring(x, by, 4)
        return remote(
            column.at[pl.ds(where * PIECE_STEP, PIECE)],
            from_x.at[by - 1],
            x_send,
            x_recv,
            by - 1,
            device(where, y, z, core),
        )

    def to_far():
        return remote(piece, from_far, f_send, f_recv, 0, device(x, y, far, core))

    def spread(by):
        return remote(done, all_pieces.at[x], a_send, a_recv, by, device(on_ring(x, by, 4), y, z, core))

    def spread_other(by):
        return remote(done, all_pieces.at[x], b_send, b_recv, by, device(on_ring(x, by, 4), y, z, 1 - core))

    @pl.when(holder)
    def _():
        column[...] = sums[lax.rem(z_lo, 4)]
        for slot, by in enumerate(HOPS):
            along_z(slot, by).wait_recv()
            column[...] += from_z[slot].astype(F32)
        for by in (1, 3, 2):
            along_x(by).start()
        piece[...] = column[pl.ds(x * PIECE_STEP, PIECE)]
        for by in (1, 3, 2):
            along_x(by).wait_recv()
            piece[...] += from_x[by - 1]
        to_far().start()
        to_far().wait_recv()
        done[...] = piece[...] + from_far[...]
        for by in (2, 1, 3):
            spread(by).start()
        for by in (2, 1, 3, 0):
            spread_other(by).start()
        all_pieces[x] = done[...]
        for by in (1, 2, 3):
            spread(by).wait_recv()
        for by in (1, 2, 3):
            along_x(by).wait_send()
        to_far().wait_send()
        for by in (1, 2, 3):
            spread(by).wait_send()
        for by in range(4):
            spread_other(by).wait_send()

    @pl.when(jnp.logical_not(holder))
    def _():
        for by in range(4):
            spread_other(by).wait_recv()

    for source in range(4):
        total[pl.ds(source * PIECE_STEP, PIECE)] = all_pieces[source]
    for by in range(4):
        across(by).wait_send()
    for by in (1, 2, 3):
        along_y(by).wait_send()
    for slot, by in enumerate(HOPS):

        @pl.when(lax.div(lax.rem(on_ring(z, by, 16), 8), 4) == core)
        def _():
            along_z(slot, by).wait_send()


def whole_kernel(
    own,
    frames,
    cotangent,
    output,
    input_grad,
    total,
    full,
    frames_above,
    frames_below,
    cotangent_above,
    cotangent_below,
    parts,
    *scratch,
):
    x, y, z, core = place()
    row, band = lax.axis_index("dp"), lax.axis_index("height")
    meet(
        [device(x, y, on_ring(z, by, 16), core) for by in (1, -1, 2, -2, 3, -3, 4, -4, 8)]
        + [device(x, on_ring(y, by, 4), z, core) for by in (1, 2, 3)]
        + [device(on_ring(x, by, 4), y, z, core) for by in (1, 2, 3)]
        + [device(on_ring(x, by, 4), y, z, 1 - core) for by in (0, 1, 2, 3)]
        + [(row, on_ring(band, -1, 16)), (row, on_ring(band, 1, 16))]
    )
    halos = (frames_above, frames_below, cotangent_above, cotangent_below)
    for_gather, for_compute, for_reduce = scratch[:8], scratch[8:28], scratch[28:]
    gather_kernel(own, frames, cotangent, full, *halos, *for_gather)
    inputs = (frames, *halos[:2], cotangent, *halos[2:], full)
    compute_kernel(*inputs, output, input_grad, parts, *for_compute)
    reduce_kernel(parts, total, *for_reduce)


def whole(packed, frames, cotangent):
    vmem, dma = pltpu.VMEM, pltpu.SemaphoreType.DMA
    spec = pl.BlockSpec(memory_space=vmem)
    gather_counts = (7, 3, 4, 4)
    reduce_counts = (4, 3, 7, 3, 1, 4, 4)
    return pl.pallas_call(
        whole_kernel,
        out_shape=(
            jax.ShapeDtypeStruct((16, 128, 128), BF16),
            jax.ShapeDtypeStruct((16, 128, 128), BF16),
            jax.ShapeDtypeStruct((PACK, 128), F32),
        ),
        in_specs=[spec] * 3,
        out_specs=(spec,) * 3,
        scratch_shapes=[
            vmem((32, PACK, 128), BF16),
            vmem((4, 128, 128), BF16),
            vmem((3, 128, 128), BF16),
            vmem((3, 128, 128), BF16),
            vmem((2, 128, 128), BF16),
            vmem((32, PACK, 128), BF16),
        ]
        + [dma((count,)) for count in gather_counts for _ in range(2)]
        + [
            vmem((23, 144, 128), F32),
            vmem((23, 64, 512), BF16),
            vmem((11, 2, 64, 384), BF16),
            vmem((11, 2, 64, 384), BF16),
            vmem((18, 64, 256), F32),
            vmem((9, 80, 128), F32),
            vmem((10, 72, 256), F32),
            vmem((10, 64, 512), BF16),
            vmem((10, 64, 512), BF16),
            vmem((18, 64, 512), BF16),
            vmem((16, 128, 128), F32),
            vmem((9, 128, 128), BF16),
            vmem((9, 128, 256), BF16),
            vmem((9, 256, 128), BF16),
            vmem((3, 512, 256), BF16),
            vmem((3, 384, 256), BF16),
            vmem((3, 512, 256), BF16),
            vmem((3, 256, 512), BF16),
            vmem((3, 256, 512), BF16),
            vmem((3, 256, 384), BF16),
        ]
        + [
            vmem((4, 4, PACK, 128), BF16),
            vmem((3, 4, PACK, 128), BF16),
            vmem((3, 4, PACK, 128), BF16),
            vmem((4, PACK, 128), F32),
            vmem((4, PACK, 128), BF16),
            vmem((7, PACK, 128), BF16),
            vmem((PACK, 128), F32),
            vmem((3, PIECE, 128), F32),
            vmem((PIECE, 128), F32),
            vmem((PIECE, 128), F32),
            vmem((PIECE, 128), F32),
            vmem((4, PIECE, 128), F32),
        ]
        + [dma((count,)) for count in reduce_counts for _ in range(2)],
        compiler_params=pltpu.CompilerParams(
            collective_id=0, has_side_effects=True, vmem_limit_bytes=56 << 20
        ),
    )(packed, frames, cotangent)


def pack(w_in, w_down, w_up):
    def rows(kernel, size):
        return jnp.pad(kernel, ((0, 0), (0, size - kernel.shape[1]), (0, 0)))

    count = w_in.shape[0]
    halves = w_down.reshape(count, 36, 2, 128).transpose(0, 2, 1, 3).reshape(count, 72, 128)
    return jnp.concatenate(
        [
            rows(w_in.reshape(count, 36, 128), DOWN_AT),
            rows(halves, UP_AT - DOWN_AT),
            rows(w_up.reshape(count, 72, 128), PACK - UP_AT),
        ],
        axis=1,
    )


def unpack(packed):
    count = packed.shape[0]
    halves = packed[:, DOWN_AT : DOWN_AT + 72].reshape(count, 2, 36, 128).transpose(0, 2, 1, 3)
    return (
        packed[:, :36].reshape(count, 9, 4, 128),
        halves.reshape(count, 9, 4, 256),
        packed[:, UP_AT : UP_AT + 72].reshape(count, 9, 8, 128),
    )


def on_device(frames, cotangent, w_in, w_down, w_up):
    frames, cotangent = frames[0], cotangent[0]
    packed = pack(w_in[None], w_down[None], w_up[None])[0]
    output, input_grad, summed = whole(packed, frames, cotangent)
    height = lax.axis_size("height")
    pixel_count = lax.axis_size("dp") * height * frames.shape[0] * frames.shape[1]
    factor = 1.0 / math.sqrt(pixel_count)
    index = lax.axis_index("height")
    shares = []
    for part in unpack(summed[None] * factor):
        width = part.shape[3] // height
        share = lax.dynamic_slice_in_dim(part[0], index * width, width, axis=2)
        shares.append(share.reshape(3, 3, part.shape[2], width))
    return (output[None], input_grad[None], *shares)


def solution(mesh):
    in_specs = (
        P("dp", "height", None, None),
        P("dp", "height", None, None),
        P(None, None, "dp", None),
        P(None, None, "dp", None),
        P(None, None, "dp", None),
    )
    out_specs = (
        P("dp", "height", None, None),
        P("dp", "height", None, None),
        P(None, None, "dp", "height"),
        P(None, None, "dp", "height"),
        P(None, None, "dp", "height"),
    )
    return jax.shard_map(
        on_device, mesh=mesh, in_specs=in_specs, out_specs=out_specs, check_vma=False
    )
```

```python
import functools
import math

import jax
import jax.numpy as jnp
from jax import lax
from jax.experimental import pallas as pl
from jax.experimental.pallas import tpu as pltpu
from jax.sharding import PartitionSpec as P

F32, BF16 = jnp.float32, jnp.bfloat16
MESH = pl.DeviceIdType.MESH

PACK = 208
DOWN_AT = 48
UP_AT = 128
HOPS = (1, -1, 2, -2, 3, -3, 4)
JOBS = ((0, 48, "x"), (48, 80, "y"), (128, 80, "x"))
IN, DOWN, UP = 0, 1, 2


def place():
    d = lax.axis_index("dp")
    h = lax.axis_index("height")
    z = lax.rem(lax.div(h, 2), 2) * 8 + lax.rem(d, 8)
    return lax.div(h, 4), lax.div(d, 8), z, lax.rem(h, 2)


def device(x, y, z, core):
    return (y * 8 + lax.rem(z, 8), x * 4 + lax.div(z, 8) * 2 + core)


def on_ring(position, by, size):
    return lax.rem(position + by + size, size)


def remote(source, target, send, recv, where):
    return pltpu.make_async_remote_copy(
        src_ref=source, dst_ref=target, send_sem=send, recv_sem=recv, device_id=where, device_id_type=MESH
    )


def when(condition, action):
    @pl.when(condition)
    def _():
        action()


def every(copies, act):
    for copy in copies:
        getattr(copy, act)()


def spread_columns(rows, first, wide, stacked, slots):
    count = rows.shape[0]
    wide[pl.ds(first, count), 8:136] = rows[...].astype(F32)
    for row in range(first, first + count):
        target = stacked.at[row] if len(stacked.shape) == 3 else stacked.at[row // 2, row % 2]
        for slot in range(slots):
            target[:, slot * 128 : slot * 128 + 128] = wide[row, pl.ds(7 + slot, 64, stride=2), :].astype(BF16)


def matmul(left, right):
    return lax.dot_general(left, right, (((1,), (0,)), ((), ())), preferred_element_type=F32)


def matmul_t(left, right):
    return lax.dot_general(left, right, (((1,), (1,)), ((), ())), preferred_element_type=F32)


def flat(cells):
    return cells.reshape(cells.shape[0] * cells.shape[1], cells.shape[2])


def shuffle(taps, channels, pitch, transposed):
    shards = 16 // channels
    dims = (shards * pitch, taps * 16) if transposed else (taps * 16, shards * pitch)
    row = lax.broadcasted_iota(jnp.int32, dims, 1 if transposed else 0)
    column = lax.broadcasted_iota(jnp.int32, dims, 0 if transposed else 1)
    bits = channels.bit_length() - 1
    wanted = ((row & 15) >> bits) * pitch + (row >> 4) * channels + (row & (channels - 1))
    return (column == wanted).astype(F32).astype(BF16)


def unpack_in(full, win):
    order = shuffle(9, 4, 48, False)
    for group in range(8):
        k, y = 4 * (group % 2), group // 2
        rows = matmul(order, full[k : k + 4, y, 0:DOWN_AT].reshape(192, 128)).astype(BF16)
        win[:, 16 * group : 16 * group + 16] = rows.reshape(9, 16, 128)


def unpack_down(full, wdn):
    order = shuffle(18, 4, 80, False)
    for group in range(8):
        k, y = 4 * (group % 2), group // 2
        rows = matmul(order, full[k : k + 4, y, DOWN_AT:UP_AT].reshape(320, 128)).astype(BF16)
        wdn[:, 16 * group : 16 * group + 16, 0:128] = rows[0:144].reshape(9, 16, 128)
        wdn[:, 16 * group : 16 * group + 16, 128:256] = rows[144:288].reshape(9, 16, 128)


def unpack_up(full, wup):
    order = shuffle(9, 8, 80, False)
    for group in range(16):
        k, y = 2 * (group % 4), group // 4
        rows = matmul(order, full[k : k + 2, y, UP_AT:PACK].reshape(160, 128)).astype(BF16)
        wup[:, 16 * group : 16 * group + 16] = rows.reshape(9, 16, 128)


def pack_in(parts, sin):
    order = shuffle(9, 4, 48, True)
    for group in range(8):
        k, y = 4 * (group % 2), group // 2
        rows = matmul(order, sin[:, 16 * group : 16 * group + 16].reshape(144, 128)).astype(BF16)
        parts[k : k + 4, y, 0:DOWN_AT] = rows.reshape(4, 48, 128)


def pack_down(parts, sdn):
    order = shuffle(18, 4, 80, True)
    for group in range(8):
        k, y = 4 * (group % 2), group // 2
        halves = [sdn[:, 16 * group : 16 * group + 16, at : at + 128].reshape(144, 128) for at in (0, 128)]
        rows = matmul(order, jnp.concatenate(halves, axis=0)).astype(BF16)
        parts[k : k + 4, y, DOWN_AT:UP_AT] = rows.reshape(4, 80, 128)


def pack_up(parts, sup):
    order = shuffle(9, 8, 80, True)
    for group in range(16):
        k, y = 2 * (group % 4), group // 4
        rows = matmul(order, sup[:, 16 * group : 16 * group + 16].reshape(144, 128)).astype(BF16)
        parts[k : k + 2, y, UP_AT:PACK] = rows.reshape(2, 80, 128)


def stack_in(win, fine, back_fine):
    blank = jnp.zeros((128, 128), BF16)
    for j in range(3):
        for slot in range(4):
            at = slice(slot * 128, slot * 128 + 128)
            fine[j, at, 0:128] = win[3 * j + slot] if slot < 3 else blank
            fine[j, at, 128:256] = win[3 * j + slot - 1] if slot > 0 else blank
            back_fine[j, 0:128, at] = win[3 * (2 - j) + 2 - slot] if slot < 3 else blank
            back_fine[j, 128:256, at] = win[3 * (2 - j) + 3 - slot] if slot > 0 else blank


def stack_down(wdn, down, back_down):
    for j in range(3):
        for slot in range(3):
            down[j, slot * 128 : slot * 128 + 128, :] = wdn[3 * j + slot]
        back_down[j, 0:128, 0:256] = wdn[3 * j + 1]
        back_down[j, 0:128, 256:512] = jnp.zeros((128, 256), BF16)
        back_down[j, 128:256, 0:256] = wdn[3 * j + 2]
        back_down[j, 128:256, 256:512] = wdn[3 * j]


def stack_up(wup, up, back_up):
    for j in range(3):
        for slot in range(3):
            back_up[j, :, slot * 128 : slot * 128 + 128] = wup[3 * (2 - j) + 2 - slot]
        up[j, 0:256, 0:128] = wup[3 * j + 1]
        up[j, 0:256, 128:256] = wup[3 * j]
        up[j, 256:512, 0:128] = jnp.zeros((256, 128), BF16)
        up[j, 256:512, 128:256] = wup[3 * j + 2]


def sigmoid(value):
    return 1.0 / (1.0 + jnp.exp(-value))


def pack_own(w_in, w_down, w_up, wide, own):
    wide[...] = jnp.zeros_like(wide)
    for tap in range(9):
        j, l = tap // 3, tap % 3
        wide[4 * tap : 4 * tap + 4] = w_in[j, l].astype(F32)
        for half in range(2):
            at = DOWN_AT + 36 * half + 4 * tap
            wide[at : at + 4] = w_down[j, l, :, 128 * half : 128 * half + 128].astype(F32)
        wide[UP_AT + 8 * tap : UP_AT + 8 * tap + 8] = w_up[j, l].astype(F32)
    own[...] = wide[...].astype(BF16)


def columns(rows, first, width):
    lane = lax.broadcasted_iota(jnp.int32, (128, width), 0)
    wanted = lax.broadcasted_iota(jnp.int32, (128, width), 1) + first
    return lax.dot_general(
        rows, (lane == wanted).astype(F32), (((1,), (0,)), ((), ())),
        precision=lax.Precision.HIGHEST, preferred_element_type=F32,
    )


def take_share(total, band, grad_in, grad_down, grad_up):
    into = columns(total[0:40], band * 8, 8)
    down = columns(total[DOWN_AT : DOWN_AT + 72], lax.rem(band, 8) * 16, 16)
    up = columns(total[UP_AT : UP_AT + 72], band * 8, 8)
    down = jnp.where(band < 8, down[0:36], down[36:72])
    for tap in range(9):
        j, l = tap // 3, tap % 3
        grad_in[j, l] = into[4 * tap : 4 * tap + 4]
        grad_down[j, l] = down[4 * tap : 4 * tap + 4]
        grad_up[j, l] = up[8 * tap : 8 * tap + 8]


class Gather:
    def __init__(self, job, own, full, sems):
        first, count, self.main = JOBS[job]
        self.rows = pl.ds(first, count)
        self.own, self.full = own, full
        self.sems = [sem.at[job] for sem in sems]
        self.x, self.y, self.z, self.core = place()
        self.carried = self.x + 4 * self.core
        self.holder = lax.rem(self.z, 8) == self.carried

    def beside(self, axis, by):
        if axis == "x":
            return device(on_ring(self.x, by, 4), self.y, self.z, self.core)
        return device(self.x, on_ring(self.y, by, 4), self.z, self.core)

    def along_z(self, count=7):
        send, recv = self.sems[0], self.sems[1]
        target = self.full.at[self.carried, self.y, self.rows]
        return [
            remote(
                self.own.at[self.rows], target, send.at[slot], recv.at[0],
                device(self.x, self.y, on_ring(self.z, by, 16), self.core),
            )
            for slot, by in enumerate(HOPS[:count])
        ]

    def light(self):
        send, recv = self.sems[2], self.sems[3]
        axis = "y" if self.main == "x" else "x"
        block = self.full.at[self.carried, self.y, self.rows]
        return [remote(block, block, send.at[by], recv.at[by], self.beside(axis, by)) for by in (1, 3, 2)]

    def piece(self, by, core):
        if self.main == "x":
            return self.full.at[on_ring(self.x, -by, 4) + 4 * core, :, self.rows]
        return self.full.at[pl.ds(4 * core, 4), on_ring(self.y, -by, 4), self.rows]

    def heavy(self, by):
        send, recv = self.sems[4], self.sems[5]
        block = self.piece(0, self.core)
        return remote(block, block, send.at[by], recv.at[by], self.beside(self.main, by))

    def across(self, by):
        send, recv = self.sems[6], self.sems[7]
        block = self.piece(by, self.core)
        other = device(self.x, self.y, self.z, 1 - self.core)
        return remote(block, block, send.at[by], recv.at[by], other)

    def step(self, stage):
        if stage == 0:

            @pl.when(self.holder)
            def _():
                every(self.along_z(), "start")
                self.full[self.carried, self.y, self.rows] = self.own[self.rows]

        if stage == 1:
            when(jnp.logical_not(self.holder), lambda: every(self.along_z(1), "wait_recv"))
            every(self.light(), "start")
        if stage == 2:
            every(self.light(), "wait_recv")
            for by in (1, 3, 2):
                self.heavy(by).start()
            self.across(0).start()
        if stage == 3:
            for by in (1, 3, 2):
                self.heavy(by).wait_recv()
                self.across(by).start()
        if stage == 4:
            for by in range(4):
                self.across(by).wait_recv()
        if stage == 5:
            when(self.holder, lambda: every(self.along_z(), "wait_send"))
            every(self.light(), "wait_send")
            for by in (1, 2, 3):
                self.heavy(by).wait_send()
            for by in range(4):
                self.across(by).wait_send()


class Reduce:
    def __init__(self, job, parts, buffers, sems, scale):
        first, count, self.main = JOBS[job]
        self.rows = pl.ds(first, count)
        self.parts = parts
        (
            self.from_core, self.heavy_out, self.heavy_in, self.sums, self.light_out, self.light_in,
            self.column, self.z_out, self.z_in, self.done, self.total,
        ) = buffers
        self.sems = [sem.at[job] for sem in sems]
        self.scale = scale
        self.x, self.y, self.z, self.core = place()
        self.carried = self.x + 4 * self.core
        self.holder = lax.rem(self.z, 8) == self.carried

    beside = Gather.beside

    def block(self, ref, by, core):
        if self.main == "x":
            return ref.at[on_ring(self.x, by, 4) + 4 * core, :, self.rows]
        return ref.at[pl.ds(4 * core, 4), on_ring(self.y, by, 4), self.rows]

    def across(self, by):
        other = device(self.x, self.y, self.z, 1 - self.core)
        return remote(
            self.block(self.parts, by, 1 - self.core), self.block(self.from_core, by, 0),
            self.sems[0].at[by], self.sems[1].at[by], other,
        )

    def heavy(self, by):
        return remote(
            self.heavy_out.at[by - 1, :, self.rows], self.heavy_in.at[by - 1, :, self.rows],
            self.sems[2].at[by], self.sems[3].at[by], self.beside(self.main, by),
        )

    def light(self, by):
        axis = "y" if self.main == "x" else "x"
        return remote(
            self.light_out.at[by - 1, self.rows], self.light_in.at[by - 1, self.rows],
            self.sems[4].at[by], self.sems[5].at[by], self.beside(axis, by),
        )

    def to_holder(self, at):
        where = self.carried + at
        slot = lax.rem(self.z - where + 31, 16)
        return remote(
            self.z_out.at[self.rows], self.z_in.at[slot, self.rows],
            self.sems[6].at[at // 8], self.sems[7].at[slot], device(self.x, self.y, where, self.core),
        )

    def from_ring(self, slot):
        return remote(
            self.z_out.at[self.rows], self.z_in.at[slot, self.rows],
            self.sems[6].at[0], self.sems[7].at[slot], device(self.x, self.y, self.z, 1 - self.core),
        )

    def spread(self, count=7):
        return [
            remote(
                self.done.at[self.rows], self.total.at[self.rows],
                self.sems[8].at[2 * by + swap], self.sems[9].at[0],
                device(on_ring(self.x, by, 4), self.y, self.z, lax.rem(self.core + swap, 2)),
            )
            for by, swap in ((2, 0), (2, 1), (1, 0), (3, 0), (1, 1), (3, 1), (0, 1))[:count]
        ]

    def both(self, by):
        own = self.block(self.parts, by, self.core)[...].astype(F32)
        return own + self.block(self.from_core, by, 0)[...].astype(F32)

    def step(self, stage):
        rows = self.rows
        if stage == 0:
            for by in (1, 3, 2, 0):
                self.across(by).start()
        if stage == 1:
            for by in (1, 3, 2):
                self.across(by).wait_recv()
                self.heavy_out[by - 1, :, rows] = self.both(by).astype(BF16)
                self.heavy(by).start()
            self.across(0).wait_recv()
            self.sums[:, rows] = self.both(0)
        if stage == 2:
            total = self.sums[:, rows]
            for by in (1, 3, 2):
                self.heavy(by).wait_recv()
                total += self.heavy_in[by - 1, :, rows].astype(F32)
            self.sums[:, rows] = total
            here = self.y if self.main == "x" else self.x
            for by in (1, 3, 2):
                self.light_out[by - 1, rows] = self.sums[on_ring(here, by, 4), rows].astype(BF16)
                self.light(by).start()
            self.column[rows] = self.sums[here, rows]
        if stage == 3:
            total = self.column[rows]
            for by in (1, 3, 2):
                self.light(by).wait_recv()
                total += self.light_in[by - 1, rows].astype(F32)
            self.column[rows] = total
            self.z_out[rows] = total.astype(BF16)
            for at in (0, 8):
                when(self.z != self.carried + at, self.to_holder(at).start)
        if stage == 4:

            @pl.when(self.holder)
            def _():
                total = self.column[rows]
                for slot in range(15):
                    self.from_ring(slot).wait_recv()
                    total += self.z_in[slot, rows].astype(F32)
                total = total * self.scale
                self.done[rows] = total
                every(self.spread(), "start")
                self.total[rows] = total

        if stage == 5:
            when(jnp.logical_not(self.holder), lambda: every(self.spread(1), "wait_recv"))
        if stage == 6:
            for by in range(4):
                self.across(by).wait_send()
            for by in (1, 2, 3):
                self.heavy(by).wait_send()
                self.light(by).wait_send()
            for at in (0, 8):
                when(self.z != self.carried + at, self.to_holder(at).wait_send)
            when(self.holder, lambda: every(self.spread(), "wait_send"))


def greet():
    x, y, z, core = place()
    carried = x + 4 * core
    holder = lax.rem(z, 8) == carried
    row, band = lax.axis_index("dp"), lax.axis_index("height")
    barrier = pltpu.get_barrier_semaphore()

    def signal(where):
        pl.semaphore_signal(barrier, inc=1, device_id=where, device_id_type=MESH)

    signal((row, on_ring(band, -1, 16)))
    signal((row, on_ring(band, 1, 16)))
    for by in (1, 2, 3):
        signal(device(x, on_ring(y, by, 4), z, core))
        signal(device(on_ring(x, by, 4), y, z, core))
    for by in range(4):
        signal(device(on_ring(x, by, 4), y, z, 1 - core))

    @pl.when(holder)
    def _():
        for by in range(1, 16):
            signal(device(x, y, on_ring(z, by, 16), core))

    @pl.when(jnp.logical_not(holder))
    def _():
        signal(device(x, y, carried, core))
        signal(device(x, y, carried + 8, core))

    return lambda: pl.semaphore_wait(barrier, jnp.where(holder, 12 + 15, 12 + 2))


def whole_kernel(
    scale,
    frames_far,
    cotangent_far,
    w_in,
    w_down,
    w_up,
    output,
    input_grad,
    grad_in,
    grad_down,
    grad_up,
    own,
    own_wide,
    frames,
    cotangent,
    frames_above,
    frames_below,
    cotangent_above,
    cotangent_below,
    full,
    parts,
    wide,
    fx,
    h3,
    c3,
    slopes,
    shifted,
    shifted_wide,
    coarse2,
    grad2,
    gx,
    mixed,
    win,
    wdn,
    wup,
    fine,
    down,
    up,
    back_fine,
    back_down,
    back_up,
    *rest,
):
    buffers, rest = rest[:11], rest[11:]
    gather_sems, reduce_sems, (halo_send, halo_recv, load_sem) = rest[:8], rest[8:18], rest[18:]
    band = lax.axis_index("height")
    top, bottom = band == 0, band == lax.axis_size("height") - 1
    under_top, over_bottom = jnp.logical_not(top), jnp.logical_not(bottom)

    loads = [
        pltpu.make_async_copy(frames_far, frames, load_sem.at[0]),
        pltpu.make_async_copy(cotangent_far, cotangent, load_sem.at[1]),
    ]
    every(loads, "start")
    gathers = [Gather(job, own, full, gather_sems) for job in range(3)]
    reduces = [Reduce(job, parts, buffers, reduce_sems, scale) for job in range(3)]

    row = lax.axis_index("dp")
    over, under = (row, on_ring(band, -1, 16)), (row, on_ring(band, 1, 16))

    def halo(slot, source, first, target, where):
        cells = source.at[pl.ds(first, target.shape[0])]
        return remote(cells, target, halo_send.at[slot], halo_recv.at[slot], where)

    downward = [
        halo(0, frames_far, 12, frames_above, under),
        halo(1, cotangent_far, 13, cotangent_above, under),
    ]
    upward = [
        halo(2, frames_far, 0, frames_below, over),
        halo(3, cotangent_far, 0, cotangent_below, over),
    ]

    all_there = greet()
    pack_own(w_in, w_down, w_up, own_wide, own)
    wide[:, 0:8] = jnp.zeros((23, 8, 128), F32)
    wide[:, 136:144] = jnp.zeros((23, 8, 128), F32)
    shifted[:, 0:8] = jnp.zeros((9, 8, 128), F32)
    shifted[:, 72:80] = jnp.zeros((9, 8, 128), F32)
    shifted_wide[:, 64:72] = jnp.zeros((10, 8, 256), F32)
    all_there()
    for job in range(3):
        gathers[job].step(0)

    @pl.when(top)
    def _():
        frames_above[...] = jnp.zeros_like(frames_above)
        cotangent_above[...] = jnp.zeros_like(cotangent_above)

    @pl.when(bottom)
    def _():
        frames_below[...] = jnp.zeros_like(frames_below)
        cotangent_below[...] = jnp.zeros_like(cotangent_below)

    every(loads, "wait")
    gathers[IN].step(1)
    gathers[DOWN].step(1)
    gathers[UP].step(1)
    when(over_bottom, lambda: every(downward, "start"))
    when(under_top, lambda: every(upward, "start"))
    spread_columns(frames, 4, wide, fx, 4)
    gathers[IN].step(2)
    gathers[DOWN].step(2)
    spread_columns(cotangent, 3, wide, c3, 3)
    gathers[IN].step(3)
    gathers[UP].step(2)
    gathers[DOWN].step(3)
    gathers[IN].step(4)
    unpack_in(full, win)
    stack_in(win, fine, back_fine)
    gathers[UP].step(3)
    gathers[DOWN].step(4)
    unpack_down(full, wdn)
    stack_down(wdn, down, back_down)
    gathers[UP].step(4)
    unpack_up(full, wup)
    stack_up(wup, up, back_up)

    when(under_top, lambda: every(downward, "wait_recv"))
    when(over_bottom, lambda: every(upward, "wait_recv"))
    spread_columns(frames_above, 0, wide, fx, 4)
    spread_columns(frames_below, 20, wide, fx, 4)
    spread_columns(cotangent_above, 0, wide, c3, 3)
    spread_columns(cotangent_below, 19, wide, c3, 3)

    for first in (0, 7, 14):
        pre = sum(matmul(flat(fx[first + j : first + j + 7]), fine[j]) for j in range(3))
        gate = sigmoid(pre)
        hidden = (pre * gate).reshape(7, 64, 256)
        slope = (gate * (1.0 + pre * (1.0 - gate))).reshape(7, 64, 256)
        shifted[0:7, 8:72] = hidden[:, :, 128:256]
        before = shifted[0:7, 7:71].astype(BF16)
        hidden = hidden.astype(BF16)
        for row in range(7):
            i = first + row
            h3[i // 2, i % 2, :, 0:128] = before[row]
            h3[i // 2, i % 2, :, 128:384] = hidden[row]
            if 2 <= i < 20:
                slopes[i - 2] = slope[row]

    @pl.when(top)
    def _():
        for i in range(3):
            h3[i // 2, i % 2] = jnp.zeros((64, 384), BF16)

    @pl.when(bottom)
    def _():
        for i in (19, 20):
            h3[i // 2, i % 2] = jnp.zeros((64, 384), BF16)

    views = ((0, 0), (0, 1), (1, 0))
    pre = sum(matmul(flat(h3[a : a + 10, b]), down[j]) for j, (a, b) in enumerate(views))
    gate = sigmoid(pre)
    coarse = (pre * gate).reshape(10, 64, 256)
    shifted_wide[:, 0:64] = coarse
    coarse2[:, :, 0:256] = coarse.astype(BF16)
    coarse2[:, :, 256:512] = shifted_wide[:, 1:65].astype(BF16)
    back = sum(matmul_t(flat(c3[a : a + 10, b]), back_up[j]) for j, (a, b) in enumerate(views))
    grad = (back * (gate * (1.0 + pre * (1.0 - gate)))).reshape(10, 64, 256)
    shifted_wide[:, 0:64] = grad
    grad2[:, :, 0:256] = grad.astype(BF16)
    grad2[:, :, 256:512] = shifted_wide[:, 1:65].astype(BF16)

    @pl.when(top)
    def _():
        grad2[0] = jnp.zeros((64, 512), BF16)

    @pl.when(bottom)
    def _():
        coarse2[9] = jnp.zeros((64, 512), BF16)
        grad2[9] = jnp.zeros((64, 512), BF16)

    turned = flat(coarse2[1:9, :, 0:256]).T
    for j, (a, b) in enumerate(views):
        found = matmul(turned, flat(c3[a + 1 : a + 9, b]))
        for slot in range(3):
            wup[3 * (2 - j) + 2 - slot] = found[:, slot * 128 : slot * 128 + 128].astype(BF16)
    pack_up(parts, wup)
    reduces[UP].step(0)
    turned = flat(grad2[1:9, :, 0:256]).T
    for j, (a, b) in enumerate(views):
        found = matmul(turned, flat(h3[a + 1 : a + 9, b]))
        for slot in range(3):
            wdn[3 * j + slot] = found[:, slot * 128 : slot * 128 + 128].T.astype(BF16)
    pack_down(parts, wdn)
    reduces[DOWN].step(0)
    reduces[UP].step(1)

    grad_even = matmul_t(flat(grad2[1:10]), back_down[1]).reshape(9, 64, 256)
    grad_odd = (
        matmul_t(flat(grad2[0:9]), back_down[2]) + matmul_t(flat(grad2[1:10]), back_down[0])
    ).reshape(9, 64, 256)
    for start, rows in ((0, grad_odd), (1, grad_even)):
        rows = jnp.concatenate([rows[m : m + 1] * slopes[start + 2 * m][None] for m in range(9)], axis=0)
        ready = rows.astype(BF16)
        shifted[:, 8:72] = rows[:, :, 128:256]
        before = shifted[:, 7:71].astype(BF16)
        shifted[:, 8:72] = rows[:, :, 0:128]
        after = shifted[:, 9:73].astype(BF16)
        for m in range(9):
            gx[start + 2 * m, :, 0:128] = before[m]
            gx[start + 2 * m, :, 128:384] = ready[m]
            gx[start + 2 * m, :, 384:512] = after[m]

    @pl.when(top)
    def _():
        gx[0] = jnp.zeros((64, 512), BF16)

    @pl.when(bottom)
    def _():
        gx[17] = jnp.zeros((64, 512), BF16)

    reduces[DOWN].step(1)
    turned = flat(gx[1:17, :, 128:384]).T
    for j in range(3):
        found = matmul(turned, flat(fx[3 + j : 19 + j]))
        for l in range(3):
            both = found[0:128, l * 128 : l * 128 + 128] + found[128:256, (l + 1) * 128 : (l + 2) * 128]
            win[3 * j + l] = both.T.astype(BF16)
    pack_in(parts, win)
    reduces[IN].step(0)
    reduces[UP].step(2)
    reduces[IN].step(1)

    def mix(row, cells):
        mixed[row, pl.ds(0, 64, stride=2), :] = cells[:, 0:128]
        mixed[row, pl.ds(1, 64, stride=2), :] = cells[:, 128:256]

    even = matmul(flat(coarse2[1:9]), up[1])
    odd = matmul(flat(coarse2[1:9]), up[0]) + matmul(flat(coarse2[2:10]), up[2])
    for t in range(8):
        mix(2 * t, even[64 * t : 64 * t + 64])
        mix(2 * t + 1, odd[64 * t : 64 * t + 64])
    output[...] = (frames[...].astype(F32) + mixed[...]).astype(BF16)
    reduces[DOWN].step(2)
    reduces[UP].step(3)
    reduces[IN].step(2)

    for first in (0, 8):
        back = sum(matmul_t(flat(gx[first + j : first + j + 8]), back_fine[j]) for j in range(3))
        for row in range(8):
            mix(first + row, back[64 * row : 64 * row + 64])
    input_grad[...] = (cotangent[...].astype(F32) + mixed[...]).astype(BF16)
    reduces[DOWN].step(3)
    reduces[IN].step(3)
    for job in (UP, DOWN, IN):
        reduces[job].step(4)
    for job in (UP, DOWN, IN):
        reduces[job].step(5)

    take_share(buffers[10], band, grad_in, grad_down, grad_up)
    for job in range(3):
        gathers[job].step(5)
        reduces[job].step(6)
    when(over_bottom, lambda: every(downward, "wait_send"))
    when(under_top, lambda: every(upward, "wait_send"))


def whole(frames, cotangent, w_in, w_down, w_up, scale):
    vmem, dma = pltpu.VMEM, pltpu.SemaphoreType.DMA
    spec, far = pl.BlockSpec(memory_space=vmem), pl.BlockSpec(memory_space=pl.ANY)
    gather_counts = (7, 1, 4, 4, 4, 4, 4, 4)
    reduce_counts = (4, 4, 4, 4, 4, 4, 2, 15, 8, 1)
    return pl.pallas_call(
        functools.partial(whole_kernel, scale),
        out_shape=(
            jax.ShapeDtypeStruct((16, 128, 128), BF16),
            jax.ShapeDtypeStruct((16, 128, 128), BF16),
            jax.ShapeDtypeStruct((3, 3, 4, 8), F32),
            jax.ShapeDtypeStruct((3, 3, 4, 16), F32),
            jax.ShapeDtypeStruct((3, 3, 8, 8), F32),
        ),
        in_specs=[far, far, spec, spec, spec],
        out_specs=(spec,) * 5,
        scratch_shapes=[
            vmem((PACK, 128), BF16),
            vmem((PACK, 128), F32),
            vmem((16, 128, 128), BF16),
            vmem((16, 128, 128), BF16),
            vmem((4, 128, 128), BF16),
            vmem((3, 128, 128), BF16),
            vmem((3, 128, 128), BF16),
            vmem((2, 128, 128), BF16),
            vmem((8, 4, PACK, 128), BF16),
            vmem((8, 4, PACK, 128), BF16),
            vmem((23, 144, 128), F32),
            vmem((23, 64, 512), BF16),
            vmem((11, 2, 64, 384), BF16),
            vmem((11, 2, 64, 384), BF16),
            vmem((18, 64, 256), F32),
            vmem((9, 80, 128), F32),
            vmem((10, 72, 256), F32),
            vmem((10, 64, 512), BF16),
            vmem((10, 64, 512), BF16),
            vmem((18, 64, 512), BF16),
            vmem((16, 128, 128), F32),
            vmem((9, 128, 128), BF16),
            vmem((9, 128, 256), BF16),
            vmem((9, 256, 128), BF16),
            vmem((3, 512, 256), BF16),
            vmem((3, 384, 256), BF16),
            vmem((3, 512, 256), BF16),
            vmem((3, 256, 512), BF16),
            vmem((3, 256, 512), BF16),
            vmem((3, 256, 384), BF16),
            vmem((4, 4, PACK, 128), BF16),
            vmem((3, 4, PACK, 128), BF16),
            vmem((3, 4, PACK, 128), BF16),
            vmem((4, PACK, 128), F32),
            vmem((3, PACK, 128), BF16),
            vmem((3, PACK, 128), BF16),
            vmem((PACK, 128), F32),
            vmem((PACK, 128), BF16),
            vmem((15, PACK, 128), BF16),
            vmem((PACK, 128), F32),
            vmem((PACK, 128), F32),
        ]
        + [dma((3, count)) for count in gather_counts + reduce_counts]
        + [dma((4,)), dma((4,)), dma((2,))],
        compiler_params=pltpu.CompilerParams(
            collective_id=0, has_side_effects=True, vmem_limit_bytes=56 << 20
        ),
    )(frames, cotangent, w_in, w_down, w_up)


def on_device(frames, cotangent, w_in, w_down, w_up):
    frames, cotangent = frames[0], cotangent[0]
    pixel_count = lax.axis_size("dp") * lax.axis_size("height") * frames.shape[0] * frames.shape[1]
    output, input_grad, *grads = whole(frames, cotangent, w_in, w_down, w_up, 1.0 / math.sqrt(pixel_count))
    return (output[None], input_grad[None], *grads)


def solution(mesh):
    in_specs = (
        P("dp", "height", None, None),
        P("dp", "height", None, None),
        P(None, None, "dp", None),
        P(None, None, "dp", None),
        P(None, None, "dp", None),
    )
    out_specs = (
        P("dp", "height", None, None),
        P("dp", "height", None, None),
        P(None, None, "dp", "height"),
        P(None, None, "dp", "height"),
        P(None, None, "dp", "height"),
    )
    return jax.shard_map(
        on_device, mesh=mesh, in_specs=in_specs, out_specs=out_specs, check_vma=False
    )
```

```python
import functools
import math

import jax
import jax.numpy as jnp
from jax import lax
from jax.experimental import pallas as pl
from jax.experimental.pallas import tpu as pltpu
from jax.sharding import PartitionSpec as P

F32, BF16 = jnp.float32, jnp.bfloat16
MESH = pl.DeviceIdType.MESH

PACK = 208
DOWN_AT = 48
UP_AT = 128
HOPS = (1, -1, 2, -2, 3, -3, 4)
JOBS = ((0, 48, "x"), (48, 80, "y"), (128, 80, "x"))
IN, DOWN, UP = 0, 1, 2


def place():
    d = lax.axis_index("dp")
    h = lax.axis_index("height")
    z = lax.rem(lax.div(h, 2), 2) * 8 + lax.rem(d, 8)
    return lax.div(h, 4), lax.div(d, 8), z, lax.rem(h, 2)


def device(x, y, z, core):
    return (y * 8 + lax.rem(z, 8), x * 4 + lax.div(z, 8) * 2 + core)


def on_ring(position, by, size):
    return lax.rem(position + by + size, size)


def remote(source, target, send, recv, where):
    return pltpu.make_async_remote_copy(
        src_ref=source, dst_ref=target, send_sem=send, recv_sem=recv, device_id=where, device_id_type=MESH
    )


def when(condition, action):
    @pl.when(condition)
    def _():
        action()


def every(copies, act):
    for copy in copies:
        getattr(copy, act)()


def spread_columns(rows, first, wide, stacked, slots):
    count = rows.shape[0]
    wide[pl.ds(first, count), 8:136] = rows[...].astype(F32)
    for row in range(first, first + count):
        target = stacked.at[row] if len(stacked.shape) == 3 else stacked.at[row // 2, row % 2]
        for slot in range(slots):
            target[:, slot * 128 : slot * 128 + 128] = wide[row, pl.ds(7 + slot, 64, stride=2), :].astype(BF16)


def matmul(left, right):
    return lax.dot_general(left, right, (((1,), (0,)), ((), ())), preferred_element_type=F32)


def matmul_t(left, right):
    return lax.dot_general(left, right, (((1,), (1,)), ((), ())), preferred_element_type=F32)


def flat(cells):
    return cells.reshape(cells.shape[0] * cells.shape[1], cells.shape[2])


def shuffle(taps, channels, pitch, transposed):
    shards = 16 // channels
    dims = (shards * pitch, taps * 16) if transposed else (taps * 16, shards * pitch)
    row = lax.broadcasted_iota(jnp.int32, dims, 1 if transposed else 0)
    column = lax.broadcasted_iota(jnp.int32, dims, 0 if transposed else 1)
    bits = channels.bit_length() - 1
    wanted = ((row & 15) >> bits) * pitch + (row >> 4) * channels + (row & (channels - 1))
    return (column == wanted).astype(F32).astype(BF16)


def unpack_in(full, win):
    order = shuffle(9, 4, 48, False)
    for group in range(8):
        k, y = 4 * (group % 2), group // 2
        rows = matmul(order, full[k : k + 4, y, 0:DOWN_AT].reshape(192, 128)).astype(BF16)
        win[:, 16 * group : 16 * group + 16] = rows.reshape(9, 16, 128)


def unpack_down(full, wdn):
    order = shuffle(18, 4, 80, False)
    for group in range(8):
        k, y = 4 * (group % 2), group // 2
        rows = matmul(order, full[k : k + 4, y, DOWN_AT:UP_AT].reshape(320, 128)).astype(BF16)
        wdn[:, 16 * group : 16 * group + 16, 0:128] = rows[0:144].reshape(9, 16, 128)
        wdn[:, 16 * group : 16 * group + 16, 128:256] = rows[144:288].reshape(9, 16, 128)


def unpack_up(full, wup):
    order = shuffle(9, 8, 80, False)
    for group in range(16):
        k, y = 2 * (group % 4), group // 4
        rows = matmul(order, full[k : k + 2, y, UP_AT:PACK].reshape(160, 128)).astype(BF16)
        wup[:, 16 * group : 16 * group + 16] = rows.reshape(9, 16, 128)


def pack_in(parts, sin):
    order = shuffle(9, 4, 48, True)
    for group in range(8):
        k, y = 4 * (group % 2), group // 2
        rows = matmul(order, sin[:, 16 * group : 16 * group + 16].reshape(144, 128)).astype(BF16)
        parts[k : k + 4, y, 0:DOWN_AT] = rows.reshape(4, 48, 128)


def pack_down(parts, sdn):
    order = shuffle(18, 4, 80, True)
    for group in range(8):
        k, y = 4 * (group % 2), group // 2
        halves = [sdn[:, 16 * group : 16 * group + 16, at : at + 128].reshape(144, 128) for at in (0, 128)]
        rows = matmul(order, jnp.concatenate(halves, axis=0)).astype(BF16)
        parts[k : k + 4, y, DOWN_AT:UP_AT] = rows.reshape(4, 80, 128)


def pack_up(parts, sup):
    order = shuffle(9, 8, 80, True)
    for group in range(16):
        k, y = 2 * (group % 4), group // 4
        rows = matmul(order, sup[:, 16 * group : 16 * group + 16].reshape(144, 128)).astype(BF16)
        parts[k : k + 2, y, UP_AT:PACK] = rows.reshape(2, 80, 128)


def stack_in(win, fine, back_fine):
    blank = jnp.zeros((128, 128), BF16)
    for j in range(3):
        for slot in range(4):
            at = slice(slot * 128, slot * 128 + 128)
            fine[j, at, 0:128] = win[3 * j + slot] if slot < 3 else blank
            fine[j, at, 128:256] = win[3 * j + slot - 1] if slot > 0 else blank
            back_fine[j, 0:128, at] = win[3 * (2 - j) + 2 - slot] if slot < 3 else blank
            back_fine[j, 128:256, at] = win[3 * (2 - j) + 3 - slot] if slot > 0 else blank


def stack_down(wdn, down, back_down):
    for j in range(3):
        for slot in range(3):
            down[j, slot * 128 : slot * 128 + 128, :] = wdn[3 * j + slot]
        back_down[j, 0:128, 0:256] = wdn[3 * j + 1]
        back_down[j, 0:128, 256:512] = jnp.zeros((128, 256), BF16)
        back_down[j, 128:256, 0:256] = wdn[3 * j + 2]
        back_down[j, 128:256, 256:512] = wdn[3 * j]


def stack_up(wup, up, back_up):
    for j in range(3):
        for slot in range(3):
            back_up[j, :, slot * 128 : slot * 128 + 128] = wup[3 * (2 - j) + 2 - slot]
        up[j, 0:256, 0:128] = wup[3 * j + 1]
        up[j, 0:256, 128:256] = wup[3 * j]
        up[j, 256:512, 0:128] = jnp.zeros((256, 128), BF16)
        up[j, 256:512, 128:256] = wup[3 * j + 2]


def sigmoid(value):
    return 1.0 / (1.0 + jnp.exp(-value))


def pack_own(w_in, w_down, w_up, wide, own):
    wide[...] = jnp.zeros_like(wide)
    for tap in range(9):
        j, l = tap // 3, tap % 3
        wide[4 * tap : 4 * tap + 4] = w_in[j, l].astype(F32)
        for half in range(2):
            at = DOWN_AT + 36 * half + 4 * tap
            wide[at : at + 4] = w_down[j, l, :, 128 * half : 128 * half + 128].astype(F32)
        wide[UP_AT + 8 * tap : UP_AT + 8 * tap + 8] = w_up[j, l].astype(F32)
    own[...] = wide[...].astype(BF16)


def columns(rows, first, width):
    lane = lax.broadcasted_iota(jnp.int32, (128, width), 0)
    wanted = lax.broadcasted_iota(jnp.int32, (128, width), 1) + first
    return lax.dot_general(
        rows, (lane == wanted).astype(F32), (((1,), (0,)), ((), ())),
        precision=lax.Precision.HIGHEST, preferred_element_type=F32,
    )


def take_share(total, band, grad_in, grad_down, grad_up):
    into = columns(total[0:40], band * 8, 8)
    down = columns(total[DOWN_AT : DOWN_AT + 72], lax.rem(band, 8) * 16, 16)
    up = columns(total[UP_AT : UP_AT + 72], band * 8, 8)
    down = jnp.where(band < 8, down[0:36], down[36:72])
    for tap in range(9):
        j, l = tap // 3, tap % 3
        grad_in[j, l] = into[4 * tap : 4 * tap + 4]
        grad_down[j, l] = down[4 * tap : 4 * tap + 4]
        grad_up[j, l] = up[8 * tap : 8 * tap + 8]


class Gather:
    def __init__(self, job, own, full, sems):
        first, count, self.main = JOBS[job]
        self.rows = pl.ds(first, count)
        self.own, self.full = own, full
        self.sems = [sem.at[job] for sem in sems]
        self.x, self.y, self.z, self.core = place()
        self.carried = self.x + 4 * self.core
        self.holder = lax.rem(self.z, 8) == self.carried

    def beside(self, axis, by):
        if axis == "x":
            return device(on_ring(self.x, by, 4), self.y, self.z, self.core)
        return device(self.x, on_ring(self.y, by, 4), self.z, self.core)

    def along_z(self, count=7):
        send, recv = self.sems[0], self.sems[1]
        target = self.full.at[self.carried, self.y, self.rows]
        return [
            remote(
                self.own.at[self.rows], target, send.at[slot], recv.at[0],
                device(self.x, self.y, on_ring(self.z, by, 16), self.core),
            )
            for slot, by in enumerate(HOPS[:count])
        ]

    def light(self):
        send, recv = self.sems[2], self.sems[3]
        axis = "y" if self.main == "x" else "x"
        block = self.full.at[self.carried, self.y, self.rows]
        return [remote(block, block, send.at[by], recv.at[by], self.beside(axis, by)) for by in (1, 3, 2)]

    def piece(self, by, core):
        if self.main == "x":
            return self.full.at[on_ring(self.x, -by, 4) + 4 * core, :, self.rows]
        return self.full.at[pl.ds(4 * core, 4), on_ring(self.y, -by, 4), self.rows]

    def heavy(self, by):
        send, recv = self.sems[4], self.sems[5]
        block = self.piece(0, self.core)
        return remote(block, block, send.at[by], recv.at[by], self.beside(self.main, by))

    def across(self, by):
        send, recv = self.sems[6], self.sems[7]
        block = self.piece(by, self.core)
        other = device(self.x, self.y, self.z, 1 - self.core)
        return remote(block, block, send.at[by], recv.at[by], other)

    def step(self, stage):
        if stage == 0:

            @pl.when(self.holder)
            def _():
                every(self.along_z(), "start")
                self.full[self.carried, self.y, self.rows] = self.own[self.rows]

        if stage == 1:
            when(jnp.logical_not(self.holder), lambda: every(self.along_z(1), "wait_recv"))
            every(self.light(), "start")
        if stage == 2:
            every(self.light(), "wait_recv")
            for by in (1, 3, 2):
                self.heavy(by).start()
            self.across(0).start()
        if stage == 3:
            for by in (1, 3, 2):
                self.heavy(by).wait_recv()
                self.across(by).start()
        if stage == 4:
            for by in range(4):
                self.across(by).wait_recv()
        if stage == 5:
            when(self.holder, lambda: every(self.along_z(), "wait_send"))
            every(self.light(), "wait_send")
            for by in (1, 2, 3):
                self.heavy(by).wait_send()
            for by in range(4):
                self.across(by).wait_send()


class Reduce:
    def __init__(self, job, parts, buffers, sems, scale):
        first, count, self.main = JOBS[job]
        self.rows = pl.ds(first, count)
        self.parts = parts
        (
            self.from_core, self.heavy_out, self.heavy_in, self.sums, self.light_out, self.light_in,
            self.column, self.z_out, self.z_in, self.done, self.total, self.direct_out, self.direct_in,
        ) = buffers
        self.sems = [sem.at[job] for sem in sems]
        self.scale = scale
        self.at_once = job == IN
        self.x, self.y, self.z, self.core = place()
        self.carried = self.x + 4 * self.core
        self.holder = lax.rem(self.z, 8) == self.carried

    beside = Gather.beside

    def block(self, ref, by, core):
        if self.main == "x":
            return ref.at[on_ring(self.x, by, 4) + 4 * core, :, self.rows]
        return ref.at[pl.ds(4 * core, 4), on_ring(self.y, by, 4), self.rows]

    def across(self, by):
        other = device(self.x, self.y, self.z, 1 - self.core)
        return remote(
            self.block(self.parts, by, 1 - self.core), self.block(self.from_core, by, 0),
            self.sems[0].at[by], self.sems[1].at[by], other,
        )

    def heavy(self, by):
        return remote(
            self.heavy_out.at[by - 1, :, self.rows], self.heavy_in.at[by - 1, :, self.rows],
            self.sems[2].at[by], self.sems[3].at[by], self.beside(self.main, by),
        )

    def light(self, by):
        axis = "y" if self.main == "x" else "x"
        return remote(
            self.light_out.at[by - 1, self.rows], self.light_in.at[by - 1, self.rows],
            self.sems[4].at[by], self.sems[5].at[by], self.beside(axis, by),
        )

    def direct(self, slot):
        where = device(on_ring(self.x, slot // 4, 4), on_ring(self.y, slot % 4, 4), self.z, self.core)
        return remote(
            self.direct_out.at[slot], self.direct_in.at[slot], self.sems[10].at[slot], self.sems[11].at[slot], where
        )

    def step_direct(self, stage):
        rows = self.rows
        if stage == 1:
            for by in (2, 1, 3, 0):
                self.across(by).wait_recv()
                self.sums[:, rows] = self.both(by)
                for turn in (2, 1, 3, 0):
                    if by or turn:
                        slot = 4 * by + turn
                        self.direct_out[slot] = self.sums[on_ring(self.y, turn, 4), rows].astype(BF16)
                        self.direct(slot).start()
            self.column[rows] = self.sums[self.y, rows]
        if stage == 3:
            total = self.column[rows]
            for slot in (4, 12, 1, 3, 8, 2, 5, 7, 13, 15, 6, 9, 11, 14, 10):
                self.direct(slot).wait_recv()
                total += self.direct_in[slot].astype(F32)
            self.column[rows] = total
            self.send_to_holders(total)

    def send_to_holders(self, total):
        self.z_out[self.rows] = total.astype(BF16)
        for at in (0, 8):
            when(self.z != self.carried + at, self.to_holder(at).start)

    def to_holder(self, at):
        where = self.carried + at
        slot = lax.rem(self.z - where + 31, 16)
        return remote(
            self.z_out.at[self.rows], self.z_in.at[slot, self.rows],
            self.sems[6].at[at // 8], self.sems[7].at[slot], device(self.x, self.y, where, self.core),
        )

    def from_ring(self, slot):
        return remote(
            self.z_out.at[self.rows], self.z_in.at[slot, self.rows],
            self.sems[6].at[0], self.sems[7].at[slot], device(self.x, self.y, self.z, 1 - self.core),
        )

    def spread(self, count=7):
        return [
            remote(
                self.done.at[self.rows], self.total.at[self.rows],
                self.sems[8].at[2 * by + swap], self.sems[9].at[0],
                device(on_ring(self.x, by, 4), self.y, self.z, lax.rem(self.core + swap, 2)),
            )
            for by, swap in ((2, 0), (2, 1), (1, 0), (3, 0), (1, 1), (3, 1), (0, 1))[:count]
        ]

    def both(self, by):
        own = self.block(self.parts, by, self.core)[...].astype(F32)
        return own + self.block(self.from_core, by, 0)[...].astype(F32)

    def step(self, stage):
        rows = self.rows
        if self.at_once and stage in (1, 2, 3):
            return self.step_direct(stage)
        if stage == 0:
            for by in (1, 3, 2, 0):
                self.across(by).start()
        if stage == 1:
            for by in (1, 3, 2):
                self.across(by).wait_recv()
                self.heavy_out[by - 1, :, rows] = self.both(by).astype(BF16)
                self.heavy(by).start()
            self.across(0).wait_recv()
            self.sums[:, rows] = self.both(0)
        if stage == 2:
            total = self.sums[:, rows]
            for by in (1, 3, 2):
                self.heavy(by).wait_recv()
                total += self.heavy_in[by - 1, :, rows].astype(F32)
            self.sums[:, rows] = total
            here = self.y if self.main == "x" else self.x
            for by in (1, 3, 2):
                self.light_out[by - 1, rows] = self.sums[on_ring(here, by, 4), rows].astype(BF16)
                self.light(by).start()
            self.column[rows] = self.sums[here, rows]
        if stage == 3:
            total = self.column[rows]
            for by in (1, 3, 2):
                self.light(by).wait_recv()
                total += self.light_in[by - 1, rows].astype(F32)
            self.column[rows] = total
            self.send_to_holders(total)
        if stage == 4:

            @pl.when(self.holder)
            def _():
                total = self.column[rows]
                for slot in range(15):
                    self.from_ring(slot).wait_recv()
                    total += self.z_in[slot, rows].astype(F32)
                total = total * self.scale
                self.done[rows] = total
                every(self.spread(), "start")
                self.total[rows] = total

        if stage == 5:
            when(jnp.logical_not(self.holder), lambda: every(self.spread(1), "wait_recv"))
        if stage == 6:
            for by in range(4):
                self.across(by).wait_send()
            if self.at_once:
                for slot in range(1, 16):
                    self.direct(slot).wait_send()
            else:
                for by in (1, 2, 3):
                    self.heavy(by).wait_send()
                    self.light(by).wait_send()
            for at in (0, 8):
                when(self.z != self.carried + at, self.to_holder(at).wait_send)
            when(self.holder, lambda: every(self.spread(), "wait_send"))


def greet():
    x, y, z, core = place()
    carried = x + 4 * core
    holder = lax.rem(z, 8) == carried
    row, band = lax.axis_index("dp"), lax.axis_index("height")
    barrier = pltpu.get_barrier_semaphore()

    def signal(where):
        pl.semaphore_signal(barrier, inc=1, device_id=where, device_id_type=MESH)

    signal((row, on_ring(band, -1, 16)))
    signal((row, on_ring(band, 1, 16)))

    @pl.when(holder)
    def _():
        for by in (8, 7, 9, 6, 10, 5, 11, 4, 12, 3, 13, 2, 14, 1, 15):
            signal(device(x, y, on_ring(z, by, 16), core))

    @pl.when(jnp.logical_not(holder))
    def _():
        signal(device(x, y, carried, core))
        signal(device(x, y, carried + 8, core))

    for slot in (10, 6, 14, 9, 11, 5, 7, 13, 15, 8, 2, 4, 12, 1, 3):
        signal(device(on_ring(x, slot // 4, 4), on_ring(y, slot % 4, 4), z, core))
    for by in (2, 1, 3, 0):
        signal(device(on_ring(x, by, 4), y, z, 1 - core))
    return lambda: pl.semaphore_wait(barrier, jnp.where(holder, 21 + 15, 21 + 2))


def whole_kernel(
    scale,
    frames_far,
    cotangent_far,
    w_in,
    w_down,
    w_up,
    output,
    input_grad,
    grad_in,
    grad_down,
    grad_up,
    own,
    own_wide,
    frames,
    cotangent,
    frames_above,
    frames_below,
    cotangent_above,
    cotangent_below,
    grad_above,
    grad_below,
    full,
    parts,
    wide,
    fx,
    h3,
    c3,
    slopes,
    shifted,
    shifted_wide,
    coarse2,
    grad2,
    gx,
    mixed,
    win,
    wdn,
    wup,
    fine,
    down,
    up,
    back_fine,
    back_down,
    back_up,
    *rest,
):
    buffers, rest = rest[:13], rest[13:]
    gather_sems, reduce_sems, (halo_send, halo_recv, load_sem) = rest[:8], rest[8:20], rest[20:]
    band = lax.axis_index("height")
    top, bottom = band == 0, band == lax.axis_size("height") - 1
    under_top, over_bottom = jnp.logical_not(top), jnp.logical_not(bottom)

    loads = [
        pltpu.make_async_copy(frames_far, frames, load_sem.at[0]),
        pltpu.make_async_copy(cotangent_far, cotangent, load_sem.at[1]),
    ]
    every(loads, "start")
    gathers = [Gather(job, own, full, gather_sems) for job in range(3)]
    reduces = [Reduce(job, parts, buffers, reduce_sems, scale) for job in range(3)]

    row = lax.axis_index("dp")
    over, under = (row, on_ring(band, -1, 16)), (row, on_ring(band, 1, 16))

    def halo(slot, source, first, target, where):
        cells = source.at[pl.ds(first, target.shape[0])]
        return remote(cells, target, halo_send.at[slot], halo_recv.at[slot], where)

    downward = [
        halo(0, frames_far, 14, frames_above, under),
        halo(1, cotangent_far, 15, cotangent_above, under),
    ]
    upward = [
        halo(2, frames_far, 0, frames_below, over),
        halo(3, cotangent_far, 0, cotangent_below, over),
    ]

    all_there = greet()
    pack_own(w_in, w_down, w_up, own_wide, own)
    wide[:, 0:8] = jnp.zeros((23, 8, 128), F32)
    wide[:, 136:144] = jnp.zeros((23, 8, 128), F32)
    shifted[:, 0:8] = jnp.zeros((9, 8, 128), F32)
    shifted[:, 72:80] = jnp.zeros((9, 8, 128), F32)
    shifted_wide[:, 64:72] = jnp.zeros((9, 8, 256), F32)
    every(loads, "wait")
    spread_columns(frames, 4, wide, fx, 4)
    all_there()
    for job in range(3):
        gathers[job].step(0)

    @pl.when(top)
    def _():
        frames_above[...] = jnp.zeros_like(frames_above)
        cotangent_above[...] = jnp.zeros_like(cotangent_above)

    @pl.when(bottom)
    def _():
        frames_below[...] = jnp.zeros_like(frames_below)
        cotangent_below[...] = jnp.zeros_like(cotangent_below)

    gathers[IN].step(1)
    gathers[DOWN].step(1)
    gathers[UP].step(1)
    when(over_bottom, lambda: every(downward, "start"))
    when(under_top, lambda: every(upward, "start"))
    gathers[IN].step(2)
    gathers[DOWN].step(2)
    spread_columns(cotangent, 3, wide, c3, 3)
    gathers[IN].step(3)
    gathers[UP].step(2)
    gathers[DOWN].step(3)
    gathers[IN].step(4)
    unpack_in(full, win)
    stack_in(win, fine, back_fine)
    gathers[UP].step(3)
    gathers[DOWN].step(4)
    unpack_down(full, wdn)
    stack_down(wdn, down, back_down)
    gathers[UP].step(4)
    unpack_up(full, wup)
    stack_up(wup, up, back_up)

    when(under_top, lambda: every(downward, "wait_recv"))
    when(over_bottom, lambda: every(upward, "wait_recv"))
    spread_columns(frames_above, 2, wide, fx, 4)
    spread_columns(frames_below, 20, wide, fx, 4)
    spread_columns(cotangent_above, 2, wide, c3, 3)
    spread_columns(cotangent_below, 19, wide, c3, 3)

    for first, count in ((2, 7), (9, 6), (15, 6)):
        pre = sum(matmul(flat(fx[first + j : first + j + count]), fine[j]) for j in range(3))
        gate = sigmoid(pre)
        hidden = (pre * gate).reshape(count, 64, 256)
        slope = (gate * (1.0 + pre * (1.0 - gate))).reshape(count, 64, 256)
        shifted[0:count, 8:72] = hidden[:, :, 128:256]
        before = shifted[0:count, 7:71].astype(BF16)
        hidden = hidden.astype(BF16)
        for row in range(count):
            i = first + row
            h3[i // 2, i % 2, :, 0:128] = before[row]
            h3[i // 2, i % 2, :, 128:384] = hidden[row]
            if 3 <= i < 19:
                slopes[i - 3] = slope[row]

    @pl.when(top)
    def _():
        h3[1, 0] = jnp.zeros((64, 384), BF16)

    @pl.when(bottom)
    def _():
        for i in (19, 20):
            h3[i // 2, i % 2] = jnp.zeros((64, 384), BF16)

    views = ((1, 0), (1, 1), (2, 0))
    pre = sum(matmul(flat(h3[a : a + 9, b]), down[j]) for j, (a, b) in enumerate(views))
    gate = sigmoid(pre)
    coarse = (pre * gate).reshape(9, 64, 256)
    shifted_wide[:, 0:64] = coarse
    coarse2[:, :, 0:256] = coarse.astype(BF16)
    coarse2[:, :, 256:512] = shifted_wide[:, 1:65].astype(BF16)
    back = sum(matmul_t(flat(c3[a : a + 9, b]), back_up[j]) for j, (a, b) in enumerate(views))
    grad = (back * (gate * (1.0 + pre * (1.0 - gate)))).reshape(9, 64, 256)
    shifted_wide[:, 0:64] = grad
    grad2[:, :, 0:256] = grad.astype(BF16)
    grad2[:, :, 256:512] = shifted_wide[:, 1:65].astype(BF16)

    @pl.when(bottom)
    def _():
        coarse2[8] = jnp.zeros((64, 512), BF16)
        grad2[8] = jnp.zeros((64, 512), BF16)

    turned = flat(coarse2[0:8, :, 0:256]).T
    for j, (a, b) in enumerate(views):
        found = matmul(turned, flat(c3[a : a + 8, b]))
        for slot in range(3):
            wup[3 * (2 - j) + 2 - slot] = found[:, slot * 128 : slot * 128 + 128].astype(BF16)
    pack_up(parts, wup)
    reduces[UP].step(0)
    turned = flat(grad2[0:8, :, 0:256]).T
    for j, (a, b) in enumerate(views):
        found = matmul(turned, flat(h3[a : a + 8, b]))
        for slot in range(3):
            wdn[3 * j + slot] = found[:, slot * 128 : slot * 128 + 128].T.astype(BF16)
    pack_down(parts, wdn)
    reduces[DOWN].step(0)
    reduces[UP].step(1)

    grad_even = matmul_t(flat(grad2[0:8]), back_down[1]).reshape(8, 64, 256)
    grad_odd = (
        matmul_t(flat(grad2[0:8]), back_down[2]) + matmul_t(flat(grad2[1:9]), back_down[0])
    ).reshape(8, 64, 256)

    def store_grad(rows, places):
        count = len(places)
        ready = rows.astype(BF16)
        shifted[0:count, 8:72] = rows[:, :, 128:256]
        before = shifted[0:count, 7:71].astype(BF16)
        shifted[0:count, 8:72] = rows[:, :, 0:128]
        after = shifted[0:count, 9:73].astype(BF16)
        for m, k in enumerate(places):
            gx[k, :, 0:128] = before[m]
            gx[k, :, 128:384] = ready[m]
            gx[k, :, 384:512] = after[m]

    for start, rows in ((1, grad_even), (2, grad_odd)):
        places = range(start, start + 16, 2)
        rows = jnp.concatenate([rows[m : m + 1] * slopes[k - 1][None] for m, k in enumerate(places)], axis=0)
        store_grad(rows, places)
    grad_down_copy = [remote(gx.at[16, :, 128:384], grad_above, halo_send.at[4], halo_recv.at[4], under)]
    grad_up_copy = [remote(gx.at[1, :, 128:384], grad_below, halo_send.at[5], halo_recv.at[5], over)]
    when(over_bottom, lambda: every(grad_down_copy, "start"))
    when(under_top, lambda: every(grad_up_copy, "start"))

    reduces[DOWN].step(1)
    turned = flat(gx[1:17, :, 128:384]).T
    for j in range(3):
        found = matmul(turned, flat(fx[3 + j : 19 + j]))
        for l in range(3):
            both = found[0:128, l * 128 : l * 128 + 128] + found[128:256, (l + 1) * 128 : (l + 2) * 128]
            win[3 * j + l] = both.T.astype(BF16)
    pack_in(parts, win)
    reduces[IN].step(0)
    reduces[UP].step(2)
    reduces[IN].step(1)

    def mix(row, cells):
        mixed[row, pl.ds(0, 64, stride=2), :] = cells[:, 0:128]
        mixed[row, pl.ds(1, 64, stride=2), :] = cells[:, 128:256]

    even = matmul(flat(coarse2[0:8]), up[1])
    odd = matmul(flat(coarse2[0:8]), up[0]) + matmul(flat(coarse2[1:9]), up[2])
    for t in range(8):
        mix(2 * t, even[64 * t : 64 * t + 64])
        mix(2 * t + 1, odd[64 * t : 64 * t + 64])
    output[...] = (frames[...].astype(F32) + mixed[...]).astype(BF16)
    reduces[DOWN].step(2)
    reduces[UP].step(3)
    reduces[IN].step(2)

    reduces[DOWN].step(3)
    reduces[IN].step(3)

    @pl.when(top)
    def _():
        grad_above[...] = jnp.zeros_like(grad_above)

    @pl.when(bottom)
    def _():
        grad_below[...] = jnp.zeros_like(grad_below)

    when(under_top, lambda: every(grad_down_copy, "wait_recv"))
    when(over_bottom, lambda: every(grad_up_copy, "wait_recv"))
    store_grad(grad_above[...].astype(F32)[None], (0,))
    store_grad(grad_below[...].astype(F32)[None], (17,))
    for first in (0, 8):
        back = sum(matmul_t(flat(gx[first + j : first + j + 8]), back_fine[j]) for j in range(3))
        for row in range(8):
            mix(first + row, back[64 * row : 64 * row + 64])
    input_grad[...] = (cotangent[...].astype(F32) + mixed[...]).astype(BF16)
    for job in (UP, DOWN, IN):
        reduces[job].step(4)
    for job in (UP, DOWN, IN):
        reduces[job].step(5)

    take_share(buffers[10], band, grad_in, grad_down, grad_up)
    for job in range(3):
        gathers[job].step(5)
        reduces[job].step(6)
    when(over_bottom, lambda: every(downward, "wait_send"))
    when(under_top, lambda: every(upward, "wait_send"))
    when(over_bottom, lambda: every(grad_down_copy, "wait_send"))
    when(under_top, lambda: every(grad_up_copy, "wait_send"))


def whole(frames, cotangent, w_in, w_down, w_up, scale):
    vmem, dma = pltpu.VMEM, pltpu.SemaphoreType.DMA
    spec, far = pl.BlockSpec(memory_space=vmem), pl.BlockSpec(memory_space=pl.ANY)
    gather_counts = (7, 1, 4, 4, 4, 4, 4, 4)
    reduce_counts = (4, 4, 4, 4, 4, 4, 2, 15, 8, 1, 16, 16)
    return pl.pallas_call(
        functools.partial(whole_kernel, scale),
        out_shape=(
            jax.ShapeDtypeStruct((16, 128, 128), BF16),
            jax.ShapeDtypeStruct((16, 128, 128), BF16),
            jax.ShapeDtypeStruct((3, 3, 4, 8), F32),
            jax.ShapeDtypeStruct((3, 3, 4, 16), F32),
            jax.ShapeDtypeStruct((3, 3, 8, 8), F32),
        ),
        in_specs=[far, far, spec, spec, spec],
        out_specs=(spec,) * 5,
        scratch_shapes=[
            vmem((PACK, 128), BF16),
            vmem((PACK, 128), F32),
            vmem((16, 128, 128), BF16),
            vmem((16, 128, 128), BF16),
            vmem((2, 128, 128), BF16),
            vmem((3, 128, 128), BF16),
            vmem((1, 128, 128), BF16),
            vmem((2, 128, 128), BF16),
            vmem((64, 256), BF16),
            vmem((64, 256), BF16),
            vmem((8, 4, PACK, 128), BF16),
            vmem((8, 4, PACK, 128), BF16),
            vmem((23, 144, 128), F32),
            vmem((23, 64, 512), BF16),
            vmem((11, 2, 64, 384), BF16),
            vmem((11, 2, 64, 384), BF16),
            vmem((16, 64, 256), F32),
            vmem((9, 80, 128), F32),
            vmem((9, 72, 256), F32),
            vmem((9, 64, 512), BF16),
            vmem((9, 64, 512), BF16),
            vmem((18, 64, 512), BF16),
            vmem((16, 128, 128), F32),
            vmem((9, 128, 128), BF16),
            vmem((9, 128, 256), BF16),
            vmem((9, 256, 128), BF16),
            vmem((3, 512, 256), BF16),
            vmem((3, 384, 256), BF16),
            vmem((3, 512, 256), BF16),
            vmem((3, 256, 512), BF16),
            vmem((3, 256, 512), BF16),
            vmem((3, 256, 384), BF16),
            vmem((4, 4, PACK, 128), BF16),
            vmem((3, 4, PACK, 128), BF16),
            vmem((3, 4, PACK, 128), BF16),
            vmem((4, PACK, 128), F32),
            vmem((3, PACK, 128), BF16),
            vmem((3, PACK, 128), BF16),
            vmem((PACK, 128), F32),
            vmem((PACK, 128), BF16),
            vmem((15, PACK, 128), BF16),
            vmem((PACK, 128), F32),
            vmem((PACK, 128), F32),
            vmem((16, DOWN_AT, 128), BF16),
            vmem((16, DOWN_AT, 128), BF16),
        ]
        + [dma((3, count)) for count in gather_counts + reduce_counts]
        + [dma((6,)), dma((6,)), dma((2,))],
        compiler_params=pltpu.CompilerParams(
            collective_id=0, has_side_effects=True, vmem_limit_bytes=56 << 20
        ),
    )(frames, cotangent, w_in, w_down, w_up)


def hand_on_kernel(*refs):
    half = len(refs) // 2
    for source, target in zip(refs[:half], refs[half:]):
        target[...] = source[...]


def hand_on(arrays):
    spec = pl.BlockSpec(memory_space=pltpu.VMEM)
    return pl.pallas_call(
        hand_on_kernel,
        out_shape=tuple(jax.ShapeDtypeStruct(array.shape, array.dtype) for array in arrays),
        in_specs=[spec] * len(arrays),
        out_specs=(spec,) * len(arrays),
        compiler_params=pltpu.CompilerParams(vmem_limit_bytes=56 << 20),
    )(*arrays)


def on_device(frames, cotangent, w_in, w_down, w_up):
    frames, cotangent = frames[0], cotangent[0]
    pixel_count = lax.axis_size("dp") * lax.axis_size("height") * frames.shape[0] * frames.shape[1]
    output, input_grad, *grads = hand_on(whole(frames, cotangent, w_in, w_down, w_up, 1.0 / math.sqrt(pixel_count)))
    return (output[None], input_grad[None], *grads)


def solution(mesh):
    in_specs = (
        P("dp", "height", None, None),
        P("dp", "height", None, None),
        P(None, None, "dp", None),
        P(None, None, "dp", None),
        P(None, None, "dp", None),
    )
    out_specs = (
        P("dp", "height", None, None),
        P("dp", "height", None, None),
        P(None, None, "dp", "height"),
        P(None, None, "dp", "height"),
        P(None, None, "dp", "height"),
    )
    return jax.shard_map(
        on_device, mesh=mesh, in_specs=in_specs, out_specs=out_specs, check_vma=False
    )
```

```python
import functools
import math

import jax
import jax.numpy as jnp
from jax import lax
from jax.experimental import pallas as pl
from jax.experimental.pallas import tpu as pltpu
from jax.sharding import PartitionSpec as P

F32, BF16 = jnp.float32, jnp.bfloat16
MESH = pl.DeviceIdType.MESH

PACK = 208
DOWN_AT = 48
UP_AT = 128
HOPS = (1, -1, 2, -2, 3, -3, 4)
JOBS = ((0, 48, "x"), (48, 80, "y"), (128, 80, "x"))
IN, DOWN, UP = 0, 1, 2


def place():
    d = lax.axis_index("dp")
    h = lax.axis_index("height")
    z = lax.rem(lax.div(h, 2), 2) * 8 + lax.rem(d, 8)
    return lax.div(h, 4), lax.div(d, 8), z, lax.rem(h, 2)


def device(x, y, z, core):
    return (y * 8 + lax.rem(z, 8), x * 4 + lax.div(z, 8) * 2 + core)


def on_ring(position, by, size):
    return lax.rem(position + by + size, size)


def remote(source, target, send, recv, where):
    return pltpu.make_async_remote_copy(
        src_ref=source, dst_ref=target, send_sem=send, recv_sem=recv, device_id=where, device_id_type=MESH
    )


def when(condition, action):
    @pl.when(condition)
    def _():
        action()


def every(copies, act):
    for copy in copies:
        getattr(copy, act)()


def spread_columns(rows, first, wide, stacked, slots):
    count = rows.shape[0]
    wide[pl.ds(first, count), 8:136] = rows[...].astype(F32)
    for row in range(first, first + count):
        target = stacked.at[row] if len(stacked.shape) == 3 else stacked.at[row // 2, row % 2]
        for slot in range(slots):
            target[:, slot * 128 : slot * 128 + 128] = wide[row, pl.ds(7 + slot, 64, stride=2), :].astype(BF16)


def matmul(left, right):
    return lax.dot_general(left, right, (((1,), (0,)), ((), ())), preferred_element_type=F32)


def matmul_t(left, right):
    return lax.dot_general(left, right, (((1,), (1,)), ((), ())), preferred_element_type=F32)


def flat(cells):
    return cells.reshape(cells.shape[0] * cells.shape[1], cells.shape[2])


def shuffle(taps, channels, pitch, transposed):
    shards = 16 // channels
    dims = (shards * pitch, taps * 16) if transposed else (taps * 16, shards * pitch)
    row = lax.broadcasted_iota(jnp.int32, dims, 1 if transposed else 0)
    column = lax.broadcasted_iota(jnp.int32, dims, 0 if transposed else 1)
    bits = channels.bit_length() - 1
    wanted = ((row & 15) >> bits) * pitch + (row >> 4) * channels + (row & (channels - 1))
    return (column == wanted).astype(F32).astype(BF16)


def unpack_in(full, win):
    order = shuffle(9, 4, 48, False)
    for group in range(8):
        k, y = 4 * (group % 2), group // 2
        rows = matmul(order, full[k : k + 4, y, 0:DOWN_AT].reshape(192, 128)).astype(BF16)
        win[:, 16 * group : 16 * group + 16] = rows.reshape(9, 16, 128)


def unpack_down(full, wdn):
    order = shuffle(18, 4, 80, False)
    for group in range(8):
        k, y = 4 * (group % 2), group // 2
        rows = matmul(order, full[k : k + 4, y, DOWN_AT:UP_AT].reshape(320, 128)).astype(BF16)
        wdn[:, 16 * group : 16 * group + 16, 0:128] = rows[0:144].reshape(9, 16, 128)
        wdn[:, 16 * group : 16 * group + 16, 128:256] = rows[144:288].reshape(9, 16, 128)


def unpack_up(full, wup):
    order = shuffle(9, 8, 80, False)
    for group in range(16):
        k, y = 2 * (group % 4), group // 4
        rows = matmul(order, full[k : k + 2, y, UP_AT:PACK].reshape(160, 128)).astype(BF16)
        wup[:, 16 * group : 16 * group + 16] = rows.reshape(9, 16, 128)


def pack_in(parts, sin):
    order = shuffle(9, 4, 48, True)
    for group in range(8):
        k, y = 4 * (group % 2), group // 2
        rows = matmul(order, sin[:, 16 * group : 16 * group + 16].reshape(144, 128)).astype(BF16)
        parts[k : k + 4, y, 0:DOWN_AT] = rows.reshape(4, 48, 128)


def pack_down(parts, sdn):
    order = shuffle(18, 4, 80, True)
    for group in range(8):
        k, y = 4 * (group % 2), group // 2
        halves = [sdn[:, 16 * group : 16 * group + 16, at : at + 128].reshape(144, 128) for at in (0, 128)]
        rows = matmul(order, jnp.concatenate(halves, axis=0)).astype(BF16)
        parts[k : k + 4, y, DOWN_AT:UP_AT] = rows.reshape(4, 80, 128)


def pack_up(parts, sup):
    order = shuffle(9, 8, 80, True)
    for group in range(16):
        k, y = 2 * (group % 4), group // 4
        rows = matmul(order, sup[:, 16 * group : 16 * group + 16].reshape(144, 128)).astype(BF16)
        parts[k : k + 2, y, UP_AT:PACK] = rows.reshape(2, 80, 128)


def stack_in(win, fine, back_fine):
    blank = jnp.zeros((128, 128), BF16)
    for j in range(3):
        for slot in range(4):
            at = slice(slot * 128, slot * 128 + 128)
            fine[j, at, 0:128] = win[3 * j + slot] if slot < 3 else blank
            fine[j, at, 128:256] = win[3 * j + slot - 1] if slot > 0 else blank
            back_fine[j, 0:128, at] = win[3 * (2 - j) + 2 - slot] if slot < 3 else blank
            back_fine[j, 128:256, at] = win[3 * (2 - j) + 3 - slot] if slot > 0 else blank


def stack_down(wdn, down, back_down):
    for j in range(3):
        for slot in range(3):
            down[j, slot * 128 : slot * 128 + 128, :] = wdn[3 * j + slot]
        back_down[j, 0:128, 0:256] = wdn[3 * j + 1]
        back_down[j, 0:128, 256:512] = jnp.zeros((128, 256), BF16)
        back_down[j, 128:256, 0:256] = wdn[3 * j + 2]
        back_down[j, 128:256, 256:512] = wdn[3 * j]


def stack_up(wup, up, back_up):
    for j in range(3):
        for slot in range(3):
            back_up[j, :, slot * 128 : slot * 128 + 128] = wup[3 * (2 - j) + 2 - slot]
        up[j, 0:256, 0:128] = wup[3 * j + 1]
        up[j, 0:256, 128:256] = wup[3 * j]
        up[j, 256:512, 0:128] = jnp.zeros((256, 128), BF16)
        up[j, 256:512, 128:256] = wup[3 * j + 2]


def sigmoid(value):
    return 0.5 + 0.5 * jnp.tanh(0.5 * value)


def pack_own(w_in, w_down, w_up, wide, own):
    wide[...] = jnp.zeros_like(wide)
    for tap in range(9):
        j, l = tap // 3, tap % 3
        wide[4 * tap : 4 * tap + 4] = w_in[j, l].astype(F32)
        for half in range(2):
            at = DOWN_AT + 36 * half + 4 * tap
            wide[at : at + 4] = w_down[j, l, :, 128 * half : 128 * half + 128].astype(F32)
        wide[UP_AT + 8 * tap : UP_AT + 8 * tap + 8] = w_up[j, l].astype(F32)
    own[...] = wide[...].astype(BF16)


def lanes(block, first, count):
    lane = lax.broadcasted_iota(jnp.int32, (count, 128), 1)
    wanted = lax.broadcasted_iota(jnp.int32, (count, 128), 0) + first
    return lax.dot_general(
        (lane == wanted).astype(F32), block, (((1,), (1,)), ((), ())),
        precision=lax.Precision.HIGHEST, preferred_element_type=F32,
    )


def take_share(share, band, grad_in, grad_down, grad_up):
    into = lanes(share[IN, 0:8], 0, 40)
    down = lanes(share[DOWN, 0:16], 36 * lax.div(band, 8), 40)
    up = lanes(share[UP, 0:8], 0, 72)
    for tap in range(9):
        j, l = tap // 3, tap % 3
        grad_in[j, l] = into[4 * tap : 4 * tap + 4]
        grad_down[j, l] = down[4 * tap : 4 * tap + 4]
        grad_up[j, l] = up[8 * tap : 8 * tap + 8]


class Gather:
    def __init__(self, job, own, full, sems):
        first, count, self.main = JOBS[job]
        self.rows = pl.ds(first, count)
        self.own, self.full = own, full
        self.sems = [sem.at[job] for sem in sems]
        self.x, self.y, self.z, self.core = place()
        self.carried = self.x + 4 * self.core
        self.holder = lax.rem(self.z, 8) == self.carried

    def beside(self, axis, by):
        if axis == "x":
            return device(on_ring(self.x, by, 4), self.y, self.z, self.core)
        return device(self.x, on_ring(self.y, by, 4), self.z, self.core)

    def along_z(self, count=7):
        send, recv = self.sems[0], self.sems[1]
        target = self.full.at[self.carried, self.y, self.rows]
        return [
            remote(
                self.own.at[self.rows], target, send.at[slot], recv.at[0],
                device(self.x, self.y, on_ring(self.z, by, 16), self.core),
            )
            for slot, by in enumerate(HOPS[:count])
        ]

    def light(self):
        send, recv = self.sems[2], self.sems[3]
        axis = "y" if self.main == "x" else "x"
        block = self.full.at[self.carried, self.y, self.rows]
        return [remote(block, block, send.at[by], recv.at[by], self.beside(axis, by)) for by in (1, 3, 2)]

    def piece(self, by, core):
        if self.main == "x":
            return self.full.at[on_ring(self.x, -by, 4) + 4 * core, :, self.rows]
        return self.full.at[pl.ds(4 * core, 4), on_ring(self.y, -by, 4), self.rows]

    def heavy(self, by):
        send, recv = self.sems[4], self.sems[5]
        block = self.piece(0, self.core)
        return remote(block, block, send.at[by], recv.at[by], self.beside(self.main, by))

    def across(self, by):
        send, recv = self.sems[6], self.sems[7]
        block = self.piece(by, self.core)
        other = device(self.x, self.y, self.z, 1 - self.core)
        return remote(block, block, send.at[by], recv.at[by], other)

    def step(self, stage):
        if stage == 0:

            @pl.when(self.holder)
            def _():
                every(self.along_z(), "start")
                self.full[self.carried, self.y, self.rows] = self.own[self.rows]

        if stage == 1:
            when(jnp.logical_not(self.holder), lambda: every(self.along_z(1), "wait_recv"))
            every(self.light(), "start")
        if stage == 2:
            every(self.light(), "wait_recv")
            for by in (1, 3, 2):
                self.heavy(by).start()
            self.across(0).start()
        if stage == 3:
            for by in (1, 3, 2):
                self.heavy(by).wait_recv()
                self.across(by).start()
        if stage == 4:
            for by in range(4):
                self.across(by).wait_recv()
        if stage == 5:
            when(self.holder, lambda: every(self.along_z(), "wait_send"))
            every(self.light(), "wait_send")
            for by in (1, 2, 3):
                self.heavy(by).wait_send()
            for by in range(4):
                self.across(by).wait_send()


class Reduce:
    def __init__(self, job, parts, buffers, sems, scale):
        first, self.count, self.main = JOBS[job]
        self.rows = pl.ds(first, self.count)
        self.job, self.width = job, 16 if job == DOWN else 8
        self.parts = parts
        (
            self.from_core, self.heavy_out, self.heavy_in, self.sums, self.light_out, self.light_in,
            self.column, self.z_out, self.z_in, self.done, self.share, self.direct_out, self.direct_in,
        ) = buffers
        self.sems = [sem.at[job] for sem in sems]
        self.scale = scale
        self.at_once = job == IN
        self.x, self.y, self.z, self.core = place()
        self.carried = self.x + 4 * self.core
        self.holder = lax.rem(self.z, 8) == self.carried

    beside = Gather.beside

    def block(self, ref, by, core):
        if self.main == "x":
            return ref.at[on_ring(self.x, by, 4) + 4 * core, :, self.rows]
        return ref.at[pl.ds(4 * core, 4), on_ring(self.y, by, 4), self.rows]

    def across(self, by):
        other = device(self.x, self.y, self.z, 1 - self.core)
        return remote(
            self.block(self.parts, by, 1 - self.core), self.block(self.from_core, by, 0),
            self.sems[0].at[by], self.sems[1].at[by], other,
        )

    def heavy(self, by):
        return remote(
            self.heavy_out.at[by - 1, :, self.rows], self.heavy_in.at[by - 1, :, self.rows],
            self.sems[2].at[by], self.sems[3].at[by], self.beside(self.main, by),
        )

    def light(self, by):
        axis = "y" if self.main == "x" else "x"
        return remote(
            self.light_out.at[by - 1, self.rows], self.light_in.at[by - 1, self.rows],
            self.sems[4].at[by], self.sems[5].at[by], self.beside(axis, by),
        )

    def direct(self, slot):
        where = device(on_ring(self.x, slot // 4, 4), on_ring(self.y, slot % 4, 4), self.z, self.core)
        return remote(
            self.direct_out.at[slot], self.direct_in.at[slot], self.sems[10].at[slot], self.sems[11].at[slot], where
        )

    def step_direct(self, stage):
        rows = self.rows
        if stage == 1:
            for by in (2, 1, 3, 0):
                self.across(by).wait_recv()
                self.sums[:, rows] = self.both(by)
                for turn in (2, 1, 3, 0):
                    if by or turn:
                        slot = 4 * by + turn
                        self.direct_out[slot] = self.sums[on_ring(self.y, turn, 4), rows].astype(BF16)
                        self.direct(slot).start()
            self.column[rows] = self.sums[self.y, rows]
        if stage == 3:
            total = self.column[rows]
            for slot in (4, 12, 1, 3, 8, 2, 5, 7, 13, 15, 6, 9, 11, 14, 10):
                self.direct(slot).wait_recv()
                total += self.direct_in[slot].astype(F32)
            self.column[rows] = total
            self.send_to_holders(total)

    def send_to_holders(self, total):
        self.z_out[self.rows] = total.astype(BF16)
        for at in (0, 8):
            when(self.z != self.carried + at, self.to_holder(at).start)

    def to_holder(self, at):
        where = self.carried + at
        slot = lax.rem(self.z - where + 31, 16)
        return remote(
            self.z_out.at[self.rows], self.z_in.at[slot, self.rows],
            self.sems[6].at[at // 8], self.sems[7].at[slot], device(self.x, self.y, where, self.core),
        )

    def from_ring(self, slot):
        return remote(
            self.z_out.at[self.rows], self.z_in.at[slot, self.rows],
            self.sems[6].at[0], self.sems[7].at[slot], device(self.x, self.y, self.z, 1 - self.core),
        )

    def columns_of(self, x, core):
        band = lax.rem(x * 4 + lax.div(self.z, 8) * 2 + core, 128 // self.width)
        return pl.ds(pl.multiple_of(band * self.width, 8), self.width)

    def spread(self, count=7):
        return [
            remote(
                self.done.at[self.job, self.columns_of(on_ring(self.x, by, 4), lax.rem(self.core + swap, 2))],
                self.share.at[self.job, pl.ds(0, self.width)],
                self.sems[8].at[2 * by + swap], self.sems[9].at[0],
                device(on_ring(self.x, by, 4), self.y, self.z, lax.rem(self.core + swap, 2)),
            )
            for by, swap in ((2, 0), (2, 1), (1, 0), (3, 0), (1, 1), (3, 1), (0, 1))[:count]
        ]

    def both(self, by):
        own = self.block(self.parts, by, self.core)[...].astype(F32)
        return own + self.block(self.from_core, by, 0)[...].astype(F32)

    def step(self, stage):
        rows = self.rows
        if self.at_once and stage in (1, 2, 3):
            return self.step_direct(stage)
        if stage == 0:
            for by in (1, 3, 2, 0):
                self.across(by).start()
        if stage == 1:
            for by in (1, 3, 2):
                self.across(by).wait_recv()
                self.heavy_out[by - 1, :, rows] = self.both(by).astype(BF16)
                self.heavy(by).start()
            self.across(0).wait_recv()
            self.sums[:, rows] = self.both(0)
        if stage == 2:
            total = self.sums[:, rows]
            for by in (1, 3, 2):
                self.heavy(by).wait_recv()
                total += self.heavy_in[by - 1, :, rows].astype(F32)
            self.sums[:, rows] = total
            here = self.y if self.main == "x" else self.x
            for by in (1, 3, 2):
                self.light_out[by - 1, rows] = self.sums[on_ring(here, by, 4), rows].astype(BF16)
                self.light(by).start()
            self.column[rows] = self.sums[here, rows]
        if stage == 3:
            total = self.column[rows]
            for by in (1, 3, 2):
                self.light(by).wait_recv()
                total += self.light_in[by - 1, rows].astype(F32)
            self.column[rows] = total
            self.send_to_holders(total)
        if stage == 4:

            @pl.when(self.holder)
            def _():
                total = self.column[rows]
                for slot in range(15):
                    self.from_ring(slot).wait_recv()
                    total += self.z_in[slot, rows].astype(F32)
                self.done[self.job, :, 0 : self.count] = (total * self.scale).T
                every(self.spread(), "start")
                self.share[self.job, 0 : self.width] = self.done[self.job, self.columns_of(self.x, self.core)]

        if stage == 5:
            when(jnp.logical_not(self.holder), lambda: every(self.spread(1), "wait_recv"))
        if stage == 6:
            for by in range(4):
                self.across(by).wait_send()
            if self.at_once:
                for slot in range(1, 16):
                    self.direct(slot).wait_send()
            else:
                for by in (1, 2, 3):
                    self.heavy(by).wait_send()
                    self.light(by).wait_send()
            for at in (0, 8):
                when(self.z != self.carried + at, self.to_holder(at).wait_send)
            when(self.holder, lambda: every(self.spread(), "wait_send"))


def greet():
    x, y, z, core = place()
    carried = x + 4 * core
    holder = lax.rem(z, 8) == carried
    row, band = lax.axis_index("dp"), lax.axis_index("height")
    barrier = pltpu.get_barrier_semaphore()

    def signal(where):
        pl.semaphore_signal(barrier, inc=1, device_id=where, device_id_type=MESH)

    signal((row, on_ring(band, -1, 16)))
    signal((row, on_ring(band, 1, 16)))

    @pl.when(holder)
    def _():
        for by in (8, 7, 9, 6, 10, 5, 11, 4, 12, 3, 13, 2, 14, 1, 15):
            signal(device(x, y, on_ring(z, by, 16), core))

    @pl.when(jnp.logical_not(holder))
    def _():
        signal(device(x, y, carried, core))
        signal(device(x, y, carried + 8, core))

    for slot in (10, 6, 14, 9, 11, 5, 7, 13, 15, 8, 2, 4, 12, 1, 3):
        signal(device(on_ring(x, slot // 4, 4), on_ring(y, slot % 4, 4), z, core))
    for by in (2, 1, 3, 0):
        signal(device(on_ring(x, by, 4), y, z, 1 - core))
    return lambda: pl.semaphore_wait(barrier, jnp.where(holder, 21 + 15, 21 + 2))


def whole_kernel(
    scale,
    frames_far,
    cotangent_far,
    w_in,
    w_down,
    w_up,
    output_far,
    input_grad_far,
    grad_in,
    grad_down,
    grad_up,
    own,
    own_wide,
    output,
    input_grad,
    frames,
    cotangent,
    frames_above,
    frames_below,
    cotangent_above,
    cotangent_below,
    grad_above,
    grad_below,
    full,
    parts,
    wide,
    fx,
    h3,
    c3,
    slopes,
    shifted,
    shifted_wide,
    coarse2,
    grad2,
    gx,
    mixed,
    win,
    wdn,
    wup,
    sup,
    turned_frames,
    fine,
    down,
    up,
    back_fine,
    back_down,
    back_up,
    *rest,
):
    buffers, rest = rest[:13], rest[13:]
    gather_sems, reduce_sems, (halo_send, halo_recv, load_sem) = rest[:8], rest[8:20], rest[20:]
    band = lax.axis_index("height")
    top, bottom = band == 0, band == lax.axis_size("height") - 1
    under_top, over_bottom = jnp.logical_not(top), jnp.logical_not(bottom)

    loads = [
        pltpu.make_async_copy(frames_far, frames, load_sem.at[0]),
        pltpu.make_async_copy(cotangent_far, cotangent, load_sem.at[1]),
    ]
    every(loads, "start")
    stores = [
        pltpu.make_async_copy(output, output_far, load_sem.at[2]),
        pltpu.make_async_copy(input_grad, input_grad_far, load_sem.at[3]),
    ]
    gathers = [Gather(job, own, full, gather_sems) for job in range(3)]
    reduces = [Reduce(job, parts, buffers, reduce_sems, scale) for job in range(3)]

    row = lax.axis_index("dp")
    over, under = (row, on_ring(band, -1, 16)), (row, on_ring(band, 1, 16))

    def halo(slot, source, first, target, where):
        cells = source.at[pl.ds(first, target.shape[0])]
        return remote(cells, target, halo_send.at[slot], halo_recv.at[slot], where)

    downward = [
        halo(0, frames_far, 14, frames_above, under),
        halo(1, cotangent_far, 15, cotangent_above, under),
    ]
    upward = [
        halo(2, frames_far, 0, frames_below, over),
        halo(3, cotangent_far, 0, cotangent_below, over),
    ]

    all_there = greet()
    pack_own(w_in, w_down, w_up, own_wide, own)
    buffers[9][...] = jnp.zeros((3, 128, 128), F32)
    wide[:, 0:8] = jnp.zeros((23, 8, 128), F32)
    wide[:, 136:144] = jnp.zeros((23, 8, 128), F32)
    shifted[:, 0:8] = jnp.zeros((9, 8, 128), F32)
    shifted[:, 72:80] = jnp.zeros((9, 8, 128), F32)
    shifted_wide[:, 64:72] = jnp.zeros((9, 8, 256), F32)
    every(loads, "wait")
    spread_columns(frames, 4, wide, fx, 4)

    def turn(j, pair):
        rows = flat(fx[3 + j + 2 * pair : 5 + j + 2 * pair])
        turned_frames[512 * j : 512 * j + 512, 128 * pair : 128 * pair + 128] = rows.T

    for pair in range(8):
        turn(1, pair)
    all_there()
    for job in range(3):
        gathers[job].step(0)

    @pl.when(top)
    def _():
        frames_above[...] = jnp.zeros_like(frames_above)
        cotangent_above[...] = jnp.zeros_like(cotangent_above)

    @pl.when(bottom)
    def _():
        frames_below[...] = jnp.zeros_like(frames_below)
        cotangent_below[...] = jnp.zeros_like(cotangent_below)

    gathers[IN].step(1)
    gathers[DOWN].step(1)
    gathers[UP].step(1)
    when(over_bottom, lambda: every(downward, "start"))
    when(under_top, lambda: every(upward, "start"))
    gathers[IN].step(2)
    gathers[DOWN].step(2)
    for pair in range(7):
        turn(0, pair + 1)
        turn(2, pair)
    spread_columns(cotangent, 3, wide, c3, 3)
    gathers[IN].step(3)
    gathers[UP].step(2)
    gathers[DOWN].step(3)
    gathers[IN].step(4)
    def fine_rows(first, count):
        pre = sum(matmul(flat(fx[first + j : first + j + count]), fine[j]) for j in range(3))
        gate = sigmoid(pre)
        hidden = (pre * gate).reshape(count, 64, 256)
        slope = (gate * (1.0 + pre * (1.0 - gate))).reshape(count, 64, 256)
        shifted[0:count, 8:72] = hidden[:, :, 128:256]
        before = shifted[0:count, 7:71].astype(BF16)
        hidden = hidden.astype(BF16)
        for row in range(count):
            i = first + row
            h3[i // 2, i % 2, :, 0:128] = before[row]
            h3[i // 2, i % 2, :, 128:384] = hidden[row]
            if 3 <= i < 19:
                slopes[i - 3] = slope[row]

    unpack_in(full, win)
    stack_in(win, fine, back_fine)
    fine_rows(4, 7)
    gathers[UP].step(3)
    gathers[DOWN].step(4)
    unpack_down(full, wdn)
    stack_down(wdn, down, back_down)
    fine_rows(11, 7)

    when(under_top, lambda: every(downward, "wait_recv"))
    when(over_bottom, lambda: every(upward, "wait_recv"))
    spread_columns(frames_above, 2, wide, fx, 4)
    spread_columns(frames_below, 20, wide, fx, 4)
    spread_columns(cotangent_above, 2, wide, c3, 3)
    spread_columns(cotangent_below, 19, wide, c3, 3)

    fine_rows(2, 2)
    fine_rows(18, 3)

    @pl.when(top)
    def _():
        h3[1, 0] = jnp.zeros((64, 384), BF16)

    @pl.when(bottom)
    def _():
        for i in (19, 20):
            h3[i // 2, i % 2] = jnp.zeros((64, 384), BF16)

    views = ((1, 0), (1, 1), (2, 0))
    pre = sum(matmul(flat(h3[a : a + 9, b]), down[j]) for j, (a, b) in enumerate(views))
    gate = sigmoid(pre)
    coarse = (pre * gate).reshape(9, 64, 256)
    shifted_wide[:, 0:64] = coarse
    coarse2[:, :, 0:256] = coarse.astype(BF16)
    coarse2[:, :, 256:512] = shifted_wide[:, 1:65].astype(BF16)
    turned = flat(coarse2[0:8, :, 0:256]).T
    for j, (a, b) in enumerate(views):
        found = matmul(turned, flat(c3[a : a + 8, b]))
        for slot in range(3):
            sup[3 * (2 - j) + 2 - slot] = found[:, slot * 128 : slot * 128 + 128].astype(BF16)
    pack_up(parts, sup)
    reduces[UP].step(0)
    gathers[UP].step(4)
    unpack_up(full, wup)
    stack_up(wup, up, back_up)
    back = sum(matmul_t(flat(c3[a : a + 9, b]), back_up[j]) for j, (a, b) in enumerate(views))
    grad = (back * (gate * (1.0 + pre * (1.0 - gate)))).reshape(9, 64, 256)
    shifted_wide[:, 0:64] = grad
    grad2[:, :, 0:256] = grad.astype(BF16)
    grad2[:, :, 256:512] = shifted_wide[:, 1:65].astype(BF16)

    @pl.when(bottom)
    def _():
        coarse2[8] = jnp.zeros((64, 512), BF16)
        grad2[8] = jnp.zeros((64, 512), BF16)

    turned = flat(grad2[0:8, :, 0:256]).T
    for j, (a, b) in enumerate(views):
        found = matmul(turned, flat(h3[a : a + 8, b]))
        for slot in range(3):
            wdn[3 * j + slot] = found[:, slot * 128 : slot * 128 + 128].astype(BF16).T
    pack_down(parts, wdn)
    reduces[DOWN].step(0)
    reduces[UP].step(1)

    grad_even = matmul_t(flat(grad2[0:8]), back_down[1]).reshape(8, 64, 256)
    grad_odd = (
        matmul_t(flat(grad2[0:8]), back_down[2]) + matmul_t(flat(grad2[1:9]), back_down[0])
    ).reshape(8, 64, 256)

    def store_grad(rows, places):
        count = len(places)
        ready = rows.astype(BF16)
        shifted[0:count, 8:72] = rows[:, :, 128:256]
        before = shifted[0:count, 7:71].astype(BF16)
        shifted[0:count, 8:72] = rows[:, :, 0:128]
        after = shifted[0:count, 9:73].astype(BF16)
        for m, k in enumerate(places):
            gx[k, :, 0:128] = before[m]
            gx[k, :, 128:384] = ready[m]
            gx[k, :, 384:512] = after[m]

    for start, rows in ((1, grad_even), (2, grad_odd)):
        places = range(start, start + 16, 2)
        rows = jnp.concatenate([rows[m : m + 1] * slopes[k - 1][None] for m, k in enumerate(places)], axis=0)
        store_grad(rows, places)
    grad_down_copy = [remote(gx.at[16, :, 128:384], grad_above, halo_send.at[4], halo_recv.at[4], under)]
    grad_up_copy = [remote(gx.at[1, :, 128:384], grad_below, halo_send.at[5], halo_recv.at[5], over)]
    when(over_bottom, lambda: every(grad_down_copy, "start"))
    when(under_top, lambda: every(grad_up_copy, "start"))

    reduces[DOWN].step(1)
    turn(0, 0)
    turn(2, 7)
    found = matmul(turned_frames[...], flat(gx[1:17, :, 128:384]))
    for j in range(3):
        for l in range(3):
            at = 512 * j + 128 * l
            both = found[at : at + 128, 0:128] + found[at + 128 : at + 256, 128:256]
            win[3 * j + l] = both.astype(BF16)
    pack_in(parts, win)
    reduces[IN].step(0)
    reduces[UP].step(2)
    reduces[IN].step(1)

    def mix(row, cells):
        mixed[row, pl.ds(0, 64, stride=2), :] = cells[:, 0:128]
        mixed[row, pl.ds(1, 64, stride=2), :] = cells[:, 128:256]

    even = matmul(flat(coarse2[0:8]), up[1])
    odd = matmul(flat(coarse2[0:8]), up[0]) + matmul(flat(coarse2[1:9]), up[2])
    for t in range(8):
        mix(2 * t, even[64 * t : 64 * t + 64])
        mix(2 * t + 1, odd[64 * t : 64 * t + 64])
    output[...] = (frames[...].astype(F32) + mixed[...]).astype(BF16)
    stores[0].start()
    reduces[DOWN].step(2)
    reduces[UP].step(3)
    reduces[IN].step(2)

    reduces[DOWN].step(3)
    reduces[IN].step(3)

    @pl.when(top)
    def _():
        grad_above[...] = jnp.zeros_like(grad_above)

    @pl.when(bottom)
    def _():
        grad_below[...] = jnp.zeros_like(grad_below)

    when(under_top, lambda: every(grad_down_copy, "wait_recv"))
    when(over_bottom, lambda: every(grad_up_copy, "wait_recv"))
    store_grad(grad_above[...].astype(F32)[None], (0,))
    store_grad(grad_below[...].astype(F32)[None], (17,))
    for first in (0, 8):
        back = sum(matmul_t(flat(gx[first + j : first + j + 8]), back_fine[j]) for j in range(3))
        for row in range(8):
            mix(first + row, back[64 * row : 64 * row + 64])
    input_grad[...] = (cotangent[...].astype(F32) + mixed[...]).astype(BF16)
    stores[1].start()
    for job in (UP, DOWN, IN):
        reduces[job].step(4)
    for job in (UP, DOWN, IN):
        reduces[job].step(5)

    take_share(buffers[10], band, grad_in, grad_down, grad_up)
    every(stores, "wait")
    for job in range(3):
        gathers[job].step(5)
        reduces[job].step(6)
    when(over_bottom, lambda: every(downward, "wait_send"))
    when(under_top, lambda: every(upward, "wait_send"))
    when(over_bottom, lambda: every(grad_down_copy, "wait_send"))
    when(under_top, lambda: every(grad_up_copy, "wait_send"))


def whole(frames, cotangent, w_in, w_down, w_up, scale):
    vmem, dma = pltpu.VMEM, pltpu.SemaphoreType.DMA
    spec, far = pl.BlockSpec(memory_space=vmem), pl.BlockSpec(memory_space=pl.ANY)
    gather_counts = (7, 1, 4, 4, 4, 4, 4, 4)
    reduce_counts = (4, 4, 4, 4, 4, 4, 2, 15, 8, 1, 16, 16)
    return pl.pallas_call(
        functools.partial(whole_kernel, scale),
        out_shape=(
            jax.ShapeDtypeStruct((16, 128, 128), BF16),
            jax.ShapeDtypeStruct((16, 128, 128), BF16),
            jax.ShapeDtypeStruct((3, 3, 4, 8), F32),
            jax.ShapeDtypeStruct((3, 3, 4, 16), F32),
            jax.ShapeDtypeStruct((3, 3, 8, 8), F32),
        ),
        in_specs=[far, far, spec, spec, spec],
        out_specs=(far, far, spec, spec, spec),
        scratch_shapes=[
            vmem((PACK, 128), BF16),
            vmem((PACK, 128), F32),
            vmem((16, 128, 128), BF16),
            vmem((16, 128, 128), BF16),
            vmem((16, 128, 128), BF16),
            vmem((16, 128, 128), BF16),
            vmem((2, 128, 128), BF16),
            vmem((3, 128, 128), BF16),
            vmem((1, 128, 128), BF16),
            vmem((2, 128, 128), BF16),
            vmem((64, 256), BF16),
            vmem((64, 256), BF16),
            vmem((8, 4, PACK, 128), BF16),
            vmem((8, 4, PACK, 128), BF16),
            vmem((23, 144, 128), F32),
            vmem((23, 64, 512), BF16),
            vmem((11, 2, 64, 384), BF16),
            vmem((11, 2, 64, 384), BF16),
            vmem((16, 64, 256), F32),
            vmem((9, 80, 128), F32),
            vmem((9, 72, 256), F32),
            vmem((9, 64, 512), BF16),
            vmem((9, 64, 512), BF16),
            vmem((18, 64, 512), BF16),
            vmem((16, 128, 128), F32),
            vmem((9, 128, 128), BF16),
            vmem((9, 128, 256), BF16),
            vmem((9, 256, 128), BF16),
            vmem((9, 256, 128), BF16),
            vmem((1536, 1024), BF16),
            vmem((3, 512, 256), BF16),
            vmem((3, 384, 256), BF16),
            vmem((3, 512, 256), BF16),
            vmem((3, 256, 512), BF16),
            vmem((3, 256, 512), BF16),
            vmem((3, 256, 384), BF16),
            vmem((4, 4, PACK, 128), BF16),
            vmem((3, 4, PACK, 128), BF16),
            vmem((3, 4, PACK, 128), BF16),
            vmem((4, PACK, 128), F32),
            vmem((3, PACK, 128), BF16),
            vmem((3, PACK, 128), BF16),
            vmem((PACK, 128), F32),
            vmem((PACK, 128), BF16),
            vmem((15, PACK, 128), BF16),
            vmem((3, 128, 128), F32),
            vmem((3, 16, 128), F32),
            vmem((16, DOWN_AT, 128), BF16),
            vmem((16, DOWN_AT, 128), BF16),
        ]
        + [dma((3, count)) for count in gather_counts + reduce_counts]
        + [dma((6,)), dma((6,)), dma((4,))],
        compiler_params=pltpu.CompilerParams(
            collective_id=0, has_side_effects=True, vmem_limit_bytes=56 << 20
        ),
    )(frames, cotangent, w_in, w_down, w_up)


def hand_on_kernel(*refs):
    half = len(refs) // 2
    for source, target in zip(refs[:half], refs[half:]):
        target[...] = source[...]


def hand_on(arrays):
    spec = pl.BlockSpec(memory_space=pltpu.VMEM)
    return pl.pallas_call(
        hand_on_kernel,
        out_shape=tuple(jax.ShapeDtypeStruct(array.shape, array.dtype) for array in arrays),
        in_specs=[spec] * len(arrays),
        out_specs=(spec,) * len(arrays),
        compiler_params=pltpu.CompilerParams(vmem_limit_bytes=56 << 20),
    )(*arrays)


def on_device(frames, cotangent, w_in, w_down, w_up):
    frames, cotangent = frames[0], cotangent[0]
    pixel_count = lax.axis_size("dp") * lax.axis_size("height") * frames.shape[0] * frames.shape[1]
    output, input_grad, *grads = hand_on(whole(frames, cotangent, w_in, w_down, w_up, 1.0 / math.sqrt(pixel_count)))
    return (output[None], input_grad[None], *grads)


def solution(mesh):
    in_specs = (
        P("dp", "height", None, None),
        P("dp", "height", None, None),
        P(None, None, "dp", None),
        P(None, None, "dp", None),
        P(None, None, "dp", None),
    )
    out_specs = (
        P("dp", "height", None, None),
        P("dp", "height", None, None),
        P(None, None, "dp", "height"),
        P(None, None, "dp", "height"),
        P(None, None, "dp", "height"),
    )
    return jax.shard_map(
        on_device, mesh=mesh, in_specs=in_specs, out_specs=out_specs, check_vma=False
    )
```

```python
import functools
import math

import jax
import jax.numpy as jnp
from jax import lax
from jax.experimental import pallas as pl
from jax.experimental.pallas import tpu as pltpu
from jax.sharding import PartitionSpec as P

F32, BF16 = jnp.float32, jnp.bfloat16
MESH = pl.DeviceIdType.MESH

PACK = 208
DOWN_AT = 48
UP_AT = 128
HOPS = (1, -1, 2, -2, 3, -3, 4)
JOBS = ((0, 48, "x"), (48, 80, "y"), (128, 80, "x"))
IN, DOWN, UP = 0, 1, 2
AT_ONCE = (IN, DOWN, UP)


def place():
    d = lax.axis_index("dp")
    h = lax.axis_index("height")
    z = lax.rem(lax.div(h, 2), 2) * 8 + lax.rem(d, 8)
    return lax.div(h, 4), lax.div(d, 8), z, lax.rem(h, 2)


def device(x, y, z, core):
    return (y * 8 + lax.rem(z, 8), x * 4 + lax.div(z, 8) * 2 + core)


def on_ring(position, by, size):
    return lax.rem(position + by + size, size)


def remote(source, target, send, recv, where):
    return pltpu.make_async_remote_copy(
        src_ref=source, dst_ref=target, send_sem=send, recv_sem=recv, device_id=where, device_id_type=MESH
    )


def when(condition, action):
    @pl.when(condition)
    def _():
        action()


def every(copies, act):
    for copy in copies:
        getattr(copy, act)()


def spread_columns(rows, first, wide, stacked, slots):
    count = rows.shape[0]
    wide[pl.ds(first, count), 8:136] = rows[...].astype(F32)
    for row in range(first, first + count):
        target = stacked.at[row] if len(stacked.shape) == 3 else stacked.at[row // 2, row % 2]
        for slot in range(slots):
            target[:, slot * 128 : slot * 128 + 128] = wide[row, pl.ds(7 + slot, 64, stride=2), :].astype(BF16)


def matmul(left, right):
    return lax.dot_general(left, right, (((1,), (0,)), ((), ())), preferred_element_type=F32)


def matmul_t(left, right):
    return lax.dot_general(left, right, (((1,), (1,)), ((), ())), preferred_element_type=F32)


def flat(cells):
    return cells.reshape(cells.shape[0] * cells.shape[1], cells.shape[2])


def shuffle(taps, channels, pitch, transposed):
    shards = 16 // channels
    dims = (shards * pitch, taps * 16) if transposed else (taps * 16, shards * pitch)
    row = lax.broadcasted_iota(jnp.int32, dims, 1 if transposed else 0)
    column = lax.broadcasted_iota(jnp.int32, dims, 0 if transposed else 1)
    bits = channels.bit_length() - 1
    wanted = ((row & 15) >> bits) * pitch + (row >> 4) * channels + (row & (channels - 1))
    return (column == wanted).astype(F32).astype(BF16)


def unpack_in(full, win):
    order = shuffle(9, 4, 48, False)
    for group in range(8):
        k, y = 4 * (group % 2), group // 2
        rows = matmul(order, full[k : k + 4, y, 0:DOWN_AT].reshape(192, 128)).astype(BF16)
        win[:, 16 * group : 16 * group + 16] = rows.reshape(9, 16, 128)


def unpack_down(full, wdn):
    order = shuffle(18, 4, 80, False)
    for group in range(8):
        k, y = 4 * (group % 2), group // 2
        rows = matmul(order, full[k : k + 4, y, DOWN_AT:UP_AT].reshape(320, 128)).astype(BF16)
        wdn[:, 16 * group : 16 * group + 16, 0:128] = rows[0:144].reshape(9, 16, 128)
        wdn[:, 16 * group : 16 * group + 16, 128:256] = rows[144:288].reshape(9, 16, 128)


def unpack_up(full, wup):
    order = shuffle(9, 8, 80, False)
    for group in range(16):
        k, y = 2 * (group % 4), group // 4
        rows = matmul(order, full[k : k + 2, y, UP_AT:PACK].reshape(160, 128)).astype(BF16)
        wup[:, 16 * group : 16 * group + 16] = rows.reshape(9, 16, 128)


def pack_in(parts, sin):
    order = shuffle(9, 4, 48, True)
    for group in range(8):
        k, y = 4 * (group % 2), group // 2
        rows = matmul(order, sin[:, 16 * group : 16 * group + 16].reshape(144, 128)).astype(BF16)
        parts[k : k + 4, y, 0:DOWN_AT] = rows.reshape(4, 48, 128)


def pack_down(parts, sdn):
    order = shuffle(18, 4, 80, True)
    for group in range(8):
        k, y = 4 * (group % 2), group // 2
        halves = [sdn[:, 16 * group : 16 * group + 16, at : at + 128].reshape(144, 128) for at in (0, 128)]
        rows = matmul(order, jnp.concatenate(halves, axis=0)).astype(BF16)
        parts[k : k + 4, y, DOWN_AT:UP_AT] = rows.reshape(4, 80, 128)


def pack_up(parts, sup):
    order = shuffle(9, 8, 80, True)
    for group in range(16):
        k, y = 2 * (group % 4), group // 4
        rows = matmul(order, sup[:, 16 * group : 16 * group + 16].reshape(144, 128)).astype(BF16)
        parts[k : k + 2, y, UP_AT:PACK] = rows.reshape(2, 80, 128)


def stack_in(win, fine, back_fine):
    blank = jnp.zeros((128, 128), BF16)
    for j in range(3):
        for slot in range(4):
            at = slice(slot * 128, slot * 128 + 128)
            fine[j, at, 0:128] = win[3 * j + slot] if slot < 3 else blank
            fine[j, at, 128:256] = win[3 * j + slot - 1] if slot > 0 else blank
            back_fine[j, 0:128, at] = win[3 * (2 - j) + 2 - slot] if slot < 3 else blank
            back_fine[j, 128:256, at] = win[3 * (2 - j) + 3 - slot] if slot > 0 else blank


def stack_down(wdn, down, back_down):
    for j in range(3):
        for slot in range(3):
            down[j, slot * 128 : slot * 128 + 128, :] = wdn[3 * j + slot]
        back_down[j, 0:128, 0:256] = wdn[3 * j + 1]
        back_down[j, 0:128, 256:512] = jnp.zeros((128, 256), BF16)
        back_down[j, 128:256, 0:256] = wdn[3 * j + 2]
        back_down[j, 128:256, 256:512] = wdn[3 * j]


def stack_up(wup, up, back_up):
    for j in range(3):
        for slot in range(3):
            back_up[j, :, slot * 128 : slot * 128 + 128] = wup[3 * (2 - j) + 2 - slot]
        up[j, 0:256, 0:128] = wup[3 * j + 1]
        up[j, 0:256, 128:256] = wup[3 * j]
        up[j, 256:512, 0:128] = jnp.zeros((256, 128), BF16)
        up[j, 256:512, 128:256] = wup[3 * j + 2]


def sigmoid(value):
    return 0.5 + 0.5 * jnp.tanh(0.5 * value)


def pack_own(w_in, w_down, w_up, wide, own):
    wide[...] = jnp.zeros_like(wide)
    for tap in range(9):
        j, l = tap // 3, tap % 3
        wide[4 * tap : 4 * tap + 4] = w_in[j, l].astype(F32)
        for half in range(2):
            at = DOWN_AT + 36 * half + 4 * tap
            wide[at : at + 4] = w_down[j, l, :, 128 * half : 128 * half + 128].astype(F32)
        wide[UP_AT + 8 * tap : UP_AT + 8 * tap + 8] = w_up[j, l].astype(F32)
    own[...] = wide[...].astype(BF16)


def lanes(block, first, count):
    lane = lax.broadcasted_iota(jnp.int32, (count, 128), 1)
    wanted = lax.broadcasted_iota(jnp.int32, (count, 128), 0) + first
    return lax.dot_general(
        (lane == wanted).astype(F32), block, (((1,), (1,)), ((), ())),
        precision=lax.Precision.HIGHEST, preferred_element_type=F32,
    )


def take_share(share, band, grad_in, grad_down, grad_up):
    into = lanes(share[IN, 0:8], 0, 40)
    down = lanes(share[DOWN, 0:16], 36 * lax.div(band, 8), 40)
    up = lanes(share[UP, 0:8], 0, 72)
    for tap in range(9):
        j, l = tap // 3, tap % 3
        grad_in[j, l] = into[4 * tap : 4 * tap + 4]
        grad_down[j, l] = down[4 * tap : 4 * tap + 4]
        grad_up[j, l] = up[8 * tap : 8 * tap + 8]


class Gather:
    def __init__(self, job, own, full, sems):
        first, count, self.main = JOBS[job]
        self.rows = pl.ds(first, count)
        self.own, self.full = own, full
        self.sems = [sem.at[job] for sem in sems]
        self.x, self.y, self.z, self.core = place()
        self.carried = self.x + 4 * self.core
        self.holder = lax.rem(self.z, 8) == self.carried

    def beside(self, axis, by):
        if axis == "x":
            return device(on_ring(self.x, by, 4), self.y, self.z, self.core)
        return device(self.x, on_ring(self.y, by, 4), self.z, self.core)

    def along_z(self, count=7):
        send, recv = self.sems[0], self.sems[1]
        target = self.full.at[self.carried, self.y, self.rows]
        return [
            remote(
                self.own.at[self.rows], target, send.at[slot], recv.at[0],
                device(self.x, self.y, on_ring(self.z, by, 16), self.core),
            )
            for slot, by in enumerate(HOPS[:count])
        ]

    def light(self):
        send, recv = self.sems[2], self.sems[3]
        axis = "y" if self.main == "x" else "x"
        block = self.full.at[self.carried, self.y, self.rows]
        return [remote(block, block, send.at[by], recv.at[by], self.beside(axis, by)) for by in (1, 3, 2)]

    def piece(self, by, core):
        if self.main == "x":
            return self.full.at[on_ring(self.x, -by, 4) + 4 * core, :, self.rows]
        return self.full.at[pl.ds(4 * core, 4), on_ring(self.y, -by, 4), self.rows]

    def heavy(self, by):
        send, recv = self.sems[4], self.sems[5]
        block = self.piece(0, self.core)
        return remote(block, block, send.at[by], recv.at[by], self.beside(self.main, by))

    def across(self, by):
        send, recv = self.sems[6], self.sems[7]
        block = self.piece(by, self.core)
        other = device(self.x, self.y, self.z, 1 - self.core)
        return remote(block, block, send.at[by], recv.at[by], other)

    def step(self, stage):
        if stage == 0:

            @pl.when(self.holder)
            def _():
                every(self.along_z(), "start")
                self.full[self.carried, self.y, self.rows] = self.own[self.rows]

        if stage == 1:
            when(jnp.logical_not(self.holder), lambda: every(self.along_z(1), "wait_recv"))
            every(self.light(), "start")
        if stage == 2:
            every(self.light(), "wait_recv")
            for by in (1, 3, 2):
                self.heavy(by).start()
            self.across(0).start()
        if stage == 3:
            for by in (1, 3, 2):
                self.heavy(by).wait_recv()
                self.across(by).start()
        if stage == 4:
            for by in range(4):
                self.across(by).wait_recv()
        if stage == 5:
            when(self.holder, lambda: every(self.along_z(), "wait_send"))
            every(self.light(), "wait_send")
            for by in (1, 2, 3):
                self.heavy(by).wait_send()
            for by in range(4):
                self.across(by).wait_send()


class Reduce:
    def __init__(self, job, parts, buffers, sems, scale):
        first, self.count, self.main = JOBS[job]
        self.rows = pl.ds(first, self.count)
        self.job, self.width = job, 16 if job == DOWN else 8
        self.parts = parts
        (
            self.from_core, self.heavy_out, self.heavy_in, self.sums, self.light_out, self.light_in,
            self.column, self.z_out, self.z_in, self.done, self.share, self.direct_out, self.direct_in,
        ) = buffers
        self.sems = [sem.at[job] for sem in sems]
        self.scale = scale
        self.at_once = job in AT_ONCE
        if self.at_once:
            self.main = "x"
        self.x, self.y, self.z, self.core = place()
        self.carried = self.x + 4 * self.core
        self.holder = lax.rem(self.z, 8) == self.carried

    beside = Gather.beside

    def block(self, ref, by, core):
        if self.main == "x":
            return ref.at[on_ring(self.x, by, 4) + 4 * core, :, self.rows]
        return ref.at[pl.ds(4 * core, 4), on_ring(self.y, by, 4), self.rows]

    def across(self, by):
        other = device(self.x, self.y, self.z, 1 - self.core)
        return remote(
            self.block(self.parts, by, 1 - self.core), self.block(self.from_core, by, 0),
            self.sems[0].at[by], self.sems[1].at[by], other,
        )

    def heavy(self, by):
        return remote(
            self.heavy_out.at[by - 1, :, self.rows], self.heavy_in.at[by - 1, :, self.rows],
            self.sems[2].at[by], self.sems[3].at[by], self.beside(self.main, by),
        )

    def light(self, by):
        axis = "y" if self.main == "x" else "x"
        return remote(
            self.light_out.at[by - 1, self.rows], self.light_in.at[by - 1, self.rows],
            self.sems[4].at[by], self.sems[5].at[by], self.beside(axis, by),
        )

    def direct(self, slot):
        where = device(on_ring(self.x, slot // 4, 4), on_ring(self.y, slot % 4, 4), self.z, self.core)
        return remote(
            self.direct_out.at[slot, self.rows], self.direct_in.at[slot, self.rows], self.sems[10].at[slot], self.sems[11].at[slot], where
        )

    def step_direct(self, stage):
        rows = self.rows
        if stage == 1:
            for by in (2, 1, 3, 0):
                self.across(by).wait_recv()
                self.sums[:, rows] = self.both(by)
                for turn in (2, 1, 3, 0):
                    if by or turn:
                        slot = 4 * by + turn
                        self.direct_out[slot, rows] = self.sums[on_ring(self.y, turn, 4), rows].astype(BF16)
                        self.direct(slot).start()
            self.column[rows] = self.sums[self.y, rows]
        if stage == 3:
            total = self.column[rows]
            for slot in (4, 12, 1, 3, 8, 2, 5, 7, 13, 15, 6, 9, 11, 14, 10):
                self.direct(slot).wait_recv()
                total += self.direct_in[slot, rows].astype(F32)
            self.column[rows] = total
            self.send_to_holders(total)

    def send_to_holders(self, total):
        self.z_out[self.rows] = total.astype(BF16)
        for at in (0, 8):
            when(self.z != self.carried + at, self.to_holder(at).start)

    def to_holder(self, at):
        where = self.carried + at
        slot = lax.rem(self.z - where + 31, 16)
        return remote(
            self.z_out.at[self.rows], self.z_in.at[slot, self.rows],
            self.sems[6].at[at // 8], self.sems[7].at[slot], device(self.x, self.y, where, self.core),
        )

    def from_ring(self, slot):
        return remote(
            self.z_out.at[self.rows], self.z_in.at[slot, self.rows],
            self.sems[6].at[0], self.sems[7].at[slot], device(self.x, self.y, self.z, 1 - self.core),
        )

    def columns_of(self, x, core):
        band = lax.rem(x * 4 + lax.div(self.z, 8) * 2 + core, 128 // self.width)
        return pl.ds(pl.multiple_of(band * self.width, 8), self.width)

    def spread(self, count=7):
        return [
            remote(
                self.done.at[self.job, self.columns_of(on_ring(self.x, by, 4), lax.rem(self.core + swap, 2))],
                self.share.at[self.job, pl.ds(0, self.width)],
                self.sems[8].at[2 * by + swap], self.sems[9].at[0],
                device(on_ring(self.x, by, 4), self.y, self.z, lax.rem(self.core + swap, 2)),
            )
            for by, swap in ((2, 0), (2, 1), (1, 0), (3, 0), (1, 1), (3, 1), (0, 1))[:count]
        ]

    def both(self, by):
        own = self.block(self.parts, by, self.core)[...].astype(F32)
        return own + self.block(self.from_core, by, 0)[...].astype(F32)

    def step(self, stage):
        rows = self.rows
        if self.at_once and stage in (1, 2, 3):
            return self.step_direct(stage)
        if stage == 0:
            for by in (1, 3, 2, 0):
                self.across(by).start()
        if stage == 1:
            for by in (1, 3, 2):
                self.across(by).wait_recv()
                self.heavy_out[by - 1, :, rows] = self.both(by).astype(BF16)
                self.heavy(by).start()
            self.across(0).wait_recv()
            self.sums[:, rows] = self.both(0)
        if stage == 2:
            total = self.sums[:, rows]
            for by in (1, 3, 2):
                self.heavy(by).wait_recv()
                total += self.heavy_in[by - 1, :, rows].astype(F32)
            self.sums[:, rows] = total
            here = self.y if self.main == "x" else self.x
            for by in (1, 3, 2):
                self.light_out[by - 1, rows] = self.sums[on_ring(here, by, 4), rows].astype(BF16)
                self.light(by).start()
            self.column[rows] = self.sums[here, rows]
        if stage == 3:
            total = self.column[rows]
            for by in (1, 3, 2):
                self.light(by).wait_recv()
                total += self.light_in[by - 1, rows].astype(F32)
            self.column[rows] = total
            self.send_to_holders(total)
        if stage == 4:

            @pl.when(self.holder)
            def _():
                total = self.column[rows]
                for slot in range(15):
                    self.from_ring(slot).wait_recv()
                    total += self.z_in[slot, rows].astype(F32)
                self.done[self.job, :, 0 : self.count] = (total * self.scale).T
                every(self.spread(), "start")
                self.share[self.job, 0 : self.width] = self.done[self.job, self.columns_of(self.x, self.core)]

        if stage == 5:
            when(jnp.logical_not(self.holder), lambda: every(self.spread(1), "wait_recv"))
        if stage == 6:
            for by in range(4):
                self.across(by).wait_send()
            if self.at_once:
                for slot in range(1, 16):
                    self.direct(slot).wait_send()
            else:
                for by in (1, 2, 3):
                    self.heavy(by).wait_send()
                    self.light(by).wait_send()
            for at in (0, 8):
                when(self.z != self.carried + at, self.to_holder(at).wait_send)
            when(self.holder, lambda: every(self.spread(), "wait_send"))


def greet():
    x, y, z, core = place()
    carried = x + 4 * core
    holder = lax.rem(z, 8) == carried
    row, band = lax.axis_index("dp"), lax.axis_index("height")
    barrier = pltpu.get_barrier_semaphore()

    def signal(where):
        pl.semaphore_signal(barrier, inc=1, device_id=where, device_id_type=MESH)

    signal((row, on_ring(band, -1, 16)))
    signal((row, on_ring(band, 1, 16)))

    @pl.when(holder)
    def _():
        for by in (8, 7, 9, 6, 10, 5, 11, 4, 12, 3, 13, 2, 14, 1, 15):
            signal(device(x, y, on_ring(z, by, 16), core))

    @pl.when(jnp.logical_not(holder))
    def _():
        signal(device(x, y, carried, core))
        signal(device(x, y, carried + 8, core))

    for slot in (10, 6, 14, 9, 11, 5, 7, 13, 15, 8, 2, 4, 12, 1, 3):
        signal(device(on_ring(x, slot // 4, 4), on_ring(y, slot % 4, 4), z, core))
    for by in (2, 1, 3, 0):
        signal(device(on_ring(x, by, 4), y, z, 1 - core))
    return lambda: pl.semaphore_wait(barrier, jnp.where(holder, 21 + 15, 21 + 2))


def whole_kernel(
    scale,
    frames_far,
    cotangent_far,
    w_in,
    w_down,
    w_up,
    output_far,
    input_grad_far,
    grad_in,
    grad_down,
    grad_up,
    own,
    own_wide,
    output,
    input_grad,
    frames,
    cotangent,
    frames_above,
    frames_below,
    cotangent_above,
    cotangent_below,
    grad_above,
    grad_below,
    full,
    parts,
    wide,
    fx,
    h3,
    c3,
    slopes,
    shifted,
    shifted_wide,
    coarse2,
    grad2,
    gx,
    mixed,
    win,
    wdn,
    wup,
    sup,
    turned_frames,
    fine,
    down,
    up,
    back_fine,
    back_down,
    back_up,
    *rest,
):
    buffers, rest = rest[:13], rest[13:]
    gather_sems, reduce_sems, (halo_send, halo_recv, load_sem) = rest[:8], rest[8:20], rest[20:]
    band = lax.axis_index("height")
    top, bottom = band == 0, band == lax.axis_size("height") - 1
    under_top, over_bottom = jnp.logical_not(top), jnp.logical_not(bottom)

    loads = [
        pltpu.make_async_copy(frames_far, frames, load_sem.at[0]),
        pltpu.make_async_copy(cotangent_far, cotangent, load_sem.at[1]),
    ]
    every(loads, "start")
    stores = [
        pltpu.make_async_copy(output, output_far, load_sem.at[2]),
        pltpu.make_async_copy(input_grad, input_grad_far, load_sem.at[3]),
    ]
    gathers = [Gather(job, own, full, gather_sems) for job in range(3)]
    reduces = [Reduce(job, parts, buffers, reduce_sems, scale) for job in range(3)]

    row = lax.axis_index("dp")
    over, under = (row, on_ring(band, -1, 16)), (row, on_ring(band, 1, 16))

    def halo(slot, source, first, target, where):
        cells = source.at[pl.ds(first, target.shape[0])]
        return remote(cells, target, halo_send.at[slot], halo_recv.at[slot], where)

    downward = [
        halo(0, frames_far, 14, frames_above, under),
        halo(1, cotangent_far, 15, cotangent_above, under),
    ]
    upward = [
        halo(2, frames_far, 0, frames_below, over),
        halo(3, cotangent_far, 0, cotangent_below, over),
    ]

    all_there = greet()
    pack_own(w_in, w_down, w_up, own_wide, own)
    buffers[9][...] = jnp.zeros((3, 128, 128), F32)
    wide[:, 0:8] = jnp.zeros((23, 8, 128), F32)
    wide[:, 136:144] = jnp.zeros((23, 8, 128), F32)
    shifted[:, 0:8] = jnp.zeros((9, 8, 128), F32)
    shifted[:, 72:80] = jnp.zeros((9, 8, 128), F32)
    shifted_wide[:, 64:72] = jnp.zeros((9, 8, 256), F32)
    every(loads, "wait")
    spread_columns(frames, 4, wide, fx, 4)

    def turn(j, pair):
        rows = flat(fx[3 + j + 2 * pair : 5 + j + 2 * pair])
        turned_frames[512 * j : 512 * j + 512, 128 * pair : 128 * pair + 128] = rows.T

    for pair in range(8):
        turn(1, pair)
    all_there()
    for job in range(3):
        gathers[job].step(0)

    @pl.when(top)
    def _():
        frames_above[...] = jnp.zeros_like(frames_above)
        cotangent_above[...] = jnp.zeros_like(cotangent_above)

    @pl.when(bottom)
    def _():
        frames_below[...] = jnp.zeros_like(frames_below)
        cotangent_below[...] = jnp.zeros_like(cotangent_below)

    gathers[IN].step(1)
    gathers[DOWN].step(1)
    gathers[UP].step(1)
    when(over_bottom, lambda: every(downward, "start"))
    when(under_top, lambda: every(upward, "start"))
    gathers[IN].step(2)
    gathers[DOWN].step(2)
    gathers[UP].step(2)
    spread_columns(cotangent, 3, wide, c3, 3)
    gathers[IN].step(3)
    gathers[DOWN].step(3)
    for pair in range(7):
        turn(0, pair + 1)
        turn(2, pair)
    gathers[IN].step(4)
    def fine_rows(first, count):
        pre = sum(matmul(flat(fx[first + j : first + j + count]), fine[j]) for j in range(3))
        gate = sigmoid(pre)
        hidden = (pre * gate).reshape(count, 64, 256)
        slope = (gate * (1.0 + pre * (1.0 - gate))).reshape(count, 64, 256)
        shifted[0:count, 8:72] = hidden[:, :, 128:256]
        before = shifted[0:count, 7:71].astype(BF16)
        hidden = hidden.astype(BF16)
        for row in range(count):
            i = first + row
            h3[i // 2, i % 2, :, 0:128] = before[row]
            h3[i // 2, i % 2, :, 128:384] = hidden[row]
            if 3 <= i < 19:
                slopes[i - 3] = slope[row]

    unpack_in(full, win)
    stack_in(win, fine, back_fine)
    fine_rows(4, 7)
    gathers[UP].step(3)
    gathers[DOWN].step(4)
    unpack_down(full, wdn)
    stack_down(wdn, down, back_down)
    fine_rows(11, 7)

    when(under_top, lambda: every(downward, "wait_recv"))
    when(over_bottom, lambda: every(upward, "wait_recv"))
    spread_columns(frames_above, 2, wide, fx, 4)
    spread_columns(frames_below, 20, wide, fx, 4)
    spread_columns(cotangent_above, 2, wide, c3, 3)
    spread_columns(cotangent_below, 19, wide, c3, 3)

    fine_rows(2, 2)
    fine_rows(18, 3)

    @pl.when(top)
    def _():
        h3[1, 0] = jnp.zeros((64, 384), BF16)

    @pl.when(bottom)
    def _():
        for i in (19, 20):
            h3[i // 2, i % 2] = jnp.zeros((64, 384), BF16)

    views = ((1, 0), (1, 1), (2, 0))
    pre = sum(matmul(flat(h3[a : a + 9, b]), down[j]) for j, (a, b) in enumerate(views))
    gate = sigmoid(pre)
    coarse = (pre * gate).reshape(9, 64, 256)
    shifted_wide[:, 0:64] = coarse
    coarse2[:, :, 0:256] = coarse.astype(BF16)
    coarse2[:, :, 256:512] = shifted_wide[:, 1:65].astype(BF16)
    turned = flat(coarse2[0:8, :, 0:256]).T
    for j, (a, b) in enumerate(views):
        found = matmul(turned, flat(c3[a : a + 8, b]))
        for slot in range(3):
            sup[3 * (2 - j) + 2 - slot] = found[:, slot * 128 : slot * 128 + 128].astype(BF16)
    pack_up(parts, sup)
    reduces[UP].step(0)
    gathers[UP].step(4)
    unpack_up(full, wup)
    stack_up(wup, up, back_up)
    back = sum(matmul_t(flat(c3[a : a + 9, b]), back_up[j]) for j, (a, b) in enumerate(views))
    grad = (back * (gate * (1.0 + pre * (1.0 - gate)))).reshape(9, 64, 256)
    shifted_wide[:, 0:64] = grad
    grad2[:, :, 0:256] = grad.astype(BF16)
    grad2[:, :, 256:512] = shifted_wide[:, 1:65].astype(BF16)

    @pl.when(bottom)
    def _():
        coarse2[8] = jnp.zeros((64, 512), BF16)
        grad2[8] = jnp.zeros((64, 512), BF16)

    turned = flat(grad2[0:8, :, 0:256]).T
    for j, (a, b) in enumerate(views):
        found = matmul(turned, flat(h3[a : a + 8, b]))
        for slot in range(3):
            wdn[3 * j + slot] = found[:, slot * 128 : slot * 128 + 128].astype(BF16).T
    pack_down(parts, wdn)
    reduces[DOWN].step(0)
    reduces[UP].step(1)

    grad_even = matmul_t(flat(grad2[0:8]), back_down[1]).reshape(8, 64, 256)
    grad_odd = (
        matmul_t(flat(grad2[0:8]), back_down[2]) + matmul_t(flat(grad2[1:9]), back_down[0])
    ).reshape(8, 64, 256)

    def store_grad(rows, places):
        count = len(places)
        ready = rows.astype(BF16)
        shifted[0:count, 8:72] = rows[:, :, 128:256]
        before = shifted[0:count, 7:71].astype(BF16)
        shifted[0:count, 8:72] = rows[:, :, 0:128]
        after = shifted[0:count, 9:73].astype(BF16)
        for m, k in enumerate(places):
            gx[k, :, 0:128] = before[m]
            gx[k, :, 128:384] = ready[m]
            gx[k, :, 384:512] = after[m]

    for start, rows in ((1, grad_even), (2, grad_odd)):
        places = range(start, start + 16, 2)
        rows = jnp.concatenate([rows[m : m + 1] * slopes[k - 1][None] for m, k in enumerate(places)], axis=0)
        store_grad(rows, places)
    grad_down_copy = [remote(gx.at[16, :, 128:384], grad_above, halo_send.at[4], halo_recv.at[4], under)]
    grad_up_copy = [remote(gx.at[1, :, 128:384], grad_below, halo_send.at[5], halo_recv.at[5], over)]
    when(over_bottom, lambda: every(grad_down_copy, "start"))
    when(under_top, lambda: every(grad_up_copy, "start"))

    reduces[DOWN].step(1)
    turn(0, 0)
    turn(2, 7)
    found = matmul(turned_frames[...], flat(gx[1:17, :, 128:384]))
    for j in range(3):
        for l in range(3):
            at = 512 * j + 128 * l
            both = found[at : at + 128, 0:128] + found[at + 128 : at + 256, 128:256]
            win[3 * j + l] = both.astype(BF16)
    pack_in(parts, win)
    reduces[IN].step(0)
    reduces[UP].step(2)
    reduces[IN].step(1)

    def mix(row, cells):
        mixed[row, pl.ds(0, 64, stride=2), :] = cells[:, 0:128]
        mixed[row, pl.ds(1, 64, stride=2), :] = cells[:, 128:256]

    even = matmul(flat(coarse2[0:8]), up[1])
    odd = matmul(flat(coarse2[0:8]), up[0]) + matmul(flat(coarse2[1:9]), up[2])
    for t in range(8):
        mix(2 * t, even[64 * t : 64 * t + 64])
        mix(2 * t + 1, odd[64 * t : 64 * t + 64])
    output[...] = (frames[...].astype(F32) + mixed[...]).astype(BF16)
    stores[0].start()
    reduces[DOWN].step(2)
    reduces[UP].step(3)
    reduces[IN].step(2)

    reduces[DOWN].step(3)
    reduces[IN].step(3)

    @pl.when(top)
    def _():
        grad_above[...] = jnp.zeros_like(grad_above)

    @pl.when(bottom)
    def _():
        grad_below[...] = jnp.zeros_like(grad_below)

    when(under_top, lambda: every(grad_down_copy, "wait_recv"))
    when(over_bottom, lambda: every(grad_up_copy, "wait_recv"))
    store_grad(grad_above[...].astype(F32)[None], (0,))
    store_grad(grad_below[...].astype(F32)[None], (17,))
    for first in (0, 8):
        back = sum(matmul_t(flat(gx[first + j : first + j + 8]), back_fine[j]) for j in range(3))
        for row in range(8):
            mix(first + row, back[64 * row : 64 * row + 64])
    input_grad[...] = (cotangent[...].astype(F32) + mixed[...]).astype(BF16)
    stores[1].start()
    for job in (UP, DOWN, IN):
        reduces[job].step(4)
    for job in (UP, DOWN, IN):
        reduces[job].step(5)

    take_share(buffers[10], band, grad_in, grad_down, grad_up)
    every(stores, "wait")
    for job in range(3):
        gathers[job].step(5)
        reduces[job].step(6)
    when(over_bottom, lambda: every(downward, "wait_send"))
    when(under_top, lambda: every(upward, "wait_send"))
    when(over_bottom, lambda: every(grad_down_copy, "wait_send"))
    when(under_top, lambda: every(grad_up_copy, "wait_send"))


def whole(frames, cotangent, w_in, w_down, w_up, scale):
    vmem, dma = pltpu.VMEM, pltpu.SemaphoreType.DMA
    spec, far = pl.BlockSpec(memory_space=vmem), pl.BlockSpec(memory_space=pl.ANY)
    gather_counts = (7, 1, 4, 4, 4, 4, 4, 4)
    reduce_counts = (4, 4, 4, 4, 4, 4, 2, 15, 8, 1, 16, 16)
    return pl.pallas_call(
        functools.partial(whole_kernel, scale),
        out_shape=(
            jax.ShapeDtypeStruct((16, 128, 128), BF16),
            jax.ShapeDtypeStruct((16, 128, 128), BF16),
            jax.ShapeDtypeStruct((3, 3, 4, 8), F32),
            jax.ShapeDtypeStruct((3, 3, 4, 16), F32),
            jax.ShapeDtypeStruct((3, 3, 8, 8), F32),
        ),
        in_specs=[far, far, spec, spec, spec],
        out_specs=(far, far, spec, spec, spec),
        scratch_shapes=[
            vmem((PACK, 128), BF16),
            vmem((PACK, 128), F32),
            vmem((16, 128, 128), BF16),
            vmem((16, 128, 128), BF16),
            vmem((16, 128, 128), BF16),
            vmem((16, 128, 128), BF16),
            vmem((2, 128, 128), BF16),
            vmem((3, 128, 128), BF16),
            vmem((1, 128, 128), BF16),
            vmem((2, 128, 128), BF16),
            vmem((64, 256), BF16),
            vmem((64, 256), BF16),
            vmem((8, 4, PACK, 128), BF16),
            vmem((8, 4, PACK, 128), BF16),
            vmem((23, 144, 128), F32),
            vmem((23, 64, 512), BF16),
            vmem((11, 2, 64, 384), BF16),
            vmem((11, 2, 64, 384), BF16),
            vmem((16, 64, 256), F32),
            vmem((9, 80, 128), F32),
            vmem((9, 72, 256), F32),
            vmem((9, 64, 512), BF16),
            vmem((9, 64, 512), BF16),
            vmem((18, 64, 512), BF16),
            vmem((16, 128, 128), F32),
            vmem((9, 128, 128), BF16),
            vmem((9, 128, 256), BF16),
            vmem((9, 256, 128), BF16),
            vmem((9, 256, 128), BF16),
            vmem((1536, 1024), BF16),
            vmem((3, 512, 256), BF16),
            vmem((3, 384, 256), BF16),
            vmem((3, 512, 256), BF16),
            vmem((3, 256, 512), BF16),
            vmem((3, 256, 512), BF16),
            vmem((3, 256, 384), BF16),
            vmem((4, 4, PACK, 128), BF16),
            vmem((3, 4, PACK, 128), BF16),
            vmem((3, 4, PACK, 128), BF16),
            vmem((4, PACK, 128), F32),
            vmem((3, PACK, 128), BF16),
            vmem((3, PACK, 128), BF16),
            vmem((PACK, 128), F32),
            vmem((PACK, 128), BF16),
            vmem((15, PACK, 128), BF16),
            vmem((3, 128, 128), F32),
            vmem((3, 16, 128), F32),
            vmem((16, PACK, 128), BF16),
            vmem((16, PACK, 128), BF16),
        ]
        + [dma((3, count)) for count in gather_counts + reduce_counts]
        + [dma((6,)), dma((6,)), dma((4,))],
        compiler_params=pltpu.CompilerParams(
            collective_id=0, has_side_effects=True, vmem_limit_bytes=56 << 20
        ),
    )(frames, cotangent, w_in, w_down, w_up)


def hand_on_kernel(*refs):
    half = len(refs) // 2
    for source, target in zip(refs[:half], refs[half:]):
        target[...] = source[...]


def hand_on(arrays):
    spec = pl.BlockSpec(memory_space=pltpu.VMEM)
    return pl.pallas_call(
        hand_on_kernel,
        out_shape=tuple(jax.ShapeDtypeStruct(array.shape, array.dtype) for array in arrays),
        in_specs=[spec] * len(arrays),
        out_specs=(spec,) * len(arrays),
        compiler_params=pltpu.CompilerParams(vmem_limit_bytes=56 << 20),
    )(*arrays)


def on_device(frames, cotangent, w_in, w_down, w_up):
    frames, cotangent = frames[0], cotangent[0]
    pixel_count = lax.axis_size("dp") * lax.axis_size("height") * frames.shape[0] * frames.shape[1]
    output, input_grad, *grads = hand_on(whole(frames, cotangent, w_in, w_down, w_up, 1.0 / math.sqrt(pixel_count)))
    return (output[None], input_grad[None], *grads)


def solution(mesh):
    in_specs = (
        P("dp", "height", None, None),
        P("dp", "height", None, None),
        P(None, None, "dp", None),
        P(None, None, "dp", None),
        P(None, None, "dp", None),
    )
    out_specs = (
        P("dp", "height", None, None),
        P("dp", "height", None, None),
        P(None, None, "dp", "height"),
        P(None, None, "dp", "height"),
        P(None, None, "dp", "height"),
    )
    return jax.shard_map(
        on_device, mesh=mesh, in_specs=in_specs, out_specs=out_specs, check_vma=False
    )
```
